32 devices in a mesh: dp: 8 (over y, x, core), head: 4 (over z).
Axes of the slice: x: 2, y: 2, z: 4, core: 2. Of those that a mesh axis runs over, the one named last changes fastest.
Arguments:
- tokens: bfloat16 [32768, 256], P(('dp', 'head')), may hold values from -6 to 6
- lengths: int32 [128], P('dp'), may hold values from 32 to 256, as said below
- cotangent: bfloat16 [32768, 256], P(('dp', 'head')), may hold values from -6 to 6
- gain_attn: float32 [2, 256], replicated, may hold values from 0.1 to 1.9
- gain_mlp: float32 [2, 256], replicated, may hold values from 0.1 to 1.9
- w_qkv: bfloat16 [2, 256, 3, 256], P(None, None, None, 'head'), may hold values from -4 to 4, as said below
- w_out: bfloat16 [2, 256, 256], P(None, 'head'), may hold values from -4 to 4, as said below
- w_up: bfloat16 [2, 256, 1024], P(None, None, 'head'), may hold values from -4 to 4, as said below
- w_down: bfloat16 [2, 1024, 256], P(None, 'head'), may hold values from -0.1875 to 0.1875
- w_cross: bfloat16 [2, 256, 256], P(None, None, 'head'), may hold values from -4 to 4, as said below
- b_cross: bfloat16 [2, 256], P(None, 'head'), may hold values from -1 to 1, as said below
Outputs:
- output: float32 [32768, 256], P(('dp', 'head'))
- grad_tokens: float32 [32768, 256], P(('dp', 'head'))
- grad_gain_attn: float32 [2, 256], replicated
- grad_gain_mlp: float32 [2, 256], replicated
- grad_w_qkv: float32 [2, 256, 3, 256], P(None, None, None, 'head')
- grad_w_out: float32 [2, 256, 256], P(None, 'head')
- grad_w_up: float32 [2, 256, 1024], P(None, None, 'head')
- grad_w_down: float32 [2, 1024, 256], P(None, 'head')
- grad_w_cross: float32 [2, 256, 256], P(None, None, 'head')
- grad_b_cross: float32 [2, 256], P(None, 'head')
The draws below stay inside these ranges and needn't reach their ends.
Inputs may be any that keep to these rules, and one draw needn't show every extreme that they name: lengths[b] slots of sample b are present and the rest are absent; some sample has exactly 256 and some exactly 32. `w_qkv`: independent entries with deviation about 1 / sqrt(128). `w_out`: independent entries with deviation about 1 / sqrt(16). `w_up`: independent entries with deviation about 1 / sqrt(256). `w_cross`: independent entries with deviation about 1 / sqrt(1024). `b_cross`: independent entries with deviation about 0.25.
All inputs are finite; a program needn't handle non-finite values.
Results may differ from the reference program's by a relative error of at most 0.019.
The reference program's roundings to bfloat16 on the way count: a program that leaves them out, or rounds other values in their place, can miss the bound.
Values may be sent and summed in bfloat16 or wider, within the bound.
No kernel may reach another device: no remote copies, remote signals or barrier semaphores. Data moves between devices by JAX's collectives and lax.ppermute only.
A program may use at most 128 MiB of HBM per device.

```python
import math
import jax
import jax.numpy as jnp
from jax import lax

D = 256
H = 4
HD = 64
FF = 1024
S = 256
LAYERS = 2
SAMPLES = 128
TOKENS = 32768


def draw_lengths(key, part):
    key = jax.random.fold_in(key, 7)
    key_one, key_two, key_three, key_full, key_short = jax.random.split(key, 5)
    counts_one = jax.random.randint(key_one, (SAMPLES,), S // 8, S + 1, dtype=jnp.int32)
    counts_two = jax.random.randint(key_two, (SAMPLES,), S // 8, S + 1, dtype=jnp.int32)
    counts_three = jax.random.randint(key_three, (SAMPLES,), S // 8, S + 1, dtype=jnp.int32)
    counts_drawn = jnp.minimum(jnp.minimum(counts_one, counts_two), counts_three)
    full_at = jax.random.randint(key_full, (), 0, SAMPLES, dtype=jnp.int32)
    short_at = (full_at + 1 + jax.random.randint(key_short, (), 0, SAMPLES - 1, dtype=jnp.int32)) % SAMPLES
    positions = jnp.arange(SAMPLES, dtype=jnp.int32)
    counts_drawn = jnp.where(positions == full_at, S, counts_drawn)
    return jnp.where(positions == short_at, S // 8, counts_drawn)


def drawn_entries(key, shape, deviation):
    values = jax.random.normal(key, shape, dtype=jnp.float32)
    return (jnp.clip(values, -4.0, 4.0) * deviation).astype(jnp.bfloat16)


def draw_w_qkv(key, part):
    key = jax.random.fold_in(key, 11)
    return drawn_entries(key, (LAYERS, D, 3, D), (D // 2) ** (-0.5))


def draw_w_out(key, part):
    key = jax.random.fold_in(key, 13)
    return drawn_entries(key, (LAYERS, D, D), (D // 16) ** (-0.5))


def draw_w_up(key, part):
    key = jax.random.fold_in(key, 17)
    return drawn_entries(key, (LAYERS, D, FF), D ** (-0.5))


def draw_w_cross(key, part):
    key = jax.random.fold_in(key, 19)
    return drawn_entries(key, (LAYERS, D, D), (4 * D) ** (-0.5))


def draw_b_cross(key, part):
    key = jax.random.fold_in(key, 23)
    return drawn_entries(key, (LAYERS, D), 0.25)


def steps_of(own_key, shape, shards, least, top_value):
    level, own = 1.0, jax.random.fold_in(own_key, 6)
    for position, blocks in shards:
        draws = jnp.exp(jax.random.uniform(jax.random.fold_in(own, position), (blocks,), jnp.float32, least / len(shards), top_value / len(shards)))
        level = level * jnp.repeat(draws, shape[position] // blocks).reshape([-1 if axis == position else 1 for axis in range(len(shape))])
    return level


def noise(rng, extent, width, most, cuts=(), kind=jnp.bfloat16):
    array = width * jax.random.normal(rng, extent, jnp.float32)
    if cuts:
        array = array * steps_of(rng, extent, cuts, -0.22, 0.18)
    return jnp.clip(array, -most, most).astype(kind)


def setup_inputs(seed: int = 0) -> dict:
    streams_of = jax.random.split(jax.random.key(seed), 12)
    return {
        "tokens": noise(streams_of[0], (TOKENS, D), 1.0, 6.0, ((0, 32),)),
        "lengths": draw_lengths(jax.random.fold_in(streams_of[11], 71), 0),
        "cotangent": noise(streams_of[2], (TOKENS, D), 1.0, 6.0, ((0, 32),)),
        "gain_attn": jnp.clip(1.0 + 0.18 * jax.random.normal(streams_of[3], (LAYERS, D), jnp.float32), 0.1, 1.9),
        "gain_mlp": jnp.clip(1.0 + 0.18 * jax.random.normal(streams_of[4], (LAYERS, D), jnp.float32), 0.1, 1.9),
        "w_qkv": draw_w_qkv(jax.random.fold_in(streams_of[11], 71), 0),
        "w_out": draw_w_out(jax.random.fold_in(streams_of[11], 71), 0),
        "w_up": draw_w_up(jax.random.fold_in(streams_of[11], 71), 0),
        "w_down": noise(streams_of[8], (LAYERS, FF, D), FF ** -0.5, 0.1875, ((1, 4),)),
        "w_cross": draw_w_cross(jax.random.fold_in(streams_of[11], 71), 0),
        "b_cross": draw_b_cross(jax.random.fold_in(streams_of[11], 71), 0),
    }


PRECISE = lax.Precision.HIGHEST
EPSILON = 1e-06

@jax.custom_vjp
def low(v):
    return lax.optimization_barrier(v.astype(jnp.bfloat16)).astype(jnp.float32)

@jax.custom_vjp
def low_back(v):
    return v

def low_keep(v):
    return (low(v), None)

def low_pass(kept, grad):
    return (grad,)

def back_keep(v):
    return (v, None)

def back_low(kept, grad):
    return (low(grad),)
low.defvjp(low_keep, low_pass)
low_back.defvjp(back_keep, back_low)

def rms_norm(values, gain):
    return values * lax.rsqrt(lax.optimization_barrier(jnp.mean(values * values, axis=-1, keepdims=True)) + EPSILON) * gain

def attend(blocked, lengths_blk):
    query_rows = blocked[:, :, 0]
    key_rows = blocked[:, :, 1]
    value_rows = blocked[:, :, 2]
    logits = low_back(jnp.einsum('bqhd,bkhd->bhqk', query_rows, key_rows, precision=PRECISE) * HD ** (-0.5))
    slot_ids = jnp.arange(S, dtype=jnp.int32)
    valid = slot_ids[None, None, None, :] < lengths_blk[:, None, None, None]
    logits = jnp.where(valid, logits, -1000000000.0)
    row_max = lax.optimization_barrier(jnp.max(logits, axis=-1, keepdims=True))
    exponent = jnp.exp(logits - row_max)
    probability = low(exponent / lax.optimization_barrier(jnp.sum(exponent, axis=-1, keepdims=True)))
    return jnp.einsum('bhqk,bkhd->bqhd', probability, value_rows, precision=PRECISE)

def dhen_layer(current, lengths_blk, attn_gain, feed_gain, w_qkv, w_out, w_up, w_down, w_cross, b_cross):
    row_count = current.shape[0]
    normed = low(rms_norm(current, attn_gain))
    qkv = low_back(low(jnp.einsum('rd,dtc->rtc', normed, w_qkv, precision=PRECISE)))
    blocked = qkv.reshape(row_count // S, S, 3, H, HD)
    attn_mix = low_back(low(attend(blocked, lengths_blk))).reshape(row_count, D)
    attended = low_back(jnp.dot(attn_mix, w_out, precision=PRECISE))
    middle = current + attended
    normed_two = low(rms_norm(middle, feed_gain))
    pre_act = low_back(jnp.dot(normed_two, w_up, precision=PRECISE))
    hidden = low(jax.nn.gelu(pre_act, approximate=False))
    feed_out = low_back(jnp.dot(hidden, w_down, precision=PRECISE))
    cross_gate = low_back(jnp.dot(normed, w_cross, precision=PRECISE) + b_cross)
    return middle + feed_out + current * cross_gate

def add_pair(left_term, right_term):
    return left_term + right_term

def reference(tokens, lengths, cotangent, gain_attn, gain_mlp, w_qkv, w_out, w_up, w_down, w_cross, b_cross):
    params = (gain_attn.astype(jnp.float32), gain_mlp.astype(jnp.float32), w_qkv.astype(jnp.float32), w_out.astype(jnp.float32), w_up.astype(jnp.float32), w_down.astype(jnp.float32), w_cross.astype(jnp.float32), b_cross.astype(jnp.float32))
    per_block = math.gcd(SAMPLES, max(1, 4096 // S))
    block_count = SAMPLES // per_block
    token_blocks = tokens.astype(jnp.float32).reshape(block_count, per_block * S, D)
    cot_blocks = cotangent.astype(jnp.float32).reshape(block_count, per_block * S, D)
    length_blocks = lengths.reshape(block_count, per_block)

    def step(totals, operands):
        rows_in, lengths_blk, cot_blk = operands

        def run_forward(current, weights):
            for layer_num in range(LAYERS):
                current = dhen_layer(current, lengths_blk, weights[0][layer_num], weights[1][layer_num], weights[2][layer_num], weights[3][layer_num], weights[4][layer_num], weights[5][layer_num], weights[6][layer_num], weights[7][layer_num])
            return current
        result, pullback = jax.vjp(run_forward, rows_in, params)
        grad_rows, grad_weights = pullback(cot_blk)
        totals = jax.tree.map(add_pair, totals, grad_weights)
        return (totals, (result, grad_rows))
    zeros = jax.tree.map(jnp.zeros_like, params)
    totals, stacked = lax.scan(step, zeros, (token_blocks, length_blocks, cot_blocks))
    output = stacked[0].reshape(TOKENS, D)
    grad_tokens = stacked[1].reshape(TOKENS, D)
    return (output, grad_tokens, totals[0], totals[1], totals[2], totals[3], totals[4], totals[5], totals[6], totals[7])
```

```python
import functools

import jax
import jax.numpy as jnp
from jax import lax
from jax.experimental import pallas as pl
from jax.experimental.pallas import tpu as pltpu
from jax.sharding import PartitionSpec as P

HD = 64
LAYERS = 2
EPSILON = 1e-06
MASKED_SCORE = -1000000000.0
BF = jnp.bfloat16
F32 = jnp.float32

VMEM_LIMIT = 48 * 2**20


def nn(a, b):
    return lax.dot_general(a, b, (((1,), (0,)), ((), ())), preferred_element_type=F32)


def nt(a, b):
    return lax.dot_general(a, b, (((1,), (1,)), ((), ())), preferred_element_type=F32)


def tn(a, b):
    return lax.dot_general(a, b, (((0,), (0,)), ((), ())), preferred_element_type=F32)


def rescale_of(values):
    return lax.rsqrt(jnp.mean(values * values, axis=-1, keepdims=True) + EPSILON)


def norm_back(values, rescale, gain, gradient):
    scaled = gradient * gain
    product_mean = jnp.mean(values * scaled, axis=-1, keepdims=True)
    normal = values * rescale
    grad_values = rescale * (scaled - normal * (rescale * product_mean))
    return grad_values, jnp.sum(gradient * normal, axis=0, keepdims=True)


def gelu_and_slope(u):
    t = 1.0 / (1.0 + (0.3275911 * 0.7071067811865476) * jnp.abs(u))
    e = jnp.exp(-0.5 * (u * u))
    poly = ((((0.5 * 1.061405429) * t - 0.5 * 1.453152027) * t + 0.5 * 1.421413741) * t - 0.5 * 0.284496736) * t + 0.5 * 0.254829592
    tail = poly * t * e
    cdf = jnp.where(u >= 0.0, 1.0 - tail, tail)
    return u * cdf, cdf + u * (e * 0.3989422804014327)


def load_pieces(own, mine, theirs, dst, half_at, sem):
    half = dst.shape[1] // 2
    keep = pl.multiple_of(half_at * half, 16)
    other = pl.multiple_of((1 - half_at) * half, 16)
    copies = [pltpu.make_async_copy(own, dst.at[0], sem)]
    for m, ref in enumerate(mine):
        copies.append(pltpu.make_async_copy(ref, dst.at[m + 1, pl.ds(keep, half)], sem))
    for m, ref in enumerate(theirs):
        copies.append(pltpu.make_async_copy(ref, dst.at[m + 1, pl.ds(other, half)], sem))
    for copy in copies:
        copy.start()
    for copy in copies:
        copy.wait()


def spread_attn(wa, w_cross, w_out, bias, head_at, heads):
    total = jnp.zeros((1, 256), F32)
    for m in range(heads):
        place = pl.multiple_of((head_at ^ m) * HD, HD)
        w_cross[pl.ds(place, HD), :] = wa[m, 192:256, :]
        w_out[m * HD:(m + 1) * HD, :] = wa[m, 256:320, :]
        total = total + wa[m, 320:336, :].astype(F32)[0:1, :]
    bias[...] = jnp.broadcast_to(total, bias.shape)


def attn_fwd_kernel(info, lens, cur_ref, gain_ref, own, m1, m2, m3, t1, t2, t3,
                    middle_ref, base_ref, nrm_ref, qkv_ref, mix_ref, lse_ref,
                    wa, w_cross, w_out, bias, sem):
    step = pl.program_id(0)

    @pl.when(step == 0)
    def _():
        load_pieces(own, (m1, m2, m3), (t1, t2, t3), wa, info[1], sem)
        spread_attn(wa, w_cross, w_out, bias, info[0], 4)

    length = lens[info[2] + step]
    cur = cur_ref[...].astype(F32)
    nrm = (cur * rescale_of(cur) * gain_ref[...]).astype(BF)
    nrm_ref[...] = nrm
    slots = lax.broadcasted_iota(jnp.int32, (256, 256), 0)
    valid = slots < length
    for m in range(4):
        qkv = nt(wa[m, 0:192, :], nrm).astype(BF)
        qkv_ref[m * 192:(m + 1) * 192, :] = qkv
        scores = tn(qkv[64:128], qkv[0:64] * BF(0.125))
        scores = jnp.where(valid, scores, MASKED_SCORE)
        top = jnp.max(scores, axis=0, keepdims=True)
        e = jnp.exp(scores - top)
        total = jnp.sum(e, axis=0, keepdims=True)
        p = (e * (1.0 / total)).astype(BF)
        mix_ref[m * HD:(m + 1) * HD, :] = nn(qkv[128:192], p).astype(BF)
        lse_ref[m:m + 1, :] = top + jnp.log(total)
    middle = cur + tn(mix_ref[...], w_out[...])
    middle_ref[...] = middle
    cross = nt(nrm, w_cross[...]) + bias[0:1, :]
    base_ref[...] = middle + cur * cross


def mlp_fwd_block(middle, gain, wm):
    r = rescale_of(middle)
    n2 = (middle * r * gain).astype(BF)
    feed = None
    kept = []
    for m in range(4):
        u = nn(n2, wm[m, 0:256, :])
        hid, slope = gelu_and_slope(u)
        hid = hid.astype(BF)
        kept.append((hid, slope.astype(BF)))
        part = nn(hid, wm[m, 256:512, :])
        feed = part if feed is None else feed + part
    return r, n2, kept, feed


def mlp_fwd_kernel(info, middle_ref, base_ref, gain_ref, own, m1, m2, m3, t1, t2, t3,
                   out_ref, hid_ref, slope_ref, wm, sem):
    @pl.when(pl.program_id(0) == 0)
    def _():
        load_pieces(own, (m1, m2, m3), (t1, t2, t3), wm, info[1], sem)

    _, _, kept, feed = mlp_fwd_block(middle_ref[...], gain_ref[...], wm)
    for m, (hid, slope) in enumerate(kept):
        hid_ref[:, m * 256:(m + 1) * 256] = hid
        slope_ref[:, m * 256:(m + 1) * 256] = slope
    out_ref[...] = base_ref[...] + feed


def mlp_bwd_block(grad, middle, r, n2, kept, gain, wm, acc, small):
    gf = grad.astype(BF)
    gn = None
    for m in range(4):
        hid, slope = kept[m]
        gp = (nt(gf, wm[m, 256:512, :]) * slope.astype(F32)).astype(BF)
        acc[1, m] += tn(hid, gf)
        acc[0, m] += tn(n2, gp)
        part = nt(gp, wm[m, 0:256, :])
        gn = part if gn is None else gn + part
    back, gain_grad = norm_back(middle, r, gain, gn)
    small[0:1, :] += gain_grad
    return grad + back


def emit_mlp_grads(info, acc, keep_ref, send_ref):
    keep_ref[...] = acc[info[1]].astype(BF)
    send_ref[...] = acc[1 - info[1]].astype(BF)


def mlp_both_kernel(info, middle_ref, base_ref, cot_ref, gain_ref, own, m1, m2, m3, t1, t2, t3,
                    out_ref, gm_ref, keep_ref, send_ref, small_ref, wm, acc, sem):
    step = pl.program_id(0)

    @pl.when(step == 0)
    def _():
        load_pieces(own, (m1, m2, m3), (t1, t2, t3), wm, info[1], sem)
        acc[...] = jnp.zeros_like(acc)
        small_ref[...] = jnp.zeros_like(small_ref)

    middle = middle_ref[...]
    gain = gain_ref[...]
    r, n2, kept, feed = mlp_fwd_block(middle, gain, wm)
    out_ref[...] = base_ref[...] + feed
    grad = cot_ref[...].astype(F32)
    gm_ref[...] = mlp_bwd_block(grad, middle, r, n2, kept, gain, wm, acc, small_ref)

    @pl.when(step == pl.num_programs(0) - 1)
    def _():
        emit_mlp_grads(info, acc, keep_ref, send_ref)


def mlp_bwd_kernel(info, grad_ref, middle_ref, hid_ref, slope_ref, gain_ref, own, m1, m2, m3, t1, t2, t3,
                   gm_ref, keep_ref, send_ref, small_ref, wm, acc, sem):
    step = pl.program_id(0)

    @pl.when(step == 0)
    def _():
        load_pieces(own, (m1, m2, m3), (t1, t2, t3), wm, info[1], sem)
        acc[...] = jnp.zeros_like(acc)
        small_ref[...] = jnp.zeros_like(small_ref)

    middle = middle_ref[...]
    gain = gain_ref[...]
    r = rescale_of(middle)
    n2 = (middle * r * gain).astype(BF)
    kept = [(hid_ref[:, m * 256:(m + 1) * 256], slope_ref[:, m * 256:(m + 1) * 256]) for m in range(4)]
    gm_ref[...] = mlp_bwd_block(grad_ref[...], middle, r, n2, kept, gain, wm, acc, small_ref)

    @pl.when(step == pl.num_programs(0) - 1)
    def _():
        emit_mlp_grads(info, acc, keep_ref, send_ref)


def attn_bwd_kernel(info, lens, grad_ref, gm_ref, cur_ref, nrm_ref, qkv_ref, mix_ref, lse_ref, gain_ref,
                    own, m1, m2, m3, t1, t2, t3,
                    out_ref, keep_ref, send_ref, small_ref,
                    wa, w_cross, w_out, bias, d_qkv, d_cross, d_out, payload, sem):
    step = pl.program_id(0)

    @pl.when(step == 0)
    def _():
        load_pieces(own, (m1, m2, m3), (t1, t2, t3), wa, info[1], sem)
        spread_attn(wa, w_cross, w_out, bias, info[0], 4)
        d_qkv[...] = jnp.zeros_like(d_qkv)
        d_cross[...] = jnp.zeros_like(d_cross)
        d_out[...] = jnp.zeros_like(d_out)
        small_ref[...] = jnp.zeros_like(small_ref)

    length = lens[info[2] + step]
    valid = lax.broadcasted_iota(jnp.int32, (256, 256), 0) < length
    grad = grad_ref[...].astype(F32)
    gm = gm_ref[...]
    cur = cur_ref[...].astype(F32)
    nrm = nrm_ref[...]
    ga = gm.astype(BF)
    d_out[...] += nn(mix_ref[...], ga)
    gmix = nt(w_out[...], ga).astype(BF)
    gc = (grad * cur).astype(BF)
    d_cross[...] += tn(gc, nrm)
    gn = nn(gc, w_cross[...])
    cross = nt(nrm, w_cross[...]) + bias[0:1, :]
    for m in range(4):
        q = qkv_ref[m * 192:m * 192 + 64, :]
        k = qkv_ref[m * 192 + 64:m * 192 + 128, :]
        v = qkv_ref[m * 192 + 128:m * 192 + 192, :]
        go = gmix[m * HD:(m + 1) * HD]
        scores = tn(k, q * BF(0.125))
        scores = jnp.where(valid, scores, MASKED_SCORE)
        p = jnp.exp(scores - lse_ref[m:m + 1, :])
        gv = nt(go, p.astype(BF))
        gp = tn(v, go)
        dot = jnp.sum(gp * p, axis=0, keepdims=True)
        gs = (p * (gp - dot)).astype(BF)
        gq = nn(k, gs) * 0.125
        gk = nt(q, gs) * 0.125
        gqkv = jnp.concatenate([gq, gk, gv], axis=0).astype(BF)
        d_qkv[m * 192:(m + 1) * 192, :] += nn(gqkv, nrm)
        gn = gn + tn(gqkv, wa[m, 0:192, :])
    r = rescale_of(cur)
    back, gain_grad = norm_back(cur, r, gain_ref[...], gn)
    small_ref[0:1, :] += gain_grad
    small_ref[1:2, :] += jnp.sum(gc.astype(F32), axis=0, keepdims=True)
    out_ref[...] = gm + grad * cross + back

    @pl.when(step == pl.num_programs(0) - 1)
    def _():
        for m in range(4):
            place = pl.multiple_of((info[0] ^ m) * HD, HD)
            payload[m, 0:192, :] = d_qkv[m * 192:(m + 1) * 192, :].astype(BF)
            payload[m, 192:256, :] = d_cross[pl.ds(place, HD), :].astype(BF)
            payload[m, 256:320, :] = d_out[m * HD:(m + 1) * HD, :].astype(BF)
        keep = pl.multiple_of(info[1] * 160, 16)
        other = pl.multiple_of((1 - info[1]) * 160, 16)
        for m in range(4):
            keep_ref[m] = payload[m, pl.ds(keep, 160), :]
            send_ref[m] = payload[m, pl.ds(other, 160), :]


SMEM = pl.BlockSpec(memory_space=pltpu.SMEM)
ANY = pl.BlockSpec(memory_space=pl.ANY)


def row_spec(width):
    return pl.BlockSpec((256, width), lambda s: (s, 0))


def col_spec(height):
    return pl.BlockSpec((height, 256), lambda s: (0, s))


def whole(shape):
    return pl.BlockSpec(shape, lambda s: (0,) * len(shape))


def call(kernel, rows, in_specs, outs, scratch, flops, name):
    shapes = [jax.ShapeDtypeStruct(shape, dtype) for shape, dtype, _ in outs]
    return pl.pallas_call(
        kernel,
        grid=(rows // 256,),
        in_specs=in_specs,
        out_specs=[spec for _, _, spec in outs],
        out_shape=shapes,
        scratch_shapes=scratch,
        compiler_params=pltpu.CompilerParams(vmem_limit_bytes=VMEM_LIMIT, dimension_semantics=("arbitrary",)),
        cost_estimate=pl.CostEstimate(flops=flops, bytes_accessed=8 * 2**20, transcendentals=2 * 2**20),
        name=name,
    )


ATTN_SCRATCH = [
    pltpu.VMEM((4, 352, 256), BF),
    pltpu.VMEM((256, 256), BF),
    pltpu.VMEM((256, 256), BF),
    pltpu.VMEM((8, 256), F32),
]


def attn_fwd(info, lens, cur, gain, pieces):
    rows = cur.shape[0]
    outs = [
        ((rows, 256), F32, row_spec(256)),
        ((rows, 256), F32, row_spec(256)),
        ((rows, 256), BF, row_spec(256)),
        ((768, rows), BF, col_spec(768)),
        ((256, rows), BF, col_spec(256)),
        ((8, rows), F32, col_spec(8)),
    ]
    return call(
        attn_fwd_kernel, rows, [SMEM, SMEM, row_spec(256), whole((1, 256))] + [ANY] * 7, outs,
        ATTN_SCRATCH + [pltpu.SemaphoreType.DMA], 2 * 10**9, "attn_fwd",
    )(info, lens, cur, gain, *pieces)


def mlp_fwd(info, middle, base, gain, pieces):
    rows = middle.shape[0]
    outs = [
        ((rows, 256), F32, row_spec(256)),
        ((rows, 1024), BF, row_spec(1024)),
        ((rows, 1024), BF, row_spec(1024)),
    ]
    return call(
        mlp_fwd_kernel, rows, [SMEM, row_spec(256), row_spec(256), whole((1, 256))] + [ANY] * 7, outs,
        [pltpu.VMEM((4, 512, 256), BF), pltpu.SemaphoreType.DMA], 2 * 10**9, "mlp_fwd",
    )(info, middle, base, gain, *pieces)


MLP_GRADS = [
    ((4, 256, 256), BF, whole((4, 256, 256))),
    ((4, 256, 256), BF, whole((4, 256, 256))),
    ((8, 256), F32, whole((8, 256))),
]
MLP_SCRATCH = [
    pltpu.VMEM((4, 512, 256), BF),
    pltpu.VMEM((2, 4, 256, 256), F32),
    pltpu.SemaphoreType.DMA,
]


def mlp_both(info, middle, base, cot, gain, pieces):
    rows = middle.shape[0]
    outs = [((rows, 256), F32, row_spec(256)), ((rows, 256), F32, row_spec(256))] + MLP_GRADS
    return call(
        mlp_both_kernel, rows, [SMEM] + [row_spec(256)] * 3 + [whole((1, 256))] + [ANY] * 7, outs,
        MLP_SCRATCH, 4 * 10**9, "mlp_both",
    )(info, middle, base, cot, gain, *pieces)


def mlp_bwd(info, grad, middle, hid, slope, gain, pieces):
    rows = middle.shape[0]
    outs = [((rows, 256), F32, row_spec(256))] + MLP_GRADS
    return call(
        mlp_bwd_kernel, rows,
        [SMEM, row_spec(256), row_spec(256), row_spec(1024), row_spec(1024), whole((1, 256))] + [ANY] * 7, outs,
        MLP_SCRATCH, 4 * 10**9, "mlp_bwd",
    )(info, grad, middle, hid, slope, gain, *pieces)


def attn_bwd(info, lens, grad, gm, cur, saved, gain, pieces):
    nrm, qkv, mix, lse = saved
    rows = cur.shape[0]
    outs = [
        ((rows, 256), F32, row_spec(256)),
        ((4, 160, 256), BF, whole((4, 160, 256))),
        ((4, 160, 256), BF, whole((4, 160, 256))),
        ((8, 256), F32, whole((8, 256))),
    ]
    scratch = ATTN_SCRATCH + [
        pltpu.VMEM((768, 256), F32),
        pltpu.VMEM((256, 256), F32),
        pltpu.VMEM((256, 256), F32),
        pltpu.VMEM((4, 320, 256), BF),
        pltpu.SemaphoreType.DMA,
    ]
    return call(
        attn_bwd_kernel, rows,
        [SMEM, SMEM] + [row_spec(256)] * 4 + [col_spec(768), col_spec(256), col_spec(8), whole((1, 256))] + [ANY] * 7, outs,
        scratch, 4 * 10**9, "attn_bwd",
    )(info, lens, grad, gm, cur, nrm, qkv, mix, lse, gain, *pieces)


def swap(x, axis, size, mask):
    return lax.ppermute(x, axis, [(i, i ^ mask) for i in range(size)])


def gather_pieces(own, half_at, head_size, dp_size):
    half = own.shape[0] // 2
    part = lax.dynamic_slice_in_dim(own, half_at * half, half, 0)
    mine = [swap(part, "head", head_size, m) for m in range(1, head_size)]
    theirs = [swap(x, "dp", dp_size, 1) for x in mine]
    return [own] + mine + theirs


def add(*terms):
    total = terms[0].astype(F32)
    for term in terms[1:]:
        total = total + term.astype(F32)
    return total


def sum_over_rest(x, dp_size, dtype):
    bit = 2
    while bit < dp_size:
        if bit * 2 < dp_size:
            a, b, c = (swap(x, "dp", dp_size, mask) for mask in (bit, 2 * bit, 3 * bit))
            x = add(x, a) + add(b, c)
            bit *= 4
        else:
            x = add(x, swap(x, "dp", dp_size, bit))
            bit *= 2
        x = x.astype(dtype)
    return x


def reduce_pieces(keep, send, half_at, head_size, dp_size):
    got = swap(send, "dp", dp_size, 1)
    sums = [add(keep[m], got[m]).astype(BF) for m in range(head_size)]
    a, b, c = (swap(sums[m], "head", head_size, m) for m in range(1, head_size))
    mine = (add(sums[0], a) + add(b, c)).astype(BF)
    mine = sum_over_rest(mine, dp_size, BF)
    theirs = swap(mine, "dp", dp_size, 1)
    first = half_at == 0
    return jnp.where(first, mine, theirs).astype(F32), jnp.where(first, theirs, mine).astype(F32)


def sum_all(x, head_size, dp_size):
    x = add(x, swap(x, "dp", dp_size, 1))
    a, b, c = (swap(x, "head", head_size, m) for m in range(1, head_size))
    x = add(x, a) + add(b, c)
    return sum_over_rest(x, dp_size, F32)


def solution(mesh):
    dp_size, head_size = mesh.shape["dp"], mesh.shape["head"]
    reduce_group = functools.partial(reduce_pieces, head_size=head_size, dp_size=dp_size)

    def body(tokens, lengths, cotangent, gain_attn, gain_mlp, w_qkv, w_out, w_up, w_down, w_cross, b_cross):
        head_at = lax.axis_index("head")
        half_at = lax.axis_index("dp") % 2
        samples = tokens.shape[0] // 256
        info = jnp.stack([head_at, half_at, head_at * samples]).astype(jnp.int32)
        width = b_cross.shape[1]
        attn_w, mlp_w = [], []
        for l in range(LAYERS):
            bias = lax.dynamic_update_slice(jnp.zeros((32, 256), BF), b_cross[l][None, :], (0, head_at * width))
            own = jnp.concatenate([
                w_qkv[l].transpose(1, 2, 0).reshape(3 * HD, 256), w_cross[l].T, w_out[l], bias])
            attn_w.append(gather_pieces(own, half_at, head_size, dp_size))
            own = jnp.concatenate([w_up[l], w_down[l]])
            mlp_w.append(gather_pieces(own, half_at, head_size, dp_size))
        ga = [gain_attn[l][None, :] for l in range(LAYERS)]
        gf = [gain_mlp[l][None, :] for l in range(LAYERS)]

        mid0, base0, *saved0 = attn_fwd(info, lengths, tokens, ga[0], attn_w[0])
        cur1, hid0, slope0 = mlp_fwd(info, mid0, base0, gf[0], mlp_w[0])
        mid1, base1, *saved1 = attn_fwd(info, lengths, cur1, ga[1], attn_w[1])
        output, gm1, keep_m1, send_m1, small_m1 = mlp_both(info, mid1, base1, cotangent, gf[1], mlp_w[1])
        grad1, keep_a1, send_a1, small_a1 = attn_bwd(info, lengths, cotangent, gm1, cur1, saved1, ga[1], attn_w[1])
        gm0, keep_m0, send_m0, small_m0 = mlp_bwd(info, grad1, mid0, hid0, slope0, gf[0], mlp_w[0])
        grad0, keep_a0, send_a0, small_a0 = attn_bwd(info, lengths, grad1, gm0, tokens, saved0, ga[0], attn_w[0])

        m1 = reduce_group(keep_m1, send_m1, half_at)
        a1 = reduce_group(keep_a1, send_a1, half_at)
        m0 = reduce_group(keep_m0, send_m0, half_at)
        a0 = reduce_group(keep_a0, send_a0, half_at)
        small = sum_all(
            jnp.concatenate([small_a0[0:2], small_m0[0:1], small_a1[0:2], small_m1[0:1], jnp.zeros((2, 256), F32)]),
            head_size, dp_size)
        attn = [jnp.concatenate(a) for a in (a0, a1)]
        d_qkv = jnp.stack([a[0:192].reshape(3, HD, 256).transpose(2, 0, 1) for a in attn])
        d_cross = jnp.stack([a[192:256].T for a in attn])
        d_out = jnp.stack([a[256:320] for a in attn])
        d_up = jnp.stack([m0[0], m1[0]])
        d_down = jnp.stack([m0[1], m1[1]])
        d_bias = lax.dynamic_slice(small[1:5:3], (0, head_at * width), (LAYERS, width))
        return (output, grad0, small[0:4:3], small[2:6:3], d_qkv, d_out, d_up, d_down, d_cross, d_bias)

    rows, weights = P(("dp", "head"), None), P(None, "head", None)
    return jax.shard_map(
        body,
        mesh=mesh,
        in_specs=(rows, P("dp"), rows, P(), P(), P(None, None, None, "head"), weights, P(None, None, "head"),
                  weights, P(None, None, "head"), P(None, "head")),
        out_specs=(rows, rows, P(), P(), P(None, None, None, "head"), weights, P(None, None, "head"),
                   weights, P(None, None, "head"), P(None, "head")),
        check_vma=False,
    )
```

```python
import functools

import jax
import jax.numpy as jnp
from jax import lax
from jax.experimental import pallas as pl
from jax.experimental.pallas import tpu as pltpu
from jax.sharding import PartitionSpec as P

HD = 64
LAYERS = 2
EPSILON = 1e-06
MASKED_SCORE = -1000000000.0
BF = jnp.bfloat16
F32 = jnp.float32

VMEM_LIMIT = 32 * 2**20
SMALL_LIMIT = 12 * 2**20
KERNEL_FLOPS = 1000


def nn(a, b):
    return lax.dot_general(a, b, (((1,), (0,)), ((), ())), preferred_element_type=F32)


def nt(a, b):
    return lax.dot_general(a, b, (((1,), (1,)), ((), ())), preferred_element_type=F32)


def tn(a, b):
    return lax.dot_general(a, b, (((0,), (0,)), ((), ())), preferred_element_type=F32)


def rescale_of(values):
    return lax.rsqrt(jnp.mean(values * values, axis=-1, keepdims=True) + EPSILON)


def norm_back(values, rescale, gain, gradient):
    scaled = gradient * gain
    product_mean = jnp.mean(values * scaled, axis=-1, keepdims=True)
    normal = values * rescale
    grad_values = rescale * (scaled - normal * (rescale * product_mean))
    return grad_values, jnp.sum(gradient * normal, axis=0, keepdims=True)


def gelu_and_slope(u):
    t = 1.0 / (1.0 + (0.3275911 * 0.7071067811865476) * jnp.abs(u))
    e = jnp.exp(-0.5 * (u * u))
    poly = ((((0.5 * 1.061405429) * t - 0.5 * 1.453152027) * t + 0.5 * 1.421413741) * t - 0.5 * 0.284496736) * t + 0.5 * 0.254829592
    tail = poly * t * e
    cdf = jnp.where(u >= 0.0, 1.0 - tail, tail)
    return u * cdf, cdf + u * (e * 0.3989422804014327)


def head_index():
    return lax.axis_index("head")


def half_index():
    return lax.axis_index("dp") & 1


def load_pieces(own, mine, theirs, dst, half_at, sem, first=0):
    half = dst.shape[1] // 2
    keep = pl.multiple_of(half_at * half, 16)
    other = pl.multiple_of((1 - half_at) * half, 16)
    copies = []
    at = 0
    for ref in own:
        copies.append(pltpu.make_async_copy(ref, dst.at[0, pl.ds(at, ref.shape[0])], sem))
        at += ref.shape[0]
    for m, ref in enumerate(mine):
        copies.append(pltpu.make_async_copy(ref.at[pl.ds(first, half)], dst.at[m + 1, pl.ds(keep, half)], sem))
    for m, ref in enumerate(theirs):
        copies.append(pltpu.make_async_copy(ref.at[pl.ds(first, half)], dst.at[m + 1, pl.ds(other, half)], sem))
    for copy in copies:
        copy.start()
    for copy in copies:
        copy.wait()


def spread_attn(wa, w_cross, w_out, bias, head_at, heads):
    total = jnp.zeros((1, 256), F32)
    for m in range(heads):
        place = pl.multiple_of((head_at ^ m) * HD, HD)
        w_cross[pl.ds(place, HD), :] = wa[m, 192:256, :]
        w_out[m * HD:(m + 1) * HD, :] = wa[m, 256:320, :]
        total = total + wa[m, 320:336, :].astype(F32)[0:1, :]
    bias[...] = jnp.broadcast_to(total, bias.shape)


def attn_fwd_kernel(layer, first, lens, cur_ref, gain_ref, own, m1, m2, m3, t1, t2, t3,
                    middle_ref, base_ref, nrm_ref, qkv_ref, mix_ref, lse_ref,
                    wa, w_cross, w_out, bias, sem):
    step = pl.program_id(0)

    @pl.when(step == 0)
    def _():
        load_pieces((own,), (m1, m2, m3), (t1, t2, t3), wa, half_index(), sem, first)
        spread_attn(wa, w_cross, w_out, bias, head_index(), 4)

    length = lens[head_index() * pl.num_programs(0) + step]
    cur = cur_ref[...].astype(F32)
    nrm = (cur * rescale_of(cur) * gain_ref[layer:layer + 1, :]).astype(BF)
    nrm_ref[...] = nrm
    slots = lax.broadcasted_iota(jnp.int32, (256, 256), 0)
    valid = slots < length
    for m in range(4):
        qkv = nt(wa[m, 0:192, :], nrm).astype(BF)
        qkv_ref[m * 192:(m + 1) * 192, :] = qkv
        scores = tn(qkv[64:128], qkv[0:64] * BF(0.125))
        scores = jnp.where(valid, scores, MASKED_SCORE)
        top = jnp.max(scores, axis=0, keepdims=True)
        e = jnp.exp(scores - top)
        total = jnp.sum(e, axis=0, keepdims=True)
        p = (e * (1.0 / total)).astype(BF)
        mix_ref[m * HD:(m + 1) * HD, :] = nn(qkv[128:192], p).astype(BF)
        lse_ref[m:m + 1, :] = top + jnp.log(total)
    middle = cur + tn(mix_ref[...], w_out[...])
    middle_ref[...] = middle
    cross = nt(nrm, w_cross[...]) + bias[0:1, :]
    base_ref[...] = middle + cur * cross


def mlp_fwd_block(middle, gain, wm):
    r = rescale_of(middle)
    n2 = (middle * r * gain).astype(BF)
    feed = None
    kept = []
    for m in range(4):
        u = nn(n2, wm[m, 0:256, :])
        hid, slope = gelu_and_slope(u)
        hid = hid.astype(BF)
        kept.append((hid, slope.astype(BF)))
        part = nn(hid, wm[m, 256:512, :])
        feed = part if feed is None else feed + part
    return r, n2, kept, feed


def mlp_fwd_kernel(layer, first, middle_ref, base_ref, gain_ref, up, down, m1, m2, m3, t1, t2, t3,
                   out_ref, hid_ref, slope_ref, wm, sem):
    @pl.when(pl.program_id(0) == 0)
    def _():
        load_pieces((up.at[layer], down.at[layer]), (m1, m2, m3), (t1, t2, t3), wm, half_index(), sem, first)

    _, _, kept, feed = mlp_fwd_block(middle_ref[...], gain_ref[layer:layer + 1, :], wm)
    for m, (hid, slope) in enumerate(kept):
        hid_ref[:, m * 256:(m + 1) * 256] = hid
        slope_ref[:, m * 256:(m + 1) * 256] = slope
    out_ref[...] = base_ref[...] + feed


def mlp_bwd_block(grad, middle, r, n2, kept, gain, wm, acc, small):
    gf = grad.astype(BF)
    gn = None
    for m in range(4):
        hid, slope = kept[m]
        gp = (nt(gf, wm[m, 256:512, :]) * slope.astype(F32)).astype(BF)
        acc[1, m] += tn(hid, gf)
        acc[0, m] += tn(n2, gp)
        part = nt(gp, wm[m, 0:256, :])
        gn = part if gn is None else gn + part
    back, gain_grad = norm_back(middle, r, gain, gn)
    small[0:1, :] += gain_grad
    return grad + back


def emit_mlp_grads(acc, keep_ref, send_ref):
    keep_ref[...] = acc[half_index()].astype(BF)
    send_ref[...] = acc[1 - half_index()].astype(BF)


def mlp_both_kernel(layer, first, middle_ref, base_ref, cot_ref, gain_ref, up, down, m1, m2, m3, t1, t2, t3,
                    out_ref, gm_ref, keep_ref, send_ref, small_ref, wm, acc, sem):
    step = pl.program_id(0)

    @pl.when(step == 0)
    def _():
        load_pieces((up.at[layer], down.at[layer]), (m1, m2, m3), (t1, t2, t3), wm, half_index(), sem, first)
        acc[...] = jnp.zeros_like(acc)
        small_ref[...] = jnp.zeros_like(small_ref)

    middle = middle_ref[...]
    gain = gain_ref[layer:layer + 1, :]
    r, n2, kept, feed = mlp_fwd_block(middle, gain, wm)
    out_ref[...] = base_ref[...] + feed
    grad = cot_ref[...].astype(F32)
    gm_ref[...] = mlp_bwd_block(grad, middle, r, n2, kept, gain, wm, acc, small_ref)

    @pl.when(step == pl.num_programs(0) - 1)
    def _():
        emit_mlp_grads(acc, keep_ref, send_ref)


def mlp_bwd_kernel(layer, first, grad_ref, middle_ref, hid_ref, slope_ref, gain_ref, up, down, m1, m2, m3, t1, t2, t3,
                   gm_ref, keep_ref, send_ref, small_ref, wm, acc, sem):
    step = pl.program_id(0)

    @pl.when(step == 0)
    def _():
        load_pieces((up.at[layer], down.at[layer]), (m1, m2, m3), (t1, t2, t3), wm, half_index(), sem, first)
        acc[...] = jnp.zeros_like(acc)
        small_ref[...] = jnp.zeros_like(small_ref)

    middle = middle_ref[...]
    gain = gain_ref[layer:layer + 1, :]
    r = rescale_of(middle)
    n2 = (middle * r * gain).astype(BF)
    kept = [(hid_ref[:, m * 256:(m + 1) * 256], slope_ref[:, m * 256:(m + 1) * 256]) for m in range(4)]
    gm_ref[...] = mlp_bwd_block(grad_ref[...], middle, r, n2, kept, gain, wm, acc, small_ref)

    @pl.when(step == pl.num_programs(0) - 1)
    def _():
        emit_mlp_grads(acc, keep_ref, send_ref)


def attn_bwd_kernel(layer, first, lens, grad_ref, gm_ref, cur_ref, nrm_ref, qkv_ref, mix_ref, lse_ref, gain_ref, mlp_small,
                    own, m1, m2, m3, t1, t2, t3,
                    out_ref, keep_ref, send_ref,
                    wa, w_cross, w_out, bias, d_qkv, d_cross, d_out, payload, small_ref, sem):
    step = pl.program_id(0)

    @pl.when(step == 0)
    def _():
        load_pieces((own,), (m1, m2, m3), (t1, t2, t3), wa, half_index(), sem, first)
        spread_attn(wa, w_cross, w_out, bias, head_index(), 4)
        d_qkv[...] = jnp.zeros_like(d_qkv)
        d_cross[...] = jnp.zeros_like(d_cross)
        d_out[...] = jnp.zeros_like(d_out)
        small_ref[...] = jnp.zeros_like(small_ref)
        small_ref[2:3, :] = mlp_small[0:1, :]

    length = lens[head_index() * pl.num_programs(0) + step]
    valid = lax.broadcasted_iota(jnp.int32, (256, 256), 0) < length
    grad = grad_ref[...].astype(F32)
    gm = gm_ref[...]
    cur = cur_ref[...].astype(F32)
    nrm = nrm_ref[...]
    ga = gm.astype(BF)
    d_out[...] += nn(mix_ref[...], ga)
    gmix = nt(w_out[...], ga).astype(BF)
    gc = (grad * cur).astype(BF)
    d_cross[...] += tn(gc, nrm)
    gn = nn(gc, w_cross[...])
    cross = nt(nrm, w_cross[...]) + bias[0:1, :]
    for m in range(4):
        q = qkv_ref[m * 192:m * 192 + 64, :]
        k = qkv_ref[m * 192 + 64:m * 192 + 128, :]
        v = qkv_ref[m * 192 + 128:m * 192 + 192, :]
        go = gmix[m * HD:(m + 1) * HD]
        scores = tn(k, q * BF(0.125))
        scores = jnp.where(valid, scores, MASKED_SCORE)
        p = jnp.exp(scores - lse_ref[m:m + 1, :])
        gv = nt(go, p.astype(BF))
        gp = tn(v, go)
        dot = jnp.sum(gp * p, axis=0, keepdims=True)
        gs = (p * (gp - dot)).astype(BF)
        gq = nn(k, gs) * 0.125
        gk = nt(q, gs) * 0.125
        gqkv = jnp.concatenate([gq, gk, gv], axis=0).astype(BF)
        d_qkv[m * 192:(m + 1) * 192, :] += nn(gqkv, nrm)
        gn = gn + tn(gqkv, wa[m, 0:192, :])
    r = rescale_of(cur)
    back, gain_grad = norm_back(cur, r, gain_ref[layer:layer + 1, :], gn)
    small_ref[0:1, :] += gain_grad
    small_ref[1:2, :] += jnp.sum(gc.astype(F32), axis=0, keepdims=True)
    out_ref[...] = gm + grad * cross + back

    @pl.when(step == pl.num_programs(0) - 1)
    def _():
        high, low = split_rows(small_ref[...])
        for m in range(4):
            place = pl.multiple_of((head_index() ^ m) * HD, HD)
            payload[m, 0:192, :] = d_qkv[m * 192:(m + 1) * 192, :].astype(BF)
            payload[m, 192:256, :] = d_cross[pl.ds(place, HD), :].astype(BF)
            payload[m, 256:320, :] = d_out[m * HD:(m + 1) * HD, :].astype(BF)
        keep = pl.multiple_of(half_index() * 160, 16)
        other = pl.multiple_of((1 - half_index()) * 160, 16)
        for m in range(4):
            for ref, at in ((keep_ref, keep), (send_ref, other)):
                ref[m, 0:160, :] = payload[m, pl.ds(at, 160), :]
                ref[m, 160:168, :] = high
                ref[m, 168:176, :] = low


def split_rows(x):
    high = x.astype(BF)
    return high, (x - high.astype(F32)).astype(BF)


def pack_kernel(qkv, cross, out, up, down, b, own0, own1, half_a0, half_r, half_m1, sems):
    copies = []
    for l, own in ((0, own0), (1, own1)):
        for t in range(3):
            copies.append(pltpu.make_async_copy(qkv.at[l, t], own.at[pl.ds(t * HD, HD)], sems.at[0]))
        copies.append(pltpu.make_async_copy(cross.at[l], own.at[pl.ds(192, HD)], sems.at[0]))
        copies.append(pltpu.make_async_copy(out.at[l], own.at[pl.ds(256, HD)], sems.at[0]))
    for copy in copies:
        copy.start()

    def mlp_half(weight):
        return (pltpu.make_async_copy(weight.at[0], half_r.at[pl.ds(0, 256)], sems.at[1]),
                pltpu.make_async_copy(weight.at[1], half_m1, sems.at[1]))

    @pl.when(half_index() == 0)
    def _():
        for copy in mlp_half(up):
            copy.start()

    @pl.when(half_index() != 0)
    def _():
        for copy in mlp_half(down):
            copy.start()

    lane = lax.broadcasted_iota(jnp.int32, (LAYERS, 256), 1) // HD
    wide = jnp.concatenate([b[...].astype(F32)] * 4, axis=1)
    wide = jnp.where(lane == head_index(), wide, 0.0)
    for l, own in ((0, own0), (1, own1)):
        own[320:352, :] = jnp.broadcast_to(wide[l:l + 1], (32, 256)).astype(BF)
    for copy in copies:
        copy.wait()
    at = pl.multiple_of(half_index() * 176, 16)
    half_a0[...] = own0[pl.ds(at, 176), :]
    half_r[256:432, :] = own1[pl.ds(at, 176), :]
    for copy in mlp_half(up):
        copy.wait()


def put_sum(out, at, small_at, rows, total):
    for low, high in ((0, small_at), (small_at + 16, rows)):
        if low < high:
            out[at + low:at + high, :] = total(low, high).astype(BF)
    if small_at < rows:
        both = total(small_at, small_at + 16)
        high, low = split_rows(both[0:8] + both[8:16])
        out[at + small_at:at + small_at + 8, :] = high
        out[at + small_at + 8:at + small_at + 16, :] = low


def core_sum_kernel(small_at, *refs):
    ins, outs = refs[:-4], refs[-4:]
    for m, out in enumerate(outs):
        at = 0
        for where, keep, got in zip(small_at, ins[0::2], ins[1::2]):
            rows = keep.shape[1]
            put_sum(out, at, where, rows, lambda i, j: keep[m, i:j].astype(F32) + got[m, i:j].astype(F32))
            at += rows


def four_sum_kernel(small_at, copied, *refs):
    done, refs, out = refs[:copied], refs[copied:-1], refs[-1]
    at = 0
    for ref in done:
        out[at:at + ref.shape[0], :] = ref[...]
        at += ref.shape[0]
    for i, where in enumerate(small_at):
        s, a, b, c = refs[4 * i:4 * i + 4]
        rows = s.shape[0]
        put_sum(out, at, where, rows, lambda i, j: (s[i:j].astype(F32) + a[i:j].astype(F32)) + (b[i:j].astype(F32) + c[i:j].astype(F32)))
        at += rows


def finish_kernel(early, early_other, late, late_other,
                  d_qkv, d_out, d_up, d_down, d_cross, gain_attn, gain_mlp, bias):
    def place(first, second, late_first, late_second):
        for l, a, b, at in ((1, first, second, 256), (0, late_first, late_second, 0)):
            d_qkv[l, 0] = a[at:at + 64].astype(F32)
            d_qkv[l, 1] = a[at + 64:at + 128].astype(F32)
            d_qkv[l, 2, 0:32] = a[at + 128:at + 160].astype(F32)
            d_qkv[l, 2, 32:64] = b[at:at + 32].astype(F32)
            d_cross[l] = b[at + 32:at + 96].astype(F32)
            d_out[l] = b[at + 96:at + 160].astype(F32)
        for l, at in ((1, 0), (0, 432)):
            d_up[l] = first[at:at + 256].astype(F32)
            d_down[l] = second[at:at + 256].astype(F32)

    @pl.when(half_index() == 0)
    def _():
        place(early, early_other, late, late_other)

    @pl.when(half_index() != 0)
    def _():
        place(early_other, early, late_other, late)

    for l, ref, at in ((0, late, 160), (1, early, 416)):
        rows = ref[at:at + 8].astype(F32) + ref[at + 8:at + 16].astype(F32)
        gain_attn[l:l + 1, :] = rows[0:1]
        gain_mlp[l:l + 1, :] = rows[2:3]
        total = jnp.zeros((1, HD), F32)
        for h in range(4):
            total = total + jnp.where(head_index() == h, rows[1:2, h * HD:(h + 1) * HD], 0.0)
        bias[l:l + 1, :] = total


SMEM = pl.BlockSpec(memory_space=pltpu.SMEM)
ANY = pl.BlockSpec(memory_space=pl.ANY)


def row_spec(width):
    return pl.BlockSpec((256, width), lambda s: (s, 0))


def col_spec(height):
    return pl.BlockSpec((height, 256), lambda s: (0, s))


def whole(shape):
    return pl.BlockSpec(shape, lambda s: (0,) * len(shape))


def call(kernel, rows, in_specs, outs, scratch, flops, name):
    shapes = [jax.ShapeDtypeStruct(shape, dtype) for shape, dtype, _ in outs]
    return pl.pallas_call(
        kernel,
        grid=(rows // 256,),
        in_specs=in_specs,
        out_specs=[spec for _, _, spec in outs],
        out_shape=shapes,
        scratch_shapes=scratch,
        compiler_params=pltpu.CompilerParams(vmem_limit_bytes=VMEM_LIMIT, dimension_semantics=("arbitrary",)),
        cost_estimate=pl.CostEstimate(flops=flops, bytes_accessed=1024, transcendentals=0),
        name=name,
    )


ATTN_SCRATCH = [
    pltpu.VMEM((4, 352, 256), BF),
    pltpu.VMEM((256, 256), BF),
    pltpu.VMEM((256, 256), BF),
    pltpu.VMEM((8, 256), F32),
]


def attn_fwd(layer, first, lens, cur, gain, pieces):
    rows = cur.shape[0]
    outs = [
        ((rows, 256), F32, row_spec(256)),
        ((rows, 256), F32, row_spec(256)),
        ((rows, 256), BF, row_spec(256)),
        ((768, rows), BF, col_spec(768)),
        ((256, rows), BF, col_spec(256)),
        ((8, rows), F32, col_spec(8)),
    ]
    return call(
        functools.partial(attn_fwd_kernel, layer, first), rows, [SMEM, row_spec(256), whole((LAYERS, 256))] + [ANY] * 7, outs,
        ATTN_SCRATCH + [pltpu.SemaphoreType.DMA], KERNEL_FLOPS, "attn_fwd",
    )(lens, cur, gain, *pieces)


def mlp_fwd(layer, first, middle, base, gain, pieces):
    rows = middle.shape[0]
    outs = [
        ((rows, 256), F32, row_spec(256)),
        ((rows, 1024), BF, row_spec(1024)),
        ((rows, 1024), BF, row_spec(1024)),
    ]
    return call(
        functools.partial(mlp_fwd_kernel, layer, first), rows, [row_spec(256), row_spec(256), whole((LAYERS, 256))] + [ANY] * 8, outs,
        [pltpu.VMEM((4, 512, 256), BF), pltpu.SemaphoreType.DMA], KERNEL_FLOPS, "mlp_fwd",
    )(middle, base, gain, *pieces)


MLP_GRADS = [
    ((4, 256, 256), BF, whole((4, 256, 256))),
    ((4, 256, 256), BF, whole((4, 256, 256))),
    ((8, 256), F32, whole((8, 256))),
]
MLP_SCRATCH = [
    pltpu.VMEM((4, 512, 256), BF),
    pltpu.VMEM((2, 4, 256, 256), F32),
    pltpu.SemaphoreType.DMA,
]


def mlp_both(layer, first, middle, base, cot, gain, pieces):
    rows = middle.shape[0]
    outs = [((rows, 256), F32, row_spec(256)), ((rows, 256), F32, row_spec(256))] + MLP_GRADS
    return call(
        functools.partial(mlp_both_kernel, layer, first), rows, [row_spec(256)] * 3 + [whole((LAYERS, 256))] + [ANY] * 8, outs,
        MLP_SCRATCH, KERNEL_FLOPS, "mlp_both",
    )(middle, base, cot, gain, *pieces)


def mlp_bwd(layer, first, grad, middle, hid, slope, gain, pieces):
    rows = middle.shape[0]
    outs = [((rows, 256), F32, row_spec(256))] + MLP_GRADS
    return call(
        functools.partial(mlp_bwd_kernel, layer, first), rows,
        [row_spec(256), row_spec(256), row_spec(1024), row_spec(1024), whole((LAYERS, 256))] + [ANY] * 8, outs,
        MLP_SCRATCH, KERNEL_FLOPS, "mlp_bwd",
    )(grad, middle, hid, slope, gain, *pieces)


def attn_bwd(layer, first, lens, grad, gm, cur, saved, gain, mlp_small, pieces):
    nrm, qkv, mix, lse = saved
    rows = cur.shape[0]
    outs = [
        ((rows, 256), F32, row_spec(256)),
        ((4, 176, 256), BF, whole((4, 176, 256))),
        ((4, 176, 256), BF, whole((4, 176, 256))),
    ]
    scratch = ATTN_SCRATCH + [
        pltpu.VMEM((768, 256), F32),
        pltpu.VMEM((256, 256), F32),
        pltpu.VMEM((256, 256), F32),
        pltpu.VMEM((4, 320, 256), BF),
        pltpu.VMEM((8, 256), F32),
        pltpu.SemaphoreType.DMA,
    ]
    return call(
        functools.partial(attn_bwd_kernel, layer, first), rows,
        [SMEM] + [row_spec(256)] * 4 + [col_spec(768), col_spec(256), col_spec(8), whole((LAYERS, 256)), whole((8, 256))] + [ANY] * 7, outs,
        scratch, KERNEL_FLOPS, "attn_bwd",
    )(lens, grad, gm, cur, nrm, qkv, mix, lse, gain, mlp_small, *pieces)


VMEM = pl.BlockSpec(memory_space=pltpu.VMEM)


def small_call(kernel, shapes, name):
    def run(*args):
        return pl.pallas_call(
            kernel,
            in_specs=[VMEM] * len(args),
            out_specs=[VMEM] * len(shapes),
            out_shape=[jax.ShapeDtypeStruct(shape, dtype) for shape, dtype in shapes],
            compiler_params=pltpu.CompilerParams(vmem_limit_bytes=SMALL_LIMIT),
            cost_estimate=pl.CostEstimate(flops=1000, bytes_accessed=1024, transcendentals=0),
            name=name,
        )(*args)
    return run


def core_sum(small_at, *groups):
    rows = sum(keep.shape[1] for keep, _ in groups)
    return small_call(functools.partial(core_sum_kernel, small_at), [((rows, 256), BF)] * 4, "core_sum")(
        *[x for group in groups for x in group])


def four_sum(small_at, *groups, done=()):
    rows = sum(x.shape[0] for x in done) + sum(group[0].shape[0] for group in groups)
    return small_call(functools.partial(four_sum_kernel, small_at, len(done)), [((rows, 256), BF)], "four_sum")(
        *done, *[x for group in groups for x in group])[0]


def swap(x, axis, size, mask):
    return lax.ppermute(x, axis, [(i, i ^ mask) for i in range(size)])


def tie(x, *before):
    return lax.optimization_barrier((x,) + before)[0]


def solution(mesh):
    dp_size, head_size = mesh.shape["dp"], mesh.shape["head"]

    def core_swap(x):
        return swap(x, "dp", dp_size, 1)

    def fetch(x):
        return [swap(x, "head", head_size, m) for m in range(1, head_size)]

    def scatter(sums):
        return [sums[0]] + [swap(sums[m], "head", head_size, m) for m in range(1, head_size)]

    def spread(x, bit):
        return [x] + [swap(x, "dp", dp_size, m * bit) for m in (1, 2, 3)]

    def sum_rest(x, small_at, before=()):
        bit = 2
        while bit < dp_size:
            if bit * 2 < dp_size:
                x = four_sum((small_at,), [tie(term, *before) for term in spread(x, bit)])
            else:
                x = four_sum((small_at,), [x, swap(x, "dp", dp_size, bit), jnp.zeros_like(x), jnp.zeros_like(x)])
            bit *= 4
        return x

    def body(tokens, lengths, cotangent, gain_attn, gain_mlp, w_qkv, w_out, w_up, w_down, w_cross, b_cross):
        own0, own1, half_a0, half_r, half_m1 = pl.pallas_call(
            pack_kernel,
            in_specs=[ANY] * 5 + [VMEM],
            out_specs=[VMEM] * 5,
            out_shape=[jax.ShapeDtypeStruct((n, 256), BF) for n in (352, 352, 176, 432, 256)],
            scratch_shapes=[pltpu.SemaphoreType.DMA((2,))],
            name="pack",
        )(w_qkv.transpose(0, 2, 3, 1), w_cross.transpose(0, 2, 1), w_out, w_up, w_down, b_cross)

        a0 = fetch(half_a0)
        r = fetch(half_r)
        m1 = fetch(half_m1)
        pieces_a0 = [own0] + a0 + [core_swap(x) for x in a0]
        mid0, base0, *saved0 = attn_fwd(0, 0, lengths, tokens, gain_attn, pieces_a0)
        r = [tie(x, mid0) for x in r]
        r = r + [core_swap(x) for x in r]
        cur1, hid0, slope0 = mlp_fwd(0, 0, mid0, base0, gain_mlp, [w_up, w_down] + r)
        mid1, base1, *saved1 = attn_fwd(1, 256, lengths, cur1, gain_attn, [own1] + r)
        m1 = [tie(x, mid1) for x in m1]
        m1 = m1 + [core_swap(x) for x in m1]
        output, gm1, keep_m1, send_m1, small_m1 = mlp_both(1, 0, mid1, base1, cotangent, gain_mlp, [w_up, w_down] + m1)
        sums_m1 = core_sum((256,), (keep_m1, core_swap(send_m1)))
        got_m1 = scatter(sums_m1)
        grad1, keep_a1, send_a1 = attn_bwd(
            1, 256, lengths, cotangent, tie(gm1, *sums_m1), cur1, saved1, gain_attn, small_m1, [own1] + r)
        early = four_sum((256,), [tie(x, grad1) for x in got_m1])
        got_a1 = core_swap(send_a1)
        gm0, keep_m0, send_m0, small_m0 = mlp_bwd(0, 0, tie(grad1, early), mid0, hid0, slope0, gain_mlp, [w_up, w_down] + r)
        sums = core_sum((160, 256), (keep_a1, tie(got_a1, gm0)), (keep_m0, core_swap(send_m0)))
        got = scatter(sums)
        grad0, keep_a0, send_a0 = attn_bwd(
            0, 0, lengths, grad1, tie(gm0, *sums), tokens, saved0, gain_attn, small_m0, pieces_a0)
        early = four_sum((160,), [tie(x, grad0) for x in got], done=(early,))
        sums_a0 = core_sum((160,), (keep_a0, core_swap(tie(send_a0, early))))
        late = scatter(sums_a0)
        early = sum_rest(early, 416, late[1:])
        late = four_sum((160,), late)
        late = sum_rest(late, 160)
        d_qkv, d_out, d_up, d_down, d_cross, d_ga, d_gm, d_bias = small_call(
            finish_kernel,
            [((LAYERS, 3, HD, 256), F32), ((LAYERS, HD, 256), F32), ((LAYERS, 256, 256), F32), ((LAYERS, 256, 256), F32),
             ((LAYERS, HD, 256), F32), ((LAYERS, 256), F32), ((LAYERS, 256), F32), ((LAYERS, HD), F32)],
            "finish",
        )(early, core_swap(early), late, core_swap(late))
        return (output, grad0, d_ga, d_gm, d_qkv.transpose(0, 3, 1, 2), d_out, d_up, d_down,
                d_cross.transpose(0, 2, 1), d_bias)

    rows, weights = P(("dp", "head"), None), P(None, "head", None)
    return jax.shard_map(
        body,
        mesh=mesh,
        in_specs=(rows, P("dp"), rows, P(), P(), P(None, None, None, "head"), weights, P(None, None, "head"),
                  weights, P(None, None, "head"), P(None, "head")),
        out_specs=(rows, rows, P(), P(), P(None, None, None, "head"), weights, P(None, None, "head"),
                   weights, P(None, None, "head"), P(None, "head")),
        check_vma=False,
    )
```

```python
import functools

import jax
import jax.numpy as jnp
from jax import lax
from jax.experimental import pallas as pl
from jax.experimental.pallas import tpu as pltpu
from jax.sharding import PartitionSpec as P

HD = 64
LAYERS = 2
EPSILON = 1e-06
MASKED_SCORE = -1000000000.0
BF = jnp.bfloat16
F32 = jnp.float32

VMEM_LIMIT = 32 * 2**20
SMALL_LIMIT = 12 * 2**20
KERNEL_FLOPS = 1000


def nn(a, b):
    return lax.dot_general(a, b, (((1,), (0,)), ((), ())), preferred_element_type=F32)


def nt(a, b):
    return lax.dot_general(a, b, (((1,), (1,)), ((), ())), preferred_element_type=F32)


def tn(a, b):
    return lax.dot_general(a, b, (((0,), (0,)), ((), ())), preferred_element_type=F32)


def rescale_of(values):
    return lax.rsqrt(jnp.mean(values * values, axis=-1, keepdims=True) + EPSILON)


def norm_back(values, rescale, gain, gradient):
    scaled = gradient * gain
    product_mean = jnp.mean(values * scaled, axis=-1, keepdims=True)
    normal = values * rescale
    grad_values = rescale * (scaled - normal * (rescale * product_mean))
    return grad_values, jnp.sum(gradient * normal, axis=0, keepdims=True)


def gelu_and_slope(u):
    d = 1.0 + (0.3275911 * 0.7071067811865476) * jnp.abs(u)
    t = pl.reciprocal(d, approx=True)
    t = t * (2.0 - d * t)
    e = jnp.exp2((-0.5 * 1.4426950408889634) * (u * u))
    poly = ((((0.5 * 1.061405429) * t - 0.5 * 1.453152027) * t + 0.5 * 1.421413741) * t - 0.5 * 0.284496736) * t + 0.5 * 0.254829592
    tail = poly * t * e
    cdf = jnp.where(u >= 0.0, 1.0 - tail, tail)
    return u * cdf, cdf + u * (e * 0.3989422804014327)


def head_index():
    return lax.axis_index("head")


def half_index():
    return lax.axis_index("dp") & 1


def place_pieces(own, mine, theirs, dst, first=0):
    half = dst.shape[1] // 2
    keep = pl.multiple_of(half_index() * half, 16)
    other = pl.multiple_of((1 - half_index()) * half, 16)
    at = 0
    for part in own:
        dst[0, at:at + part.shape[0], :] = part
        at += part.shape[0]
    for m in range(3):
        dst[m + 1, pl.ds(keep, half), :] = mine[m][first:first + half, :]
        dst[m + 1, pl.ds(other, half), :] = theirs[m][first:first + half, :]


def place_attn(first, pieces, wa, w_cross, w_out):
    place_pieces((pieces[0][...],), pieces[1:4], pieces[4:7], wa, first)
    total = jnp.zeros((1, 256), F32)
    for m in range(4):
        place = pl.multiple_of((head_index() ^ m) * HD, HD)
        w_cross[pl.ds(place, HD), :] = wa[m, 192:256, :]
        w_out[m * HD:(m + 1) * HD, :] = wa[m, 256:320, :]
        total = total + wa[m, 320:336, :].astype(F32)[0:1, :]
    return total


def place_mlp(layer, first, pieces, wm):
    place_pieces((pieces[0][layer], pieces[1][layer]), pieces[2:5], pieces[5:8], wm, first)


def attn_fwd_kernel(layer, first, cur_ref, mask_ref, gain_ref, p0, p1, p2, p3, p4, p5, p6,
                    middle_ref, base_ref, nrm_ref, qkv_ref, mix_ref, lse_ref, wa, w_cross, w_out):
    bias = place_attn(first, (p0, p1, p2, p3, p4, p5, p6), wa, w_cross, w_out)
    gain = gain_ref[layer:layer + 1, :]
    for s in range(cur_ref.shape[0] // 256):
        rows = slice(s * 256, s * 256 + 256)
        cur = cur_ref[rows, :].astype(F32)
        nrm = (cur * rescale_of(cur) * gain).astype(BF)
        nrm_ref[rows, :] = nrm
        mask = jnp.concatenate([mask_ref[rows, :]] * 2, axis=1)
        qkv = [nt(wa[m, 0:192, :], nrm).astype(BF) for m in range(4)]
        scores = [tn(qkv[m][64:128], qkv[m][0:64] * BF(0.125)) + mask for m in range(4)]
        cross = nt(nrm, w_cross[...]) + bias
        probs = []
        for m in range(4):
            qkv_ref[m * 192:(m + 1) * 192, rows] = qkv[m]
            top = jnp.max(scores[m], axis=0, keepdims=True)
            e = jnp.exp(scores[m] - top)
            total = jnp.sum(e, axis=0, keepdims=True)
            probs.append((e * (1.0 / total)).astype(BF))
            lse_ref[m:m + 1, rows] = top + jnp.log(total)
        mix = jnp.concatenate([nn(qkv[m][128:192], probs[m]).astype(BF) for m in range(4)], axis=0)
        mix_ref[:, rows] = mix
        middle = cur + tn(mix, w_out[...])
        middle_ref[rows, :] = middle
        base_ref[rows, :] = middle + cur * cross


def mlp_fwd_block(middle, gain, wm):
    r = rescale_of(middle)
    n2 = (middle * r * gain).astype(BF)
    us = [nn(n2, wm[m, 0:256, :]) for m in range(4)]
    kept = []
    for u in us:
        hid, slope = gelu_and_slope(u)
        kept.append((hid.astype(BF), slope.astype(BF)))
    feed = [nn(kept[m][0], wm[m, 256:512, :]) for m in range(4)]
    return r, n2, kept, (feed[0] + feed[1]) + (feed[2] + feed[3])


def mlp_fwd_kernel(layer, first, middle_ref, base_ref, gain_ref, p0, p1, p2, p3, p4, p5, p6, p7,
                   out_ref, hid_ref, slope_ref, wm):
    place_mlp(layer, first, (p0, p1, p2, p3, p4, p5, p6, p7), wm)
    gain = gain_ref[layer:layer + 1, :]
    for s in range(middle_ref.shape[0] // 256):
        rows = slice(s * 256, s * 256 + 256)
        _, _, kept, feed = mlp_fwd_block(middle_ref[rows, :], gain, wm)
        for m, (hid, slope) in enumerate(kept):
            hid_ref[rows, m * 256:(m + 1) * 256] = hid
            slope_ref[rows, m * 256:(m + 1) * 256] = slope
        out_ref[rows, :] = base_ref[rows, :] + feed


def mlp_bwd_block(gf, kept, wm):
    ghs = [nt(gf, wm[m, 256:512, :]) for m in range(4)]
    gps = [(gh * slope.astype(F32)).astype(BF) for gh, (_, slope) in zip(ghs, kept)]
    gn = [nt(gps[m], wm[m, 0:256, :]) for m in range(4)]
    return gps, (gn[0] + gn[1]) + (gn[2] + gn[3])


def put_mlp_grads(hid, gp, n2, gf, keep_ref, send_ref):
    for m in range(4):
        columns = slice(m * 256, (m + 1) * 256)
        up = tn(n2[...], gp[:, columns]).astype(BF)
        down = tn(hid[:, columns], gf[...]).astype(BF)
        own_up = half_index() == 0
        keep_ref[m] = jnp.where(own_up, up, down)
        send_ref[m] = jnp.where(own_up, down, up)


def mlp_both_kernel(layer, first, middle_ref, base_ref, cot_ref, gain_ref, p0, p1, p2, p3, p4, p5, p6, p7,
                    out_ref, gm_ref, keep_ref, send_ref, small_ref, wm, hid_all, gp_all, n2_all):
    place_mlp(layer, first, (p0, p1, p2, p3, p4, p5, p6, p7), wm)
    gain = gain_ref[layer:layer + 1, :]
    gain_grad = jnp.zeros((1, 256), F32)
    for s in range(middle_ref.shape[0] // 256):
        rows = slice(s * 256, s * 256 + 256)
        middle = middle_ref[rows, :]
        r, n2, kept, feed = mlp_fwd_block(middle, gain, wm)
        out_ref[rows, :] = base_ref[rows, :] + feed
        gf = cot_ref[rows, :]
        gps, gn = mlp_bwd_block(gf, kept, wm)
        n2_all[rows, :] = n2
        for m in range(4):
            hid_all[rows, m * 256:(m + 1) * 256] = kept[m][0]
            gp_all[rows, m * 256:(m + 1) * 256] = gps[m]
        back, part = norm_back(middle, r, gain, gn)
        gain_grad = gain_grad + part
        gm_ref[rows, :] = gf.astype(F32) + back
    small_ref[...] = jnp.broadcast_to(gain_grad, small_ref.shape)
    put_mlp_grads(hid_all, gp_all, n2_all, cot_ref, keep_ref, send_ref)


def mlp_bwd_kernel(layer, first, grad_ref, middle_ref, hid_ref, slope_ref, gain_ref, p0, p1, p2, p3, p4, p5, p6, p7,
                   gm_ref, keep_ref, send_ref, small_ref, wm, gp_all, n2_all, gf_all):
    place_mlp(layer, first, (p0, p1, p2, p3, p4, p5, p6, p7), wm)
    gain = gain_ref[layer:layer + 1, :]
    gain_grad = jnp.zeros((1, 256), F32)
    for s in range(middle_ref.shape[0] // 256):
        rows = slice(s * 256, s * 256 + 256)
        middle = middle_ref[rows, :]
        r = rescale_of(middle)
        n2_all[rows, :] = (middle * r * gain).astype(BF)
        grad = grad_ref[rows, :]
        gf = grad.astype(BF)
        gf_all[rows, :] = gf
        kept = [(None, slope_ref[rows, m * 256:(m + 1) * 256]) for m in range(4)]
        gps, gn = mlp_bwd_block(gf, kept, wm)
        for m in range(4):
            gp_all[rows, m * 256:(m + 1) * 256] = gps[m]
        back, part = norm_back(middle, r, gain, gn)
        gain_grad = gain_grad + part
        gm_ref[rows, :] = grad + back
    small_ref[...] = jnp.broadcast_to(gain_grad, small_ref.shape)
    put_mlp_grads(hid_ref, gp_all, n2_all, gf_all, keep_ref, send_ref)


def attn_bwd_kernel(layer, first, grad_ref, gm_ref, cur_ref, mask_ref, nrm_ref, qkv_ref, mix_ref, lse_ref, gain_ref, mlp_small,
                    p0, p1, p2, p3, p4, p5, p6,
                    out_ref, keep_ref, send_ref,
                    wa, w_cross, w_out, ga_all, gc_all, gqkv_all, payload):
    bias = place_attn(first, (p0, p1, p2, p3, p4, p5, p6), wa, w_cross, w_out)
    gain = gain_ref[layer:layer + 1, :]
    gain_grad = jnp.zeros((1, 256), F32)
    bias_grad = jnp.zeros((1, 256), F32)
    for s in range(cur_ref.shape[0] // 256):
        rows = slice(s * 256, s * 256 + 256)
        mask = jnp.concatenate([mask_ref[rows, :]] * 2, axis=1)
        grad = grad_ref[rows, :].astype(F32)
        gm = gm_ref[rows, :]
        cur = cur_ref[rows, :].astype(F32)
        nrm = nrm_ref[rows, :]
        ga = gm.astype(BF)
        ga_all[rows, :] = ga
        gc = (grad * cur).astype(BF)
        gc_all[rows, :] = gc
        bias_grad = bias_grad + jnp.sum(gc.astype(F32), axis=0, keepdims=True)
        gmix = nt(w_out[...], ga).astype(BF)
        parts = []
        for m in range(4):
            q, k, v = (qkv_ref[m * 192 + i * HD:m * 192 + (i + 1) * HD, rows] for i in range(3))
            parts.append((q, k, v, gmix[m * HD:(m + 1) * HD]))
        scores = [tn(k, q * BF(0.125)) + mask for q, k, v, go in parts]
        gps = [tn(v, go) for q, k, v, go in parts]
        gn = nn(gc, w_cross[...])
        cross = nt(nrm, w_cross[...]) + bias
        ps, gss = [], []
        for m in range(4):
            p = jnp.exp(scores[m] - lse_ref[m:m + 1, rows])
            weighted = gps[m] * p
            dot = jnp.sum(weighted, axis=0, keepdims=True)
            ps.append(p.astype(BF))
            gss.append((weighted - p * dot).astype(BF))
        for m in range(4):
            q, k, v, go = parts[m]
            gqkv = jnp.concatenate([nn(k, gss[m]) * 0.125, nt(q, gss[m]) * 0.125, nt(go, ps[m])], axis=0).astype(BF)
            gqkv_all[m * 192:(m + 1) * 192, rows] = gqkv
            gn = gn + tn(gqkv, wa[m, 0:192, :])
        back, part = norm_back(cur, rescale_of(cur), gain, gn)
        gain_grad = gain_grad + part
        out_ref[rows, :] = gm + grad * cross + back
    nrm = nrm_ref[...]
    d_cross = tn(gc_all[...], nrm).astype(BF)
    d_out = nn(mix_ref[...], ga_all[...]).astype(BF)
    w_cross[...] = d_cross
    for m in range(4):
        place = pl.multiple_of((head_index() ^ m) * HD, HD)
        payload[m, 0:192, :] = nn(gqkv_all[m * 192:(m + 1) * 192, :], nrm).astype(BF)
        payload[m, 192:256, :] = w_cross[pl.ds(place, HD), :]
        payload[m, 256:320, :] = d_out[m * HD:(m + 1) * HD]
    high, low = split_rows(jnp.concatenate([gain_grad, bias_grad, mlp_small[0:1, :], jnp.zeros((5, 256), F32)], axis=0))
    keep = pl.multiple_of(half_index() * 160, 16)
    other = pl.multiple_of((1 - half_index()) * 160, 16)
    for m in range(4):
        for ref, at in ((keep_ref, keep), (send_ref, other)):
            ref[m, 0:160, :] = payload[m, pl.ds(at, 160), :]
            ref[m, 160:168, :] = high
            ref[m, 168:176, :] = low


def split_rows(x):
    high = x.astype(BF)
    return high, (x - high.astype(F32)).astype(BF)


def pack_kernel(lens, qkv, cross, out, up, down, b, own0, own1, half_a0, half_r, half_m1, mask, sems):
    copies = []
    for l, own in ((0, own0), (1, own1)):
        for t in range(3):
            copies.append(pltpu.make_async_copy(qkv.at[l, t], own.at[pl.ds(t * HD, HD)], sems.at[0]))
        copies.append(pltpu.make_async_copy(cross.at[l], own.at[pl.ds(192, HD)], sems.at[0]))
        copies.append(pltpu.make_async_copy(out.at[l], own.at[pl.ds(256, HD)], sems.at[0]))
    for copy in copies:
        copy.start()

    def mlp_half(weight):
        return (pltpu.make_async_copy(weight.at[0], half_r.at[pl.ds(0, 256)], sems.at[1]),
                pltpu.make_async_copy(weight.at[1], half_m1, sems.at[1]))

    @pl.when(half_index() == 0)
    def _():
        for copy in mlp_half(up):
            copy.start()

    @pl.when(half_index() != 0)
    def _():
        for copy in mlp_half(down):
            copy.start()

    slots = lax.broadcasted_iota(jnp.int32, (256, 128), 0)
    samples = mask.shape[0] // 256
    for i in range(samples):
        length = lens[head_index() * samples + i]
        mask[i * 256:(i + 1) * 256, :] = jnp.where(slots < length, 0.0, MASKED_SCORE)
    lane = lax.broadcasted_iota(jnp.int32, (LAYERS, 256), 1) // HD
    wide = jnp.concatenate([b[...].astype(F32)] * 4, axis=1)
    wide = jnp.where(lane == head_index(), wide, 0.0)
    for l, own in ((0, own0), (1, own1)):
        own[320:352, :] = jnp.broadcast_to(wide[l:l + 1], (32, 256)).astype(BF)
    for copy in copies:
        copy.wait()
    at = pl.multiple_of(half_index() * 176, 16)
    half_a0[...] = own0[pl.ds(at, 176), :]
    half_r[256:432, :] = own1[pl.ds(at, 176), :]
    for copy in mlp_half(up):
        copy.wait()


def put_sum(out, at, small_at, rows, total):
    for low, high in ((0, small_at), (small_at + 16, rows)):
        if low < high:
            out[at + low:at + high, :] = total(low, high).astype(BF)
    if small_at < rows:
        both = total(small_at, small_at + 16)
        high, low = split_rows(both[0:8] + both[8:16])
        out[at + small_at:at + small_at + 8, :] = high
        out[at + small_at + 8:at + small_at + 16, :] = low


def core_sum_kernel(small_at, *refs):
    ins, outs = refs[:-4], refs[-4:]
    for m, out in enumerate(outs):
        at = 0
        for where, keep, got in zip(small_at, ins[0::2], ins[1::2]):
            rows = keep.shape[1]
            put_sum(out, at, where, rows, lambda i, j: keep[m, i:j].astype(F32) + got[m, i:j].astype(F32))
            at += rows


def four_sum_kernel(small_at, copied, *refs):
    done, refs, out = refs[:copied], refs[copied:-1], refs[-1]
    at = 0
    for ref in done:
        out[at:at + ref.shape[0], :] = ref[...]
        at += ref.shape[0]
    for i, where in enumerate(small_at):
        s, a, b, c = refs[4 * i:4 * i + 4]
        rows = s.shape[0]
        put_sum(out, at, where, rows, lambda i, j: (s[i:j].astype(F32) + a[i:j].astype(F32)) + (b[i:j].astype(F32) + c[i:j].astype(F32)))
        at += rows


def finish_kernel(early, early_other, late, late_other,
                  d_qkv, d_out, d_up, d_down, d_cross, gain_attn, gain_mlp, bias):
    def place(first, second, late_first, late_second):
        for l, a, b, at in ((1, first, second, 256), (0, late_first, late_second, 0)):
            d_qkv[l, 0] = a[at:at + 64].astype(F32)
            d_qkv[l, 1] = a[at + 64:at + 128].astype(F32)
            d_qkv[l, 2, 0:32] = a[at + 128:at + 160].astype(F32)
            d_qkv[l, 2, 32:64] = b[at:at + 32].astype(F32)
            d_cross[l] = b[at + 32:at + 96].astype(F32)
            d_out[l] = b[at + 96:at + 160].astype(F32)
        for l, at in ((1, 0), (0, 432)):
            d_up[l] = first[at:at + 256].astype(F32)
            d_down[l] = second[at:at + 256].astype(F32)

    @pl.when(half_index() == 0)
    def _():
        place(early, early_other, late, late_other)

    @pl.when(half_index() != 0)
    def _():
        place(early_other, early, late_other, late)

    for l, ref, at in ((0, late, 160), (1, early, 416)):
        rows = ref[at:at + 8].astype(F32) + ref[at + 8:at + 16].astype(F32)
        gain_attn[l:l + 1, :] = rows[0:1]
        gain_mlp[l:l + 1, :] = rows[2:3]
        total = jnp.zeros((1, HD), F32)
        for h in range(4):
            total = total + jnp.where(head_index() == h, rows[1:2, h * HD:(h + 1) * HD], 0.0)
        bias[l:l + 1, :] = total


SMEM = pl.BlockSpec(memory_space=pltpu.SMEM)
ANY = pl.BlockSpec(memory_space=pl.ANY)


def call(kernel, outs, scratch, name, *args):
    return pl.pallas_call(
        kernel,
        in_specs=[VMEM] * len(args),
        out_specs=[VMEM] * len(outs),
        out_shape=[jax.ShapeDtypeStruct(shape, dtype) for shape, dtype in outs],
        scratch_shapes=[pltpu.VMEM(shape, dtype) for shape, dtype in scratch],
        compiler_params=pltpu.CompilerParams(vmem_limit_bytes=VMEM_LIMIT),
        cost_estimate=pl.CostEstimate(flops=KERNEL_FLOPS, bytes_accessed=1024, transcendentals=0),
        name=name,
    )(*args)


ATTN_SCRATCH = [((4, 352, 256), BF), ((256, 256), BF), ((256, 256), BF)]
MLP_GRADS = [((4, 256, 256), BF), ((4, 256, 256), BF), ((8, 256), F32)]


def attn_fwd(layer, first, cur, mask, gain, pieces):
    rows = cur.shape[0]
    outs = [((rows, 256), F32), ((rows, 256), F32), ((rows, 256), BF), ((768, rows), BF), ((256, rows), BF), ((8, rows), F32)]
    return call(functools.partial(attn_fwd_kernel, layer, first), outs, ATTN_SCRATCH, "attn_fwd", cur, mask, gain, *pieces)


def mlp_fwd(layer, first, middle, base, gain, pieces):
    rows = middle.shape[0]
    outs = [((rows, 256), F32), ((rows, 1024), BF), ((rows, 1024), BF)]
    return call(functools.partial(mlp_fwd_kernel, layer, first), outs, [((4, 512, 256), BF)], "mlp_fwd",
                middle, base, gain, *pieces)


def mlp_both(layer, first, middle, base, cot, gain, pieces):
    rows = middle.shape[0]
    outs = [((rows, 256), F32), ((rows, 256), F32)] + MLP_GRADS
    scratch = [((4, 512, 256), BF), ((rows, 1024), BF), ((rows, 1024), BF), ((rows, 256), BF)]
    return call(functools.partial(mlp_both_kernel, layer, first), outs, scratch, "mlp_both", middle, base, cot, gain, *pieces)


def mlp_bwd(layer, first, grad, middle, hid, slope, gain, pieces):
    rows = middle.shape[0]
    outs = [((rows, 256), F32)] + MLP_GRADS
    scratch = [((4, 512, 256), BF), ((rows, 1024), BF), ((rows, 256), BF), ((rows, 256), BF)]
    return call(functools.partial(mlp_bwd_kernel, layer, first), outs, scratch, "mlp_bwd",
                grad, middle, hid, slope, gain, *pieces)


def attn_bwd(layer, first, grad, gm, cur, mask, saved, gain, mlp_small, pieces):
    rows = cur.shape[0]
    outs = [((rows, 256), F32), ((4, 176, 256), BF), ((4, 176, 256), BF)]
    scratch = ATTN_SCRATCH + [((rows, 256), BF), ((rows, 256), BF), ((768, rows), BF), ((4, 320, 256), BF)]
    return call(functools.partial(attn_bwd_kernel, layer, first), outs, scratch, "attn_bwd",
                grad, gm, cur, mask, *saved, gain, mlp_small, *pieces)


VMEM = pl.BlockSpec(memory_space=pltpu.VMEM)


def small_call(kernel, shapes, name):
    def run(*args):
        return pl.pallas_call(
            kernel,
            in_specs=[VMEM] * len(args),
            out_specs=[VMEM] * len(shapes),
            out_shape=[jax.ShapeDtypeStruct(shape, dtype) for shape, dtype in shapes],
            compiler_params=pltpu.CompilerParams(vmem_limit_bytes=SMALL_LIMIT),
            cost_estimate=pl.CostEstimate(flops=1000, bytes_accessed=1024, transcendentals=0),
            name=name,
        )(*args)
    return run


def core_sum(small_at, *groups):
    rows = sum(keep.shape[1] for keep, _ in groups)
    return small_call(functools.partial(core_sum_kernel, small_at), [((rows, 256), BF)] * 4, "core_sum")(
        *[x for group in groups for x in group])


def four_sum(small_at, *groups, done=()):
    rows = sum(x.shape[0] for x in done) + sum(group[0].shape[0] for group in groups)
    return small_call(functools.partial(four_sum_kernel, small_at, len(done)), [((rows, 256), BF)], "four_sum")(
        *done, *[x for group in groups for x in group])[0]


def swap(x, axis, size, mask):
    return lax.ppermute(x, axis, [(i, i ^ mask) for i in range(size)])


def tie(x, *before):
    return lax.optimization_barrier((x,) + before)[0]


def solution(mesh):
    dp_size, head_size = mesh.shape["dp"], mesh.shape["head"]

    def core_swap(x):
        return swap(x, "dp", dp_size, 1)

    def fetch(x):
        return [swap(x, "head", head_size, m) for m in range(1, head_size)]

    def scatter(sums):
        return [sums[0]] + [swap(sums[m], "head", head_size, m) for m in range(1, head_size)]

    def spread(x, bit):
        return [x] + [swap(x, "dp", dp_size, m * bit) for m in (1, 2, 3)]

    def sum_rest(x, small_at, before=()):
        bit = 2
        while bit < dp_size:
            if bit * 2 < dp_size:
                x = four_sum((small_at,), [tie(term, *before) for term in spread(x, bit)])
            else:
                x = four_sum((small_at,), [x, swap(x, "dp", dp_size, bit), jnp.zeros_like(x), jnp.zeros_like(x)])
            bit *= 4
        return x

    def body(tokens, lengths, cotangent, gain_attn, gain_mlp, w_qkv, w_out, w_up, w_down, w_cross, b_cross):
        rows = tokens.shape[0]
        own0, own1, half_a0, half_r, half_m1, mask = pl.pallas_call(
            pack_kernel,
            in_specs=[SMEM] + [ANY] * 5 + [VMEM],
            out_specs=[VMEM] * 6,
            out_shape=[jax.ShapeDtypeStruct((n, 256), BF) for n in (352, 352, 176, 432, 256)]
            + [jax.ShapeDtypeStruct((rows, 128), F32)],
            scratch_shapes=[pltpu.SemaphoreType.DMA((2,))],
            name="pack",
        )(lengths, w_qkv.transpose(0, 2, 3, 1), w_cross.transpose(0, 2, 1), w_out, w_up, w_down, b_cross)

        a0 = fetch(half_a0)
        r = fetch(half_r)
        m1 = fetch(half_m1)
        pieces_a0 = [own0] + a0 + [core_swap(x) for x in a0]
        mid0, base0, *saved0 = attn_fwd(0, 0, tokens, mask, gain_attn, pieces_a0)
        r = [tie(x, mid0) for x in r]
        r = r + [core_swap(x) for x in r]
        cur1, hid0, slope0 = mlp_fwd(0, 0, mid0, base0, gain_mlp, [w_up, w_down] + r)
        mid1, base1, *saved1 = attn_fwd(1, 256, cur1, mask, gain_attn, [own1] + r)
        m1 = [tie(x, mid1) for x in m1]
        m1 = m1 + [core_swap(x) for x in m1]
        output, gm1, keep_m1, send_m1, small_m1 = mlp_both(1, 0, mid1, base1, cotangent, gain_mlp, [w_up, w_down] + m1)
        sums_m1 = core_sum((256,), (keep_m1, core_swap(send_m1)))
        got_m1 = scatter(sums_m1)
        grad1, keep_a1, send_a1 = attn_bwd(
            1, 256, cotangent, tie(gm1, *sums_m1), cur1, mask, saved1, gain_attn, small_m1, [own1] + r)
        early = four_sum((256,), [tie(x, grad1) for x in got_m1])
        got_a1 = core_swap(send_a1)
        gm0, keep_m0, send_m0, small_m0 = mlp_bwd(0, 0, tie(grad1, early), mid0, hid0, slope0, gain_mlp, [w_up, w_down] + r)
        sums = core_sum((160, 256), (keep_a1, tie(got_a1, gm0)), (keep_m0, core_swap(send_m0)))
        got = scatter(sums)
        grad0, keep_a0, send_a0 = attn_bwd(
            0, 0, grad1, tie(gm0, *sums), tokens, mask, saved0, gain_attn, small_m0, pieces_a0)
        early = four_sum((160,), [tie(x, grad0) for x in got], done=(early,))
        sums_a0 = core_sum((160,), (keep_a0, core_swap(tie(send_a0, early))))
        late = scatter(sums_a0)
        early = sum_rest(early, 416, late[1:])
        late = four_sum((160,), late)
        late = sum_rest(late, 160)
        d_qkv, d_out, d_up, d_down, d_cross, d_ga, d_gm, d_bias = small_call(
            finish_kernel,
            [((LAYERS, 3, HD, 256), F32), ((LAYERS, HD, 256), F32), ((LAYERS, 256, 256), F32), ((LAYERS, 256, 256), F32),
             ((LAYERS, HD, 256), F32), ((LAYERS, 256), F32), ((LAYERS, 256), F32), ((LAYERS, HD), F32)],
            "finish",
        )(early, core_swap(early), late, core_swap(late))
        return (output, grad0, d_ga, d_gm, d_qkv.transpose(0, 3, 1, 2), d_out, d_up, d_down,
                d_cross.transpose(0, 2, 1), d_bias)

    rows, weights = P(("dp", "head"), None), P(None, "head", None)
    return jax.shard_map(
        body,
        mesh=mesh,
        in_specs=(rows, P("dp"), rows, P(), P(), P(None, None, None, "head"), weights, P(None, None, "head"),
                  weights, P(None, None, "head"), P(None, "head")),
        out_specs=(rows, rows, P(), P(), P(None, None, None, "head"), weights, P(None, None, "head"),
                   weights, P(None, None, "head"), P(None, "head")),
        check_vma=False,
    )
```

```python
import functools

import jax
import jax.numpy as jnp
from jax import lax
from jax.experimental import pallas as pl
from jax.experimental.pallas import tpu as pltpu
from jax.sharding import PartitionSpec as P

HD = 64
LAYERS = 2
EPSILON = 1e-06
MASKED_SCORE = -1000000000.0
BF = jnp.bfloat16
F32 = jnp.float32

VMEM_LIMIT = 32 * 2**20
SMALL_LIMIT = 12 * 2**20
CUT = 96
UNROLL = {"attn_fwd": 4, "mlp_fwd": 4, "mlp_both": 4, "mlp_bwd": 4, "attn_bwd": 2, "attn_pre": 2, "attn_post": 2}
KERNEL_FLOPS = 1000
LONG = 50 * 10**9


def nn(a, b):
    return lax.dot_general(a, b, (((1,), (0,)), ((), ())), preferred_element_type=F32)


def nt(a, b):
    return lax.dot_general(a, b, (((1,), (1,)), ((), ())), preferred_element_type=F32)


def tn(a, b):
    return lax.dot_general(a, b, (((0,), (0,)), ((), ())), preferred_element_type=F32)


def rescale_of(values):
    return lax.rsqrt(jnp.mean(values * values, axis=-1, keepdims=True) + EPSILON)


def norm_back(values, rescale, gain, gradient):
    scaled = gradient * gain
    product_mean = jnp.mean(values * scaled, axis=-1, keepdims=True)
    normal = values * rescale
    grad_values = rescale * (scaled - normal * (rescale * product_mean))
    return grad_values, jnp.sum(gradient * normal, axis=0, keepdims=True)


def gelu_and_slope(u):
    d = 1.0 + (0.3275911 * 0.7071067811865476) * jnp.abs(u)
    t = pl.reciprocal(d, approx=True)
    t = t * (2.0 - d * t)
    e = jnp.exp2((-0.5 * 1.4426950408889634) * (u * u))
    poly = ((((0.5 * 1.061405429) * t - 0.5 * 1.453152027) * t + 0.5 * 1.421413741) * t - 0.5 * 0.284496736) * t + 0.5 * 0.254829592
    tail = poly * t * e
    cdf = jnp.where(u >= 0.0, 1.0 - tail, tail)
    return u * cdf, cdf + u * (e * 0.3989422804014327)


def head_index():
    return lax.axis_index("head")


def half_index():
    return lax.axis_index("dp") & 1


def quarter_index():
    return (lax.axis_index("dp") >> 1) & 1


def place_pieces(own, mine, theirs, dst, first=0):
    half = dst.shape[1] // 2
    keep = pl.multiple_of(half_index() * half, 16)
    other = pl.multiple_of((1 - half_index()) * half, 16)
    at = 0
    for part in own:
        dst[0, at:at + part.shape[0], :] = part
        at += part.shape[0]
    for m in range(3):
        dst[m + 1, pl.ds(keep, half), :] = mine[m][first:first + half, :]
        dst[m + 1, pl.ds(other, half), :] = theirs[m][first:first + half, :]


def place_attn(first, pieces, wa, w_cross, w_out):
    place_pieces((pieces[0][...],), pieces[1:4], pieces[4:7], wa, first)
    total = jnp.zeros((1, 256), F32)
    for m in range(4):
        place = pl.multiple_of((head_index() ^ m) * HD, HD)
        w_cross[pl.ds(place, HD), :] = wa[m, 192:256, :]
        w_out[m * HD:(m + 1) * HD, :] = wa[m, 256:320, :]
        total = total + wa[m, 320:336, :].astype(F32)[0:1, :]
    return total


def place_mlp(layer, first, pieces, wm):
    place_pieces((pieces[0][layer], pieces[1][layer]), pieces[2:5], pieces[5:8], wm, first)


def each_sample(rows, unroll, step, *init):
    def body(i, carried):
        return step(pl.ds(pl.multiple_of(i * 256, 256), 256), *carried)

    return lax.fori_loop(0, rows // 256, body, init, unroll=unroll)


def attn_fwd_kernel(layer, first, cur_ref, mask_ref, gain_ref, p0, p1, p2, p3, p4, p5, p6,
                    middle_ref, base_ref, nrm_ref, qkv_ref, mix_ref, lse_ref, wa, w_cross, w_out):
    bias = place_attn(first, (p0, p1, p2, p3, p4, p5, p6), wa, w_cross, w_out)
    gain = gain_ref[layer:layer + 1, :]
    def step(rows):
        cur = cur_ref[rows, :].astype(F32)
        nrm = (cur * rescale_of(cur) * gain).astype(BF)
        nrm_ref[rows, :] = nrm
        mask = jnp.concatenate([mask_ref[rows, :]] * 2, axis=1)
        qkv = [nt(wa[m, 0:192, :], nrm).astype(BF) for m in range(4)]
        scores = [tn(qkv[m][64:128], qkv[m][0:64] * BF(0.125)) + mask for m in range(4)]
        cross = nt(nrm, w_cross[...]) + bias
        probs = []
        for m in range(4):
            qkv_ref[m * 192:(m + 1) * 192, rows] = qkv[m]
            top = jnp.max(scores[m], axis=0, keepdims=True)
            e = jnp.exp(scores[m] - top)
            total = jnp.sum(e, axis=0, keepdims=True)
            probs.append((e * (1.0 / total)).astype(BF))
            lse_ref[m:m + 1, rows] = top + jnp.log(total)
        mix = jnp.concatenate([nn(qkv[m][128:192], probs[m]).astype(BF) for m in range(4)], axis=0)
        mix_ref[:, rows] = mix
        middle = cur + tn(mix, w_out[...])
        middle_ref[rows, :] = middle
        base_ref[rows, :] = middle + cur * cross
        return ()

    each_sample(cur_ref.shape[0], UNROLL["attn_fwd"], step)


def mlp_fwd_block(middle, gain, wm):
    r = rescale_of(middle)
    n2 = (middle * r * gain).astype(BF)
    us = [nn(n2, wm[m, 0:256, :]) for m in range(4)]
    kept = []
    for u in us:
        hid, slope = gelu_and_slope(u)
        kept.append((hid.astype(BF), slope.astype(BF)))
    feed = [nn(kept[m][0], wm[m, 256:512, :]) for m in range(4)]
    return r, n2, kept, (feed[0] + feed[1]) + (feed[2] + feed[3])


def mlp_fwd_kernel(layer, first, middle_ref, base_ref, gain_ref, p0, p1, p2, p3, p4, p5, p6, p7,
                   out_ref, hid_ref, slope_ref, wm):
    place_mlp(layer, first, (p0, p1, p2, p3, p4, p5, p6, p7), wm)
    gain = gain_ref[layer:layer + 1, :]
    def step(rows):
        _, _, kept, feed = mlp_fwd_block(middle_ref[rows, :], gain, wm)
        for m, (hid, slope) in enumerate(kept):
            hid_ref[rows, m * 256:(m + 1) * 256] = hid
            slope_ref[rows, m * 256:(m + 1) * 256] = slope
        out_ref[rows, :] = base_ref[rows, :] + feed
        return ()

    each_sample(middle_ref.shape[0], UNROLL["mlp_fwd"], step)


def mlp_bwd_block(gf, kept, wm):
    ghs = [nt(gf, wm[m, 256:512, :]) for m in range(4)]
    gps = [(gh * slope.astype(F32)).astype(BF) for gh, (_, slope) in zip(ghs, kept)]
    gn = [nt(gps[m], wm[m, 0:256, :]) for m in range(4)]
    return gps, (gn[0] + gn[1]) + (gn[2] + gn[3])


def put_mlp_grads(hid, gp, n2, gf, keep_ref, send_ref):
    for m in range(4):
        columns = slice(m * 256, (m + 1) * 256)
        up = tn(n2[...], gp[:, columns]).astype(BF)
        down = tn(hid[:, columns], gf[...]).astype(BF)
        own_up = half_index() == 0
        keep_ref[m] = jnp.where(own_up, up, down)
        send_ref[m] = jnp.where(own_up, down, up)


def mlp_both_kernel(layer, first, middle_ref, base_ref, cot_ref, gain_ref, p0, p1, p2, p3, p4, p5, p6, p7,
                    out_ref, gm_ref, keep_ref, send_ref, small_ref, wm, hid_all, gp_all, n2_all):
    place_mlp(layer, first, (p0, p1, p2, p3, p4, p5, p6, p7), wm)
    gain = gain_ref[layer:layer + 1, :]
    def step(rows, gain_grad):
        middle = middle_ref[rows, :]
        r, n2, kept, feed = mlp_fwd_block(middle, gain, wm)
        out_ref[rows, :] = base_ref[rows, :] + feed
        gf = cot_ref[rows, :]
        gps, gn = mlp_bwd_block(gf, kept, wm)
        n2_all[rows, :] = n2
        for m in range(4):
            hid_all[rows, m * 256:(m + 1) * 256] = kept[m][0]
            gp_all[rows, m * 256:(m + 1) * 256] = gps[m]
        back, part = norm_back(middle, r, gain, gn)
        gain_grad = gain_grad + part
        gm_ref[rows, :] = gf.astype(F32) + back
        return (gain_grad, )

    gain_grad, = each_sample(middle_ref.shape[0], UNROLL["mlp_both"], step, jnp.zeros((1, 256), F32))
    small_ref[...] = jnp.broadcast_to(gain_grad, small_ref.shape)
    put_mlp_grads(hid_all, gp_all, n2_all, cot_ref, keep_ref, send_ref)


def mlp_bwd_kernel(layer, first, grad_ref, middle_ref, hid_ref, slope_ref, gain_ref, p0, p1, p2, p3, p4, p5, p6, p7,
                   gm_ref, keep_ref, send_ref, small_ref, wm, gp_all, n2_all, gf_all):
    place_mlp(layer, first, (p0, p1, p2, p3, p4, p5, p6, p7), wm)
    gain = gain_ref[layer:layer + 1, :]
    def step(rows, gain_grad):
        middle = middle_ref[rows, :]
        r = rescale_of(middle)
        n2_all[rows, :] = (middle * r * gain).astype(BF)
        grad = grad_ref[rows, :]
        gf = grad.astype(BF)
        gf_all[rows, :] = gf
        kept = [(None, slope_ref[rows, m * 256:(m + 1) * 256]) for m in range(4)]
        gps, gn = mlp_bwd_block(gf, kept, wm)
        for m in range(4):
            gp_all[rows, m * 256:(m + 1) * 256] = gps[m]
        back, part = norm_back(middle, r, gain, gn)
        gain_grad = gain_grad + part
        gm_ref[rows, :] = grad + back
        return (gain_grad, )

    gain_grad, = each_sample(middle_ref.shape[0], UNROLL["mlp_bwd"], step, jnp.zeros((1, 256), F32))
    small_ref[...] = jnp.broadcast_to(gain_grad, small_ref.shape)
    put_mlp_grads(hid_ref, gp_all, n2_all, gf_all, keep_ref, send_ref)


def attn_pre_kernel(layer, first, grad_ref, gm_ref, cur_ref, nrm_ref, mix_ref, p0, p1, p2, p3, p4, p5, p6,
                    gmix_ref, d_cross_ref, d_out_ref, base_ref, gn_ref, small_ref,
                    wa, w_cross, w_out, ga_all, gc_all):
    bias = place_attn(first, (p0, p1, p2, p3, p4, p5, p6), wa, w_cross, w_out)

    def step(rows, bias_grad):
        grad = grad_ref[rows, :].astype(F32)
        gm = gm_ref[rows, :]
        ga = gm.astype(BF)
        ga_all[rows, :] = ga
        gc = (grad * cur_ref[rows, :].astype(F32)).astype(BF)
        gc_all[rows, :] = gc
        gmix_ref[:, rows] = nt(w_out[...], ga).astype(BF)
        gn_ref[rows, :] = nn(gc, w_cross[...])
        base_ref[rows, :] = gm + grad * (nt(nrm_ref[rows, :], w_cross[...]) + bias)
        return (bias_grad + jnp.sum(gc.astype(F32), axis=0, keepdims=True), )

    bias_grad, = each_sample(cur_ref.shape[0], UNROLL["attn_pre"], step, jnp.zeros((1, 256), F32))
    d_cross = tn(gc_all[...], nrm_ref[...])
    d_cross_ref[...] = d_cross.astype(BF)
    d_out_ref[...] = nn(mix_ref[...], ga_all[...]).astype(BF)
    small_ref[0:1, :] = bias_grad
    small_ref[1:2, :] = jnp.sum(d_cross * w_cross[...].astype(F32), axis=0, keepdims=True)


def qkv_back(rows, mask_ref, qkv_ref, lse_ref, gmix_ref):
    mask = jnp.concatenate([mask_ref[rows, :]] * 2, axis=1)
    parts = []
    for m in range(4):
        q, k, v = (qkv_ref[m * 192 + i * HD:m * 192 + (i + 1) * HD, rows] for i in range(3))
        parts.append((q, k, v, gmix_ref[m * HD:(m + 1) * HD, rows]))
    scores = [tn(k, q * BF(0.125)) + mask for q, k, v, go in parts]
    gps = [tn(v, go) for q, k, v, go in parts]
    ps, gss = [], []
    for m in range(4):
        p = jnp.exp(scores[m] - lse_ref[m:m + 1, rows])
        weighted = gps[m] * p
        dot = jnp.sum(weighted, axis=0, keepdims=True)
        ps.append(p.astype(BF))
        gss.append((weighted - p * dot).astype(BF))
    return [
        jnp.concatenate([nn(k, gs) * 0.125, nt(q, gs) * 0.125, nt(go, p)], axis=0).astype(BF)
        for (q, k, v, go), p, gs in zip(parts, ps, gss)
    ]


def norm_grad(cur, gain, gn):
    r = rescale_of(cur)
    scaled = gn * gain
    return r * (scaled - cur * (r * r * jnp.mean(cur * scaled, axis=-1, keepdims=True)))


def place_qkv(first, pieces, wa):
    place_pieces((pieces[0][...],), pieces[1:4], pieces[4:7], wa, first)


def put_attn_grads(layer, nrm, gqkv_all, wa, gain_ref, d_cross_ref, d_out_ref, small, mlp_small, payload, keep_ref, sends):
    gain_grad = small[1:2, :]
    for m in range(4):
        place = pl.multiple_of((head_index() ^ m) * HD, HD)
        d_qkv = nn(gqkv_all[m * 192:(m + 1) * 192, :], nrm)
        gain_grad = gain_grad + jnp.sum(d_qkv * wa[m, 0:192, :].astype(F32), axis=0, keepdims=True)
        payload[m, 0:192, :] = d_qkv.astype(BF)
        payload[m, 192:256, :] = d_cross_ref[pl.ds(place, HD), :]
        payload[m, 256:320, :] = d_out_ref[m * HD:(m + 1) * HD, :]
    gain_grad = gain_grad / gain_ref[layer:layer + 1, :]
    high, low = split_rows(jnp.concatenate([gain_grad, small[0:1, :], mlp_small[0:1, :], jnp.zeros((5, 256), F32)], axis=0))
    keep = pl.multiple_of(half_index() * 160, 16)
    other = pl.multiple_of((1 - half_index()) * 160, 16)
    for m in range(4):
        each = 4 // len(sends)
        for ref, i, at in ((keep_ref, m, keep), (sends[m // each], m % each, other)):
            ref[i, 0:160, :] = payload[m, pl.ds(at, 160), :]
            ref[i, 160:168, :] = high
            ref[i, 168:176, :] = low


def attn_bwd_kernel(layer, first, mask_ref, nrm_ref, qkv_ref, lse_ref, gain_ref, gmix_ref, d_cross_ref, d_out_ref, small, mlp_small,
                    cur_ref, base_ref, gn_ref, p0, p1, p2, p3, p4, p5, p6,
                    out_ref, keep_ref, send_ref, wa, gqkv_all, payload):
    place_qkv(first, (p0, p1, p2, p3, p4, p5, p6), wa)

    def step(rows):
        gn = gn_ref[rows, :]
        for m, gqkv in enumerate(qkv_back(rows, mask_ref, qkv_ref, lse_ref, gmix_ref)):
            gqkv_all[m * 192:(m + 1) * 192, rows] = gqkv
            gn = gn + tn(gqkv, wa[m, 0:192, :])
        out_ref[rows, :] = base_ref[rows, :] + norm_grad(cur_ref[rows, :].astype(F32), gain_ref[layer:layer + 1, :], gn)
        return ()

    each_sample(nrm_ref.shape[0], UNROLL["attn_bwd"], step)
    put_attn_grads(layer, nrm_ref[...], gqkv_all, wa, gain_ref, d_cross_ref, d_out_ref, small, mlp_small,
                   payload, keep_ref, (send_ref,))


def attn_grads_kernel(layer, first, mask_ref, nrm_ref, qkv_ref, lse_ref, gain_ref, gmix_ref, d_cross_ref, d_out_ref, small, mlp_small,
                      p0, p1, p2, p3, p4, p5, p6, gqkv_all, keep_ref, send_low, send_high, wa, payload):
    place_qkv(first, (p0, p1, p2, p3, p4, p5, p6), wa)

    def step(rows):
        for m, gqkv in enumerate(qkv_back(rows, mask_ref, qkv_ref, lse_ref, gmix_ref)):
            gqkv_all[m * 192:(m + 1) * 192, rows] = gqkv
        return ()

    each_sample(nrm_ref.shape[0], UNROLL["attn_bwd"], step)
    put_attn_grads(layer, nrm_ref[...], gqkv_all, wa, gain_ref, d_cross_ref, d_out_ref, small, mlp_small,
                   payload, keep_ref, (send_low, send_high))


def attn_post_kernel(layer, first, gqkv_all, gain_ref, cur_ref, base_ref, gn_ref, p0, p1, p2, p3, p4, p5, p6, out_ref, wa):
    place_qkv(first, (p0, p1, p2, p3, p4, p5, p6), wa)

    def step(rows):
        gn = gn_ref[rows, :]
        for m in range(4):
            gn = gn + tn(gqkv_all[m * 192:(m + 1) * 192, rows], wa[m, 0:192, :])
        out_ref[rows, :] = base_ref[rows, :] + norm_grad(cur_ref[rows, :].astype(F32), gain_ref[layer:layer + 1, :], gn)
        return ()

    each_sample(cur_ref.shape[0], UNROLL["attn_post"], step)


def split_rows(x):
    high = x.astype(BF)
    return high, (x - high.astype(F32)).astype(BF)


def pack_kernel(lens, qkv, cross, out, up, down, b, own0, own1, half_a0, half_r, half_m1, mask, sems):
    copies = []
    for l, own in ((0, own0), (1, own1)):
        for t in range(3):
            copies.append(pltpu.make_async_copy(qkv.at[l, t], own.at[pl.ds(t * HD, HD)], sems.at[0]))
        copies.append(pltpu.make_async_copy(cross.at[l], own.at[pl.ds(192, HD)], sems.at[0]))
        copies.append(pltpu.make_async_copy(out.at[l], own.at[pl.ds(256, HD)], sems.at[0]))
    for copy in copies:
        copy.start()

    def mlp_half(weight):
        return (pltpu.make_async_copy(weight.at[0], half_r.at[pl.ds(0, 256)], sems.at[1]),
                pltpu.make_async_copy(weight.at[1], half_m1, sems.at[1]))

    @pl.when(half_index() == 0)
    def _():
        for copy in mlp_half(up):
            copy.start()

    @pl.when(half_index() != 0)
    def _():
        for copy in mlp_half(down):
            copy.start()

    slots = lax.broadcasted_iota(jnp.int32, (256, 128), 0)
    samples = mask.shape[0] // 256
    for i in range(samples):
        length = lens[head_index() * samples + i]
        mask[i * 256:(i + 1) * 256, :] = jnp.where(slots < length, 0.0, MASKED_SCORE)
    lane = lax.broadcasted_iota(jnp.int32, (LAYERS, 256), 1) // HD
    wide = jnp.concatenate([b[...].astype(F32)] * 4, axis=1)
    wide = jnp.where(lane == head_index(), wide, 0.0)
    for l, own in ((0, own0), (1, own1)):
        own[320:352, :] = jnp.broadcast_to(wide[l:l + 1], (32, 256)).astype(BF)
    for copy in copies:
        copy.wait()
    at = pl.multiple_of(half_index() * 176, 16)
    half_a0[...] = own0[pl.ds(at, 176), :]
    half_r[256:432, :] = own1[pl.ds(at, 176), :]
    for copy in mlp_half(up):
        copy.wait()


def put_sum(out, at, small_at, rows, total):
    for low, high in ((0, small_at), (small_at + 16, rows)):
        if low < high:
            out[at + low:at + high, :] = total(low, high).astype(BF)
    if small_at < rows:
        both = total(small_at, small_at + 16)
        high, low = split_rows(both[0:8] + both[8:16])
        out[at + small_at:at + small_at + 8, :] = high
        out[at + small_at + 8:at + small_at + 16, :] = low


def core_sum_kernel(small_at, *refs):
    ins, outs = refs[:-4], refs[-4:]
    for m, out in enumerate(outs):
        at = 0
        rest = list(ins)
        for where in small_at:
            keep = rest.pop(0)
            if where is None:
                out[at:at + keep.shape[1], :] = keep[m]
                at += keep.shape[1]
                continue
            got, index = rest.pop(0), m
            if got.shape[0] < keep.shape[0]:
                got, index = (got, rest.pop(0))[m // 2], m % 2
            rows = keep.shape[1]
            put_sum(out, at, where, rows, lambda i, j: keep[m, i:j].astype(F32) + got[index, i:j].astype(F32))
            at += rows


def core_split_kernel(keep, got, keep_out, send_out):
    at = pl.multiple_of(quarter_index() * 128, 16)
    other = pl.multiple_of((1 - quarter_index()) * 128, 16)
    for out, rows in ((keep_out, pl.ds(at, 128)), (send_out, pl.ds(other, 128))):
        for m in range(4):
            out[m] = (keep[m, rows, :].astype(F32) + got[m, rows, :].astype(F32)).astype(BF)


def add_kernel(a, b, out):
    out[...] = (a[...].astype(F32) + b[...].astype(F32)).astype(BF)


def four_sum_kernel(small_at, *refs):
    s, a, b, c, out = refs
    put_sum(out, 0, small_at, s.shape[0],
            lambda i, j: (s[i:j].astype(F32) + a[i:j].astype(F32)) + (b[i:j].astype(F32) + c[i:j].astype(F32)))


def early_sum_kernel(one, s, a, b, c, low, high):
    total = (s[...].astype(F32) + a[...].astype(F32)) + (b[...].astype(F32) + c[...].astype(F32))
    low[0:176, :] = one[128:304, :]
    low[176:176 + CUT, :] = total[0:CUT].astype(BF)
    high[0:256 - CUT, :] = total[CUT:256].astype(BF)
    high[256 - CUT:384 - CUT, :] = one[0:128, :]


def pair_sum_kernel(low, low_got, high, high_got, low_out, high_out):
    put_sum(low_out, 0, 160, low.shape[0], lambda i, j: low[i:j].astype(F32) + low_got[i:j].astype(F32))
    high_out[...] = (high[...].astype(F32) + high_got[...].astype(F32)).astype(BF)


def last_pair_kernel(low, low_got, high, high_got, low_out, high_out):
    put_sum(low_out, 0, 160, low.shape[0], lambda i, j: low[i:j].astype(F32) + low_got[i:j].astype(F32))
    rows = 256 - CUT
    high_out[0:rows, :] = (high[0:rows].astype(F32) + high_got[0:rows].astype(F32)).astype(BF)
    high_out[rows:rows + 128, :] = high[rows:rows + 128]
    high_out[rows + 128:rows + 256, :] = high_got[rows:rows + 128]


def finish_kernel(low, low_other, high, high_other, late, late_other,
                  d_qkv, d_out, d_up, d_down, d_cross, gain_attn, gain_mlp, bias):
    rows = 256 - CUT
    mine = pl.multiple_of(quarter_index() * 128, 16)
    other = pl.multiple_of((1 - quarter_index()) * 128, 16)

    def place(first, second):
        for l, a, b in ((1, first[0], second[0]), (0, first[2], second[2])):
            d_qkv[l, 0] = a[0:64].astype(F32)
            d_qkv[l, 1] = a[64:128].astype(F32)
            d_qkv[l, 2, 0:32] = a[128:160].astype(F32)
            d_qkv[l, 2, 32:64] = b[0:32].astype(F32)
            d_cross[l] = b[32:96].astype(F32)
            d_out[l] = b[96:160].astype(F32)
        for dst, (lo, hi, _) in ((d_up, first), (d_down, second)):
            dst[0, 0:CUT] = lo[176:176 + CUT].astype(F32)
            dst[0, CUT:256] = hi[0:rows].astype(F32)
            dst[1, pl.ds(mine, 128)] = hi[rows:rows + 128].astype(F32)
            dst[1, pl.ds(other, 128)] = hi[rows + 128:rows + 256].astype(F32)

    @pl.when(half_index() == 0)
    def _():
        place((low, high, late), (low_other, high_other, late_other))

    @pl.when(half_index() != 0)
    def _():
        place((low_other, high_other, late_other), (low, high, late))

    for l, ref in ((0, late), (1, low)):
        small = ref[160:168].astype(F32) + ref[168:176].astype(F32)
        gain_attn[l:l + 1, :] = small[0:1]
        gain_mlp[l:l + 1, :] = small[2:3]
        total = jnp.zeros((1, HD), F32)
        for h in range(4):
            total = total + jnp.where(head_index() == h, small[1:2, h * HD:(h + 1) * HD], 0.0)
        bias[l:l + 1, :] = total


SMEM = pl.BlockSpec(memory_space=pltpu.SMEM)
ANY = pl.BlockSpec(memory_space=pl.ANY)


def call(kernel, outs, scratch, name, *args):
    return pl.pallas_call(
        kernel,
        in_specs=[VMEM] * len(args),
        out_specs=[VMEM] * len(outs),
        out_shape=[jax.ShapeDtypeStruct(shape, dtype) for shape, dtype in outs],
        scratch_shapes=[pltpu.VMEM(shape, dtype) for shape, dtype in scratch],
        compiler_params=pltpu.CompilerParams(vmem_limit_bytes=VMEM_LIMIT),
        cost_estimate=pl.CostEstimate(flops=KERNEL_FLOPS, bytes_accessed=1024, transcendentals=0),
        name=name,
    )(*args)


ATTN_SCRATCH = [((4, 352, 256), BF), ((256, 256), BF), ((256, 256), BF)]
MLP_GRADS = [((4, 256, 256), BF), ((4, 256, 256), BF), ((8, 256), F32)]


def attn_fwd(layer, first, cur, mask, gain, pieces):
    rows = cur.shape[0]
    outs = [((rows, 256), F32), ((rows, 256), F32), ((rows, 256), BF), ((768, rows), BF), ((256, rows), BF), ((8, rows), F32)]
    return call(functools.partial(attn_fwd_kernel, layer, first), outs, ATTN_SCRATCH, "attn_fwd", cur, mask, gain, *pieces)


def mlp_fwd(layer, first, middle, base, gain, pieces):
    rows = middle.shape[0]
    outs = [((rows, 256), F32), ((rows, 1024), BF), ((rows, 1024), BF)]
    return call(functools.partial(mlp_fwd_kernel, layer, first), outs, [((4, 512, 256), BF)], "mlp_fwd",
                middle, base, gain, *pieces)


def mlp_both(layer, first, middle, base, cot, gain, pieces):
    rows = middle.shape[0]
    outs = [((rows, 256), F32), ((rows, 256), F32)] + MLP_GRADS
    scratch = [((4, 512, 256), BF), ((rows, 1024), BF), ((rows, 1024), BF), ((rows, 256), BF)]
    return call(functools.partial(mlp_both_kernel, layer, first), outs, scratch, "mlp_both", middle, base, cot, gain, *pieces)


def mlp_bwd(layer, first, grad, middle, hid, slope, gain, pieces):
    rows = middle.shape[0]
    outs = [((rows, 256), F32)] + MLP_GRADS
    scratch = [((4, 512, 256), BF), ((rows, 1024), BF), ((rows, 256), BF), ((rows, 256), BF)]
    return call(functools.partial(mlp_bwd_kernel, layer, first), outs, scratch, "mlp_bwd",
                grad, middle, hid, slope, gain, *pieces)


def attn_pre(layer, first, grad, gm, cur, saved, pieces):
    rows = cur.shape[0]
    nrm, _, mix, _ = saved
    outs = [((256, rows), BF), ((256, 256), BF), ((256, 256), BF), ((rows, 256), F32), ((rows, 256), F32), ((8, 256), F32)]
    scratch = ATTN_SCRATCH + [((rows, 256), BF), ((rows, 256), BF)]
    return call(functools.partial(attn_pre_kernel, layer, first), outs, scratch, "attn_pre", grad, gm, cur, nrm, mix, *pieces)


PAYLOAD = [((4, 176, 256), BF), ((4, 176, 256), BF)]


def attn_bwd(layer, first, cur, mask, saved, gain, pre, mlp_small, pieces):
    rows = cur.shape[0]
    nrm, qkv, _, lse = saved
    gmix, d_cross, d_out, base, gn, small = pre
    scratch = [((4, 352, 256), BF), ((768, rows), BF), ((4, 320, 256), BF)]
    return call(functools.partial(attn_bwd_kernel, layer, first), [((rows, 256), F32)] + PAYLOAD, scratch, "attn_bwd",
                mask, nrm, qkv, lse, gain, gmix, d_cross, d_out, small, mlp_small, cur, base, gn, *pieces)


def attn_grads(layer, first, mask, saved, gain, pre, mlp_small, pieces):
    nrm, qkv, _, lse = saved
    gmix, d_cross, d_out, _, _, small = pre
    scratch = [((4, 352, 256), BF), ((4, 320, 256), BF)]
    return call(functools.partial(attn_grads_kernel, layer, first), [((768, nrm.shape[0]), BF), ((4, 176, 256), BF), ((2, 176, 256), BF), ((2, 176, 256), BF)], scratch, "attn_grads",
                mask, nrm, qkv, lse, gain, gmix, d_cross, d_out, small, mlp_small, *pieces)


def attn_post(layer, first, gqkv, gain, cur, pre, pieces):
    return call(functools.partial(attn_post_kernel, layer, first), [((cur.shape[0], 256), F32)], [((4, 352, 256), BF)], "attn_post",
                gqkv, gain, cur, pre[3], pre[4], *pieces)[0]


VMEM = pl.BlockSpec(memory_space=pltpu.VMEM)


def small_call(kernel, shapes, name, flops=1000):
    def run(*args):
        return pl.pallas_call(
            kernel,
            in_specs=[VMEM] * len(args),
            out_specs=[VMEM] * len(shapes),
            out_shape=[jax.ShapeDtypeStruct(shape, dtype) for shape, dtype in shapes],
            compiler_params=pltpu.CompilerParams(vmem_limit_bytes=SMALL_LIMIT),
            cost_estimate=pl.CostEstimate(flops=flops, bytes_accessed=1024, transcendentals=0),
            name=name,
        )(*args)
    return run


def core_sum(small_at, *groups):
    rows = sum(group[0].shape[1] for group in groups)
    return small_call(functools.partial(core_sum_kernel, small_at), [((rows, 256), BF)] * 4, "core_sum")(
        *[x for group in groups for x in group])


def four_sum(small_at, terms, flops=1000):
    return small_call(functools.partial(four_sum_kernel, small_at), [(terms[0].shape, BF)], "four_sum", flops)(*terms)[0]


def swap(x, axis, size, mask):
    return lax.ppermute(x, axis, [(i, i ^ mask) for i in range(size)])


def tie(x, *before):
    return lax.optimization_barrier((x,) + before)[0]


def solution(mesh):
    dp_size, head_size = mesh.shape["dp"], mesh.shape["head"]

    def core_swap(x):
        return swap(x, "dp", dp_size, 1)

    def fetch(x):
        return [swap(x, "head", head_size, m) for m in range(1, head_size)]

    def scatter(sums):
        return [sums[0]] + [swap(sums[m], "head", head_size, m) for m in range(1, head_size)]

    bits = [1 << i for i in range(1, dp_size.bit_length() - 1)]

    def late_steps():
        return [(bits[i], bits[i + 1], bits[i] + bits[i + 1]) if i + 1 < len(bits) else (bits[i],) for i in range(0, len(bits), 2)]

    def sum_early_late(low, high, late):
        pairs = list(zip(bits, bits[1:] + bits[:1]))

        def pair(low, high, masks, before, last):
            got = [tie(swap(x, "dp", dp_size, mask), *before) for x, mask in zip((low, high), masks)]
            kernel, more = (last_pair_kernel, 128) if last else (pair_sum_kernel, 0)
            return small_call(kernel, [(low.shape, BF), ((high.shape[0] + more, 256), BF)], "pair_sum")(low, got[0], high, got[1])

        low, high = pair(low, high, pairs[0], late[1:], len(pairs) == 1)
        late = four_sum(160, late)
        for masks in late_steps():
            terms = [late] + [swap(late, "dp", dp_size, mask) for mask in masks]
            before = terms[1:]
            late = four_sum(160, terms + [jnp.zeros_like(late)] * (4 - len(terms)))
        for i, masks in enumerate(pairs[1:]):
            low, high = pair(low, high, masks, before, i == len(pairs) - 2)
        return low, high, late

    def body(tokens, lengths, cotangent, gain_attn, gain_mlp, w_qkv, w_out, w_up, w_down, w_cross, b_cross):
        rows = tokens.shape[0]
        own0, own1, half_a0, half_r, half_m1, mask = pl.pallas_call(
            pack_kernel,
            in_specs=[SMEM] + [ANY] * 5 + [VMEM],
            out_specs=[VMEM] * 6,
            out_shape=[jax.ShapeDtypeStruct((n, 256), BF) for n in (352, 352, 176, 432, 256)]
            + [jax.ShapeDtypeStruct((rows, 128), F32)],
            scratch_shapes=[pltpu.SemaphoreType.DMA((2,))],
            name="pack",
        )(lengths, w_qkv.transpose(0, 2, 3, 1), w_cross.transpose(0, 2, 1), w_out, w_up, w_down, b_cross)

        a0 = fetch(half_a0)
        r = fetch(half_r)
        m1 = fetch(half_m1)
        pieces_a0 = [own0] + a0 + [core_swap(x) for x in a0]
        mid0, base0, *saved0 = attn_fwd(0, 0, tokens, mask, gain_attn, pieces_a0)
        r = [tie(x, mid0) for x in r]
        r = r + [core_swap(x) for x in r]
        cur1, hid0, slope0 = mlp_fwd(0, 0, mid0, base0, gain_mlp, [w_up, w_down] + r)
        mid1, base1, *saved1 = attn_fwd(1, 256, cur1, mask, gain_attn, [own1] + r)
        m1 = [tie(x, mid1) for x in m1]
        m1 = m1 + [core_swap(x) for x in m1]
        output, gm1, keep_m1, send_m1, small_m1 = mlp_both(1, 0, mid1, base1, cotangent, gain_mlp, [w_up, w_down] + m1)
        pre = attn_pre(1, 256, cotangent, gm1, cur1, saved1, [own1] + r)
        pre_done = pre[0]
        keep_m1, send_m1 = small_call(core_split_kernel, [((4, 128, 256), BF)] * 2, "core_split")(
            keep_m1, tie(core_swap(send_m1), pre_done))
        got_m1 = swap(send_m1, "dp", dp_size, 2)
        grad1, keep_a1, send_a1 = attn_bwd(1, 256, cur1, tie(mask, send_m1), saved1, gain_attn, pre, small_m1, [own1] + r)
        m1_sum = small_call(add_kernel, [((4, 128, 256), BF)], "add", LONG)(keep_m1, tie(got_m1, grad1))[0]
        sums = core_sum((None, 160), (m1_sum,), (keep_a1, tie(core_swap(send_a1), m1_sum)))
        got = scatter(sums)
        gm0, keep_m0, send_m0, small_m0 = mlp_bwd(0, 0, tie(grad1, *sums), mid0, hid0, slope0, gain_mlp, [w_up, w_down] + r)
        pre = attn_pre(0, 0, grad1, gm0, tokens, saved0, pieces_a0)
        gqkv, keep_a0, *send_a0 = attn_grads(0, 0, mask, saved0, gain_attn, pre, small_m0, pieces_a0)
        one = four_sum(288, [tie(x, gqkv) for x in got], LONG)
        sums = core_sum((256,), (keep_m0, tie(core_swap(send_m0), one)))
        got = scatter(sums)
        grad0 = attn_post(0, 0, tie(gqkv, *sums), gain_attn, tokens, pre, pieces_a0)
        low, high = small_call(early_sum_kernel, [((176 + CUT, 256), BF), ((384 - CUT, 256), BF)], "early_sum")(
            one, *[tie(x, grad0) for x in got])
        sums_a0 = core_sum((160,), (keep_a0, *[tie(core_swap(x), low) for x in send_a0]))
        late = scatter(sums_a0)
        low, high, late = sum_early_late(low, high, late)
        d_qkv, d_out, d_up, d_down, d_cross, d_ga, d_gm, d_bias = small_call(
            finish_kernel,
            [((LAYERS, 3, HD, 256), F32), ((LAYERS, HD, 256), F32), ((LAYERS, 256, 256), F32), ((LAYERS, 256, 256), F32),
             ((LAYERS, HD, 256), F32), ((LAYERS, 256), F32), ((LAYERS, 256), F32), ((LAYERS, HD), F32)],
            "finish",
        )(low, core_swap(low), high, core_swap(high), late, core_swap(late))
        return (output, grad0, d_ga, d_gm, d_qkv.transpose(0, 3, 1, 2), d_out, d_up, d_down,
                d_cross.transpose(0, 2, 1), d_bias)

    rows, weights = P(("dp", "head"), None), P(None, "head", None)
    return jax.shard_map(
        body,
        mesh=mesh,
        in_specs=(rows, P("dp"), rows, P(), P(), P(None, None, None, "head"), weights, P(None, None, "head"),
                  weights, P(None, None, "head"), P(None, "head")),
        out_specs=(rows, rows, P(), P(), P(None, None, None, "head"), weights, P(None, None, "head"),
                   weights, P(None, None, "head"), P(None, "head")),
        check_vma=False,
    )
```

```python
import functools

import jax
import jax.numpy as jnp
from jax import lax
from jax.experimental import pallas as pl
from jax.experimental.pallas import tpu as pltpu
from jax.sharding import PartitionSpec as P

HD = 64
LAYERS = 2
EPSILON = 1e-06
MASKED_SCORE = -1000000000.0
BF = jnp.bfloat16
F32 = jnp.float32

VMEM_LIMIT = 32 * 2**20
SMALL_LIMIT = 12 * 2**20
CUT = 96
UNROLL = {"attn_fwd": 4, "mlp_fwd": 4, "mlp_both": 4, "mlp_bwd": 4, "attn_bwd": 2, "attn_pre": 2, "attn_post": 2}
KERNEL_FLOPS = 1000
LONG = 50 * 10**9


def nn(a, b):
    return lax.dot_general(a, b, (((1,), (0,)), ((), ())), preferred_element_type=F32)


def nt(a, b):
    return lax.dot_general(a, b, (((1,), (1,)), ((), ())), preferred_element_type=F32)


def tn(a, b):
    return lax.dot_general(a, b, (((0,), (0,)), ((), ())), preferred_element_type=F32)


def rescale_of(values):
    return lax.rsqrt(jnp.mean(values * values, axis=-1, keepdims=True) + EPSILON)


def norm_back(values, rescale, gain, gradient):
    scaled = gradient * gain
    product_mean = jnp.mean(values * scaled, axis=-1, keepdims=True)
    normal = values * rescale
    grad_values = rescale * (scaled - normal * (rescale * product_mean))
    return grad_values, jnp.sum(gradient * normal, axis=0, keepdims=True)


def gelu_and_slope(u):
    cdf = 0.5 + 0.5 * lax.erf(u * 0.7071067811865476)
    density = jnp.exp2((-0.5 * 1.4426950408889634) * (u * u))
    return u * cdf, cdf + u * (density * 0.3989422804014327)


def slot_scores(q, k, mask):
    ones = jnp.where(lax.broadcasted_iota(jnp.int32, mask.shape, 0) == 0, 1.0, 0.0).astype(BF)
    return tn(jnp.concatenate([k, mask], axis=0), jnp.concatenate([q * BF(0.125), ones], axis=0))


def mask_rows(mask_ref, rows):
    return mask_ref[pl.ds(pl.multiple_of(rows.start // 16, 16), 16), :]


def head_index():
    return lax.axis_index("head")


def half_index():
    return lax.axis_index("dp") & 1


def quarter_index():
    return (lax.axis_index("dp") >> 1) & 1


def place_pieces(own, mine, theirs, dst, first=0):
    half = dst.shape[1] // 2
    keep = pl.multiple_of(half_index() * half, 16)
    other = pl.multiple_of((1 - half_index()) * half, 16)
    at = 0
    for part in own:
        dst[0, at:at + part.shape[0], :] = part
        at += part.shape[0]
    for m in range(3):
        dst[m + 1, pl.ds(keep, half), :] = mine[m][first:first + half, :]
        dst[m + 1, pl.ds(other, half), :] = theirs[m][first:first + half, :]


def place_attn(first, pieces, wa, w_cross, w_out):
    place_pieces((pieces[0][...],), pieces[1:4], pieces[4:7], wa, first)
    total = jnp.zeros((1, 256), F32)
    for m in range(4):
        place = pl.multiple_of((head_index() ^ m) * HD, HD)
        w_cross[pl.ds(place, HD), :] = wa[m, 192:256, :]
        w_out[m * HD:(m + 1) * HD, :] = wa[m, 256:320, :]
        total = total + wa[m, 320:336, :].astype(F32)[0:1, :]
    return total


def place_mlp(layer, first, pieces, wm):
    place_pieces((pieces[0][layer], pieces[1][layer]), pieces[2:5], pieces[5:8], wm, first)


def each_sample(rows, unroll, step, *init, size=256):
    def body(i, carried):
        return step(pl.ds(pl.multiple_of(i * size, size), size), *carried)

    return lax.fori_loop(0, rows // size, body, init, unroll=unroll)


def attn_fwd_kernel(layer, first, cur_ref, mask_ref, gain_ref, p0, p1, p2, p3, p4, p5, p6,
                    middle_ref, base_ref, nrm_ref, qkv_ref, mix_ref, lse_ref, wa, w_cross, w_out):
    bias = place_attn(first, (p0, p1, p2, p3, p4, p5, p6), wa, w_cross, w_out)
    gain = gain_ref[layer:layer + 1, :]
    def step(rows):
        cur = cur_ref[rows, :].astype(F32)
        nrm = (cur * rescale_of(cur) * gain).astype(BF)
        nrm_ref[rows, :] = nrm
        mask = mask_rows(mask_ref, rows)
        qkv = [nt(wa[m, 0:192, :], nrm).astype(BF) for m in range(4)]
        scores = [slot_scores(qkv[m][0:64], qkv[m][64:128], mask) for m in range(4)]
        cross = nt(nrm, w_cross[...]) + bias
        probs = []
        for m in range(4):
            qkv_ref[m * 192:(m + 1) * 192, rows] = qkv[m]
            top = jnp.max(scores[m], axis=0, keepdims=True)
            e = jnp.exp(scores[m] - top)
            total = jnp.sum(e, axis=0, keepdims=True)
            probs.append((e * (1.0 / total)).astype(BF))
            lse_ref[m:m + 1, rows] = top + jnp.log(total)
        mix = jnp.concatenate([nn(qkv[m][128:192], probs[m]).astype(BF) for m in range(4)], axis=0)
        mix_ref[:, rows] = mix
        middle = cur + tn(mix, w_out[...])
        middle_ref[rows, :] = middle
        base_ref[rows, :] = middle + cur * cross
        return ()

    each_sample(cur_ref.shape[0], UNROLL["attn_fwd"], step)


def mlp_fwd_block(middle, gain, wm):
    r = rescale_of(middle)
    n2 = (middle * r * gain).astype(BF)
    us = [nn(n2, wm[m, 0:256, :]) for m in range(4)]
    kept = []
    for u in us:
        hid, slope = gelu_and_slope(u)
        kept.append((hid.astype(BF), slope.astype(BF)))
    feed = [nn(kept[m][0], wm[m, 256:512, :]) for m in range(4)]
    return r, n2, kept, (feed[0] + feed[1]) + (feed[2] + feed[3])


def mlp_fwd_kernel(layer, first, middle_ref, base_ref, gain_ref, p0, p1, p2, p3, p4, p5, p6, p7,
                   out_ref, hid_ref, slope_ref, wm):
    place_mlp(layer, first, (p0, p1, p2, p3, p4, p5, p6, p7), wm)
    gain = gain_ref[layer:layer + 1, :]
    def step(rows):
        _, _, kept, feed = mlp_fwd_block(middle_ref[rows, :], gain, wm)
        for m, (hid, slope) in enumerate(kept):
            hid_ref[rows, m * 256:(m + 1) * 256] = hid
            slope_ref[rows, m * 256:(m + 1) * 256] = slope
        out_ref[rows, :] = base_ref[rows, :] + feed
        return ()

    each_sample(middle_ref.shape[0], UNROLL["mlp_fwd"], step)


def mlp_bwd_block(gf, kept, wm):
    ghs = [nt(gf, wm[m, 256:512, :]) for m in range(4)]
    gps = [(gh * slope.astype(F32)).astype(BF) for gh, (_, slope) in zip(ghs, kept)]
    gn = [nt(gps[m], wm[m, 0:256, :]) for m in range(4)]
    return gps, (gn[0] + gn[1]) + (gn[2] + gn[3])


def put_mlp_grads(hid, gp, n2, gf, keep_ref, send_ref):
    for m in range(4):
        columns = slice(m * 256, (m + 1) * 256)
        up = tn(n2[...], gp[:, columns]).astype(BF)
        down = tn(hid[:, columns], gf[...]).astype(BF)
        own_up = half_index() == 0
        keep_ref[m] = jnp.where(own_up, up, down)
        send_ref[m] = jnp.where(own_up, down, up)


def mlp_both_kernel(layer, first, middle_ref, base_ref, cot_ref, gain_ref, p0, p1, p2, p3, p4, p5, p6, p7,
                    out_ref, gm_ref, keep_ref, send_ref, small_ref, wm, hid_all, gp_all, n2_all):
    place_mlp(layer, first, (p0, p1, p2, p3, p4, p5, p6, p7), wm)
    gain = gain_ref[layer:layer + 1, :]
    def step(rows, gain_grad):
        middle = middle_ref[rows, :]
        r, n2, kept, feed = mlp_fwd_block(middle, gain, wm)
        out_ref[rows, :] = base_ref[rows, :] + feed
        gf = cot_ref[rows, :]
        gps, gn = mlp_bwd_block(gf, kept, wm)
        n2_all[rows, :] = n2
        for m in range(4):
            hid_all[rows, m * 256:(m + 1) * 256] = kept[m][0]
            gp_all[rows, m * 256:(m + 1) * 256] = gps[m]
        back, part = norm_back(middle, r, gain, gn)
        gain_grad = gain_grad + part
        gm_ref[rows, :] = gf.astype(F32) + back
        return (gain_grad, )

    gain_grad, = each_sample(middle_ref.shape[0], UNROLL["mlp_both"], step, jnp.zeros((1, 256), F32))
    small_ref[...] = jnp.broadcast_to(gain_grad, small_ref.shape)
    put_mlp_grads(hid_all, gp_all, n2_all, cot_ref, keep_ref, send_ref)


def mlp_bwd_kernel(layer, first, grad_ref, middle_ref, hid_ref, slope_ref, gain_ref, p0, p1, p2, p3, p4, p5, p6, p7,
                   gm_ref, keep_ref, send_ref, small_ref, wm, gp_all, n2_all, gf_all):
    place_mlp(layer, first, (p0, p1, p2, p3, p4, p5, p6, p7), wm)
    gain = gain_ref[layer:layer + 1, :]
    def step(rows, gain_grad):
        middle = middle_ref[rows, :]
        r = rescale_of(middle)
        n2_all[rows, :] = (middle * r * gain).astype(BF)
        grad = grad_ref[rows, :]
        gf = grad.astype(BF)
        gf_all[rows, :] = gf
        kept = [(None, slope_ref[rows, m * 256:(m + 1) * 256]) for m in range(4)]
        gps, gn = mlp_bwd_block(gf, kept, wm)
        for m in range(4):
            gp_all[rows, m * 256:(m + 1) * 256] = gps[m]
        back, part = norm_back(middle, r, gain, gn)
        gain_grad = gain_grad + part
        gm_ref[rows, :] = grad + back
        return (gain_grad, )

    gain_grad, = each_sample(middle_ref.shape[0], UNROLL["mlp_bwd"], step, jnp.zeros((1, 256), F32))
    small_ref[...] = jnp.broadcast_to(gain_grad, small_ref.shape)
    put_mlp_grads(hid_ref, gp_all, n2_all, gf_all, keep_ref, send_ref)


def attn_pre_kernel(layer, first, grad_ref, gm_ref, cur_ref, nrm_ref, mix_ref, p0, p1, p2, p3, p4, p5, p6,
                    gmix_ref, d_cross_ref, d_out_ref, base_ref, gn_ref, small_ref, dot_ref,
                    wa, w_cross, w_out, ga_all, gc_all):
    bias = place_attn(first, (p0, p1, p2, p3, p4, p5, p6), wa, w_cross, w_out)

    def step(rows, bias_grad):
        grad = grad_ref[rows, :].astype(F32)
        gm = gm_ref[rows, :]
        ga = gm.astype(BF)
        ga_all[rows, :] = ga
        gc = (grad * cur_ref[rows, :].astype(F32)).astype(BF)
        gc_all[rows, :] = gc
        gmix = nt(w_out[...], ga).astype(BF)
        gmix_ref[:, rows] = gmix
        for m in range(4):
            head = slice(m * HD, (m + 1) * HD)
            product = gmix[head].astype(F32) * mix_ref[head, rows].astype(F32)
            dot_ref[m:m + 1, rows] = jnp.sum(product, axis=0, keepdims=True)
        gn_ref[rows, :] = nn(gc, w_cross[...])
        base_ref[rows, :] = gm + grad * (nt(nrm_ref[rows, :], w_cross[...]) + bias)
        return (bias_grad + jnp.sum(gc.astype(F32), axis=0, keepdims=True), )

    bias_grad, = each_sample(cur_ref.shape[0], UNROLL["attn_pre"], step, jnp.zeros((1, 256), F32))
    d_cross = tn(gc_all[...], nrm_ref[...])
    d_cross_ref[...] = d_cross.astype(BF)
    d_out_ref[...] = nn(mix_ref[...], ga_all[...]).astype(BF)
    small_ref[0:1, :] = bias_grad
    small_ref[1:2, :] = jnp.sum(d_cross * w_cross[...].astype(F32), axis=0, keepdims=True)


def qkv_back(rows, mask_ref, qkv_ref, lse_ref, gmix_ref, dot_ref):
    mask = mask_rows(mask_ref, rows)
    parts = []
    for m in range(4):
        q, k, v = (qkv_ref[m * 192 + i * HD:m * 192 + (i + 1) * HD, rows] for i in range(3))
        parts.append((q, k, v, gmix_ref[m * HD:(m + 1) * HD, rows]))
    scores = [slot_scores(q, k, mask) for q, k, v, go in parts]
    gps = [tn(v, go) for q, k, v, go in parts]
    ps, gss = [], []
    for m in range(4):
        p = jnp.exp(scores[m] - lse_ref[m:m + 1, rows])
        ps.append(p.astype(BF))
        gss.append((p * (gps[m] - dot_ref[m:m + 1, rows])).astype(BF))
    return [
        jnp.concatenate([nn(k, gs) * 0.125, nt(q, gs) * 0.125, nt(go, p)], axis=0).astype(BF)
        for (q, k, v, go), p, gs in zip(parts, ps, gss)
    ]


def norm_grad(cur, gain, gn):
    r = rescale_of(cur)
    scaled = gn * gain
    return r * (scaled - cur * (r * r * jnp.mean(cur * scaled, axis=-1, keepdims=True)))


def place_qkv(first, pieces, wa):
    place_pieces((pieces[0][...],), pieces[1:4], pieces[4:7], wa, first)


def put_attn_grads(layer, nrm, gqkv_all, wa, gain_ref, d_cross_ref, d_out_ref, small, mlp_small, payload, keep_ref, sends):
    gain_grad = small[1:2, :]
    for m in range(4):
        place = pl.multiple_of((head_index() ^ m) * HD, HD)
        d_qkv = nn(gqkv_all[m * 192:(m + 1) * 192, :], nrm)
        gain_grad = gain_grad + jnp.sum(d_qkv * wa[m, 0:192, :].astype(F32), axis=0, keepdims=True)
        payload[m, 0:192, :] = d_qkv.astype(BF)
        payload[m, 192:256, :] = d_cross_ref[pl.ds(place, HD), :]
        payload[m, 256:320, :] = d_out_ref[m * HD:(m + 1) * HD, :]
    gain_grad = gain_grad / gain_ref[layer:layer + 1, :]
    high, low = split_rows(jnp.concatenate([gain_grad, small[0:1, :], mlp_small[0:1, :], jnp.zeros((5, 256), F32)], axis=0))
    keep = pl.multiple_of(half_index() * 160, 16)
    other = pl.multiple_of((1 - half_index()) * 160, 16)
    for m in range(4):
        each = 4 // len(sends)
        for ref, i, at in ((keep_ref, m, keep), (sends[m // each], m % each, other)):
            ref[i, 0:160, :] = payload[m, pl.ds(at, 160), :]
            ref[i, 160:168, :] = high
            ref[i, 168:176, :] = low


def attn_bwd_kernel(layer, first, mask_ref, nrm_ref, qkv_ref, lse_ref, gain_ref, gmix_ref, d_cross_ref, d_out_ref, small, dot_ref, mlp_small,
                    cur_ref, base_ref, gn_ref, p0, p1, p2, p3, p4, p5, p6,
                    out_ref, keep_ref, send_ref, wa, gqkv_all, payload):
    place_qkv(first, (p0, p1, p2, p3, p4, p5, p6), wa)

    def step(rows):
        gn = gn_ref[rows, :]
        for m, gqkv in enumerate(qkv_back(rows, mask_ref, qkv_ref, lse_ref, gmix_ref, dot_ref)):
            gqkv_all[m * 192:(m + 1) * 192, rows] = gqkv
            gn = gn + tn(gqkv, wa[m, 0:192, :])
        out_ref[rows, :] = base_ref[rows, :] + norm_grad(cur_ref[rows, :].astype(F32), gain_ref[layer:layer + 1, :], gn)
        return ()

    each_sample(nrm_ref.shape[0], UNROLL["attn_bwd"], step)
    put_attn_grads(layer, nrm_ref[...], gqkv_all, wa, gain_ref, d_cross_ref, d_out_ref, small, mlp_small,
                   payload, keep_ref, (send_ref,))


def attn_grads_kernel(layer, first, mask_ref, nrm_ref, qkv_ref, lse_ref, gain_ref, gmix_ref, d_cross_ref, d_out_ref, small, dot_ref, mlp_small,
                      p0, p1, p2, p3, p4, p5, p6, gqkv_all, keep_ref, send_low, send_high, wa, payload):
    place_qkv(first, (p0, p1, p2, p3, p4, p5, p6), wa)

    def step(rows):
        for m, gqkv in enumerate(qkv_back(rows, mask_ref, qkv_ref, lse_ref, gmix_ref, dot_ref)):
            gqkv_all[m * 192:(m + 1) * 192, rows] = gqkv
        return ()

    each_sample(nrm_ref.shape[0], UNROLL["attn_bwd"], step)
    put_attn_grads(layer, nrm_ref[...], gqkv_all, wa, gain_ref, d_cross_ref, d_out_ref, small, mlp_small,
                   payload, keep_ref, (send_low, send_high))


def attn_post_kernel(layer, first, gqkv_all, gain_ref, cur_ref, base_ref, gn_ref, p0, p1, p2, p3, p4, p5, p6, out_ref, wa):
    place_qkv(first, (p0, p1, p2, p3, p4, p5, p6), wa)

    def step(rows):
        gn = gn_ref[rows, :]
        for m in range(4):
            gn = gn + tn(gqkv_all[m * 192:(m + 1) * 192, rows], wa[m, 0:192, :])
        out_ref[rows, :] = base_ref[rows, :] + norm_grad(cur_ref[rows, :].astype(F32), gain_ref[layer:layer + 1, :], gn)
        return ()

    each_sample(cur_ref.shape[0], UNROLL["attn_post"], step)


def split_rows(x):
    high = x.astype(BF)
    return high, (x - high.astype(F32)).astype(BF)


def pack_kernel(lens, qkv, cross, out, up, down, b, own0, own1, half_a0, half_r, half_m1, mask, sems):
    copies = []
    for l, own in ((0, own0), (1, own1)):
        for t in range(3):
            copies.append(pltpu.make_async_copy(qkv.at[l, t], own.at[pl.ds(t * HD, HD)], sems.at[0]))
        copies.append(pltpu.make_async_copy(cross.at[l], own.at[pl.ds(192, HD)], sems.at[0]))
        copies.append(pltpu.make_async_copy(out.at[l], own.at[pl.ds(256, HD)], sems.at[0]))
    for copy in copies:
        copy.start()

    def mlp_half(weight):
        return (pltpu.make_async_copy(weight.at[0], half_r.at[pl.ds(0, 256)], sems.at[1]),
                pltpu.make_async_copy(weight.at[1], half_m1, sems.at[1]))

    @pl.when(half_index() == 0)
    def _():
        for copy in mlp_half(up):
            copy.start()

    @pl.when(half_index() != 0)
    def _():
        for copy in mlp_half(down):
            copy.start()

    slots = lax.broadcasted_iota(jnp.int32, (16, 256), 1)
    first = lax.broadcasted_iota(jnp.int32, (16, 256), 0) == 0
    samples = mask.shape[0] // 16
    for i in range(samples):
        length = lens[head_index() * samples + i]
        mask[i * 16:(i + 1) * 16, :] = jnp.where(jnp.logical_and(first, slots >= length), MASKED_SCORE, 0.0).astype(BF)
    lane = lax.broadcasted_iota(jnp.int32, (LAYERS, 256), 1) // HD
    wide = jnp.concatenate([b[...].astype(F32)] * 4, axis=1)
    wide = jnp.where(lane == head_index(), wide, 0.0)
    for l, own in ((0, own0), (1, own1)):
        own[320:352, :] = jnp.broadcast_to(wide[l:l + 1], (32, 256)).astype(BF)
    for copy in copies:
        copy.wait()
    at = pl.multiple_of(half_index() * 176, 16)
    half_a0[...] = own0[pl.ds(at, 176), :]
    half_r[256:432, :] = own1[pl.ds(at, 176), :]
    for copy in mlp_half(up):
        copy.wait()


def put_sum(out, at, small_at, rows, total):
    for low, high in ((0, small_at), (small_at + 16, rows)):
        if low < high:
            out[at + low:at + high, :] = total(low, high).astype(BF)
    if small_at < rows:
        both = total(small_at, small_at + 16)
        high, low = split_rows(both[0:8] + both[8:16])
        out[at + small_at:at + small_at + 8, :] = high
        out[at + small_at + 8:at + small_at + 16, :] = low


def core_sum_kernel(small_at, *refs):
    ins, outs = refs[:-4], refs[-4:]
    for m, out in enumerate(outs):
        at = 0
        rest = list(ins)
        for where in small_at:
            keep = rest.pop(0)
            if where is None:
                out[at:at + keep.shape[1], :] = keep[m]
                at += keep.shape[1]
                continue
            got, index = rest.pop(0), m
            if got.shape[0] < keep.shape[0]:
                got, index = (got, rest.pop(0))[m // 2], m % 2
            rows = keep.shape[1]
            put_sum(out, at, where, rows, lambda i, j: keep[m, i:j].astype(F32) + got[index, i:j].astype(F32))
            at += rows


def core_split_kernel(keep, got, keep_out, send_out):
    at = pl.multiple_of(quarter_index() * 128, 16)
    other = pl.multiple_of((1 - quarter_index()) * 128, 16)
    for out, rows in ((keep_out, pl.ds(at, 128)), (send_out, pl.ds(other, 128))):
        for m in range(4):
            out[m] = (keep[m, rows, :].astype(F32) + got[m, rows, :].astype(F32)).astype(BF)


def add_kernel(a, b, out):
    out[...] = (a[...].astype(F32) + b[...].astype(F32)).astype(BF)


def four_sum_kernel(small_at, *refs):
    s, a, b, c, out = refs
    put_sum(out, 0, small_at, s.shape[0],
            lambda i, j: (s[i:j].astype(F32) + a[i:j].astype(F32)) + (b[i:j].astype(F32) + c[i:j].astype(F32)))


def early_sum_kernel(one, s, a, b, c, low, high):
    total = (s[...].astype(F32) + a[...].astype(F32)) + (b[...].astype(F32) + c[...].astype(F32))
    low[0:176, :] = one[128:304, :]
    low[176:176 + CUT, :] = total[0:CUT].astype(BF)
    high[0:256 - CUT, :] = total[CUT:256].astype(BF)
    high[256 - CUT:384 - CUT, :] = one[0:128, :]


def pair_sum_kernel(low, low_got, high, high_got, low_out, high_out):
    put_sum(low_out, 0, 160, low.shape[0], lambda i, j: low[i:j].astype(F32) + low_got[i:j].astype(F32))
    high_out[...] = (high[...].astype(F32) + high_got[...].astype(F32)).astype(BF)


def last_pair_kernel(low, low_got, high, high_got, low_out, high_out):
    put_sum(low_out, 0, 160, low.shape[0], lambda i, j: low[i:j].astype(F32) + low_got[i:j].astype(F32))
    rows = 256 - CUT
    high_out[0:rows, :] = (high[0:rows].astype(F32) + high_got[0:rows].astype(F32)).astype(BF)
    high_out[rows:rows + 128, :] = high[rows:rows + 128]
    high_out[rows + 128:rows + 256, :] = high_got[rows:rows + 128]


def finish_kernel(low, low_other, high, high_other, late, late_other,
                  d_qkv, d_out, d_up, d_down, d_cross, gain_attn, gain_mlp, bias):
    rows = 256 - CUT
    mine = pl.multiple_of(quarter_index() * 128, 16)
    other = pl.multiple_of((1 - quarter_index()) * 128, 16)

    def place(first, second):
        for l, a, b in ((1, first[0], second[0]), (0, first[2], second[2])):
            d_qkv[l, 0] = a[0:64].astype(F32)
            d_qkv[l, 1] = a[64:128].astype(F32)
            d_qkv[l, 2, 0:32] = a[128:160].astype(F32)
            d_qkv[l, 2, 32:64] = b[0:32].astype(F32)
            d_cross[l] = b[32:96].astype(F32)
            d_out[l] = b[96:160].astype(F32)
        for dst, (lo, hi, _) in ((d_up, first), (d_down, second)):
            dst[0, 0:CUT] = lo[176:176 + CUT].astype(F32)
            dst[0, CUT:256] = hi[0:rows].astype(F32)
            dst[1, pl.ds(mine, 128)] = hi[rows:rows + 128].astype(F32)
            dst[1, pl.ds(other, 128)] = hi[rows + 128:rows + 256].astype(F32)

    @pl.when(half_index() == 0)
    def _():
        place((low, high, late), (low_other, high_other, late_other))

    @pl.when(half_index() != 0)
    def _():
        place((low_other, high_other, late_other), (low, high, late))

    for l, ref in ((0, late), (1, low)):
        small = ref[160:168].astype(F32) + ref[168:176].astype(F32)
        gain_attn[l:l + 1, :] = small[0:1]
        gain_mlp[l:l + 1, :] = small[2:3]
        total = jnp.zeros((1, HD), F32)
        for h in range(4):
            total = total + jnp.where(head_index() == h, small[1:2, h * HD:(h + 1) * HD], 0.0)
        bias[l:l + 1, :] = total


SMEM = pl.BlockSpec(memory_space=pltpu.SMEM)
ANY = pl.BlockSpec(memory_space=pl.ANY)


def call(kernel, outs, scratch, name, *args):
    return pl.pallas_call(
        kernel,
        in_specs=[VMEM] * len(args),
        out_specs=[VMEM] * len(outs),
        out_shape=[jax.ShapeDtypeStruct(shape, dtype) for shape, dtype in outs],
        scratch_shapes=[pltpu.VMEM(shape, dtype) for shape, dtype in scratch],
        compiler_params=pltpu.CompilerParams(vmem_limit_bytes=VMEM_LIMIT),
        cost_estimate=pl.CostEstimate(flops=KERNEL_FLOPS, bytes_accessed=1024, transcendentals=0),
        name=name,
    )(*args)


ATTN_SCRATCH = [((4, 352, 256), BF), ((256, 256), BF), ((256, 256), BF)]
MLP_GRADS = [((4, 256, 256), BF), ((4, 256, 256), BF), ((8, 256), F32)]


def attn_fwd(layer, first, cur, mask, gain, pieces):
    rows = cur.shape[0]
    outs = [((rows, 256), F32), ((rows, 256), F32), ((rows, 256), BF), ((768, rows), BF), ((256, rows), BF), ((8, rows), F32)]
    return call(functools.partial(attn_fwd_kernel, layer, first), outs, ATTN_SCRATCH, "attn_fwd", cur, mask, gain, *pieces)


def mlp_fwd(layer, first, middle, base, gain, pieces):
    rows = middle.shape[0]
    outs = [((rows, 256), F32), ((rows, 1024), BF), ((rows, 1024), BF)]
    return call(functools.partial(mlp_fwd_kernel, layer, first), outs, [((4, 512, 256), BF)], "mlp_fwd",
                middle, base, gain, *pieces)


def mlp_both(layer, first, middle, base, cot, gain, pieces):
    rows = middle.shape[0]
    outs = [((rows, 256), F32), ((rows, 256), F32)] + MLP_GRADS
    scratch = [((4, 512, 256), BF), ((rows, 1024), BF), ((rows, 1024), BF), ((rows, 256), BF)]
    return call(functools.partial(mlp_both_kernel, layer, first), outs, scratch, "mlp_both", middle, base, cot, gain, *pieces)


def mlp_bwd(layer, first, grad, middle, hid, slope, gain, pieces):
    rows = middle.shape[0]
    outs = [((rows, 256), F32)] + MLP_GRADS
    scratch = [((4, 512, 256), BF), ((rows, 1024), BF), ((rows, 256), BF), ((rows, 256), BF)]
    return call(functools.partial(mlp_bwd_kernel, layer, first), outs, scratch, "mlp_bwd",
                grad, middle, hid, slope, gain, *pieces)


def attn_pre(layer, first, grad, gm, cur, saved, pieces):
    rows = cur.shape[0]
    nrm, _, mix, _ = saved
    outs = [((256, rows), BF), ((256, 256), BF), ((256, 256), BF), ((rows, 256), F32), ((rows, 256), F32), ((8, 256), F32), ((8, rows), F32)]
    scratch = ATTN_SCRATCH + [((rows, 256), BF), ((rows, 256), BF)]
    return call(functools.partial(attn_pre_kernel, layer, first), outs, scratch, "attn_pre", grad, gm, cur, nrm, mix, *pieces)


PAYLOAD = [((4, 176, 256), BF), ((4, 176, 256), BF)]


def attn_bwd(layer, first, cur, mask, saved, gain, pre, mlp_small, pieces):
    rows = cur.shape[0]
    nrm, qkv, _, lse = saved
    gmix, d_cross, d_out, base, gn, small, dot = pre
    scratch = [((4, 352, 256), BF), ((768, rows), BF), ((4, 320, 256), BF)]
    return call(functools.partial(attn_bwd_kernel, layer, first), [((rows, 256), F32)] + PAYLOAD, scratch, "attn_bwd",
                mask, nrm, qkv, lse, gain, gmix, d_cross, d_out, small, dot, mlp_small, cur, base, gn, *pieces)


def attn_grads(layer, first, mask, saved, gain, pre, mlp_small, pieces):
    nrm, qkv, _, lse = saved
    gmix, d_cross, d_out, _, _, small, dot = pre
    scratch = [((4, 352, 256), BF), ((4, 320, 256), BF)]
    return call(functools.partial(attn_grads_kernel, layer, first), [((768, nrm.shape[0]), BF), ((4, 176, 256), BF), ((2, 176, 256), BF), ((2, 176, 256), BF)], scratch, "attn_grads",
                mask, nrm, qkv, lse, gain, gmix, d_cross, d_out, small, dot, mlp_small, *pieces)


def attn_post(layer, first, gqkv, gain, cur, pre, pieces):
    return call(functools.partial(attn_post_kernel, layer, first), [((cur.shape[0], 256), F32)], [((4, 352, 256), BF)], "attn_post",
                gqkv, gain, cur, pre[3], pre[4], *pieces)[0]


VMEM = pl.BlockSpec(memory_space=pltpu.VMEM)


def small_call(kernel, shapes, name, flops=1000):
    def run(*args):
        return pl.pallas_call(
            kernel,
            in_specs=[VMEM] * len(args),
            out_specs=[VMEM] * len(shapes),
            out_shape=[jax.ShapeDtypeStruct(shape, dtype) for shape, dtype in shapes],
            compiler_params=pltpu.CompilerParams(vmem_limit_bytes=SMALL_LIMIT),
            cost_estimate=pl.CostEstimate(flops=flops, bytes_accessed=1024, transcendentals=0),
            name=name,
        )(*args)
    return run


def core_sum(small_at, *groups):
    rows = sum(group[0].shape[1] for group in groups)
    return small_call(functools.partial(core_sum_kernel, small_at), [((rows, 256), BF)] * 4, "core_sum")(
        *[x for group in groups for x in group])


def four_sum(small_at, terms, flops=1000):
    return small_call(functools.partial(four_sum_kernel, small_at), [(terms[0].shape, BF)], "four_sum", flops)(*terms)[0]


def swap(x, axis, size, mask):
    return lax.ppermute(x, axis, [(i, i ^ mask) for i in range(size)])


def tie(x, *before):
    return lax.optimization_barrier((x,) + before)[0]


def solution(mesh):
    dp_size, head_size = mesh.shape["dp"], mesh.shape["head"]

    def core_swap(x):
        return swap(x, "dp", dp_size, 1)

    def fetch(x):
        return [swap(x, "head", head_size, m) for m in range(1, head_size)]

    def scatter(sums):
        return [sums[0]] + [swap(sums[m], "head", head_size, m) for m in range(1, head_size)]

    bits = [1 << i for i in range(1, dp_size.bit_length() - 1)]

    def late_steps():
        return [(bits[i], bits[i + 1], bits[i] + bits[i + 1]) if i + 1 < len(bits) else (bits[i],) for i in range(0, len(bits), 2)]

    def sum_early_late(low, high, late):
        pairs = list(zip(bits, bits[1:] + bits[:1]))

        def pair(low, high, masks, before, last):
            got = [tie(swap(x, "dp", dp_size, mask), *before) for x, mask in zip((low, high), masks)]
            kernel, more = (last_pair_kernel, 128) if last else (pair_sum_kernel, 0)
            return small_call(kernel, [(low.shape, BF), ((high.shape[0] + more, 256), BF)], "pair_sum")(low, got[0], high, got[1])

        late = four_sum(160, late, LONG)
        low, high = pair(low, high, pairs[0], [late], len(pairs) == 1)
        for masks in late_steps():
            terms = [late] + [swap(late, "dp", dp_size, mask) for mask in masks]
            before = terms[1:]
            late = four_sum(160, terms + [jnp.zeros_like(late)] * (4 - len(terms)))
        for i, masks in enumerate(pairs[1:]):
            low, high = pair(low, high, masks, before, i == len(pairs) - 2)
        return low, high, late

    def body(tokens, lengths, cotangent, gain_attn, gain_mlp, w_qkv, w_out, w_up, w_down, w_cross, b_cross):
        rows = tokens.shape[0]
        own0, own1, half_a0, half_r, half_m1, mask = pl.pallas_call(
            pack_kernel,
            in_specs=[SMEM] + [ANY] * 5 + [VMEM],
            out_specs=[VMEM] * 6,
            out_shape=[jax.ShapeDtypeStruct((n, 256), BF) for n in (352, 352, 176, 432, 256)]
            + [jax.ShapeDtypeStruct((rows // 16, 256), BF)],
            scratch_shapes=[pltpu.SemaphoreType.DMA((2,))],
            name="pack",
        )(lengths, w_qkv.transpose(0, 2, 3, 1), w_cross.transpose(0, 2, 1), w_out, w_up, w_down, b_cross)

        a0 = fetch(half_a0)
        r = fetch(half_r)
        m1 = fetch(half_m1)
        pieces_a0 = [own0] + a0 + [core_swap(x) for x in a0]
        mid0, base0, *saved0 = attn_fwd(0, 0, tokens, mask, gain_attn, pieces_a0)
        r = [tie(x, mid0) for x in r]
        r = r + [core_swap(x) for x in r]
        cur1, hid0, slope0 = mlp_fwd(0, 0, mid0, base0, gain_mlp, [w_up, w_down] + r)
        mid1, base1, *saved1 = attn_fwd(1, 256, cur1, mask, gain_attn, [own1] + r)
        m1 = [tie(x, mid1) for x in m1]
        m1 = m1 + [core_swap(x) for x in m1]
        output, gm1, keep_m1, send_m1, small_m1 = mlp_both(1, 0, mid1, base1, cotangent, gain_mlp, [w_up, w_down] + m1)
        pre = attn_pre(1, 256, cotangent, gm1, cur1, saved1, [own1] + r)
        pre_done = pre[0]
        keep_m1, send_m1 = small_call(core_split_kernel, [((4, 128, 256), BF)] * 2, "core_split")(
            keep_m1, tie(core_swap(send_m1), pre_done))
        got_m1 = swap(send_m1, "dp", dp_size, 2)
        grad1, keep_a1, send_a1 = attn_bwd(1, 256, cur1, tie(mask, send_m1), saved1, gain_attn, pre, small_m1, [own1] + r)
        m1_sum = small_call(add_kernel, [((4, 128, 256), BF)], "add", LONG)(keep_m1, tie(got_m1, grad1))[0]
        sums = core_sum((None, 160), (m1_sum,), (keep_a1, tie(core_swap(send_a1), m1_sum)))
        got = scatter(sums)
        gm0, keep_m0, send_m0, small_m0 = mlp_bwd(0, 0, tie(grad1, *sums), mid0, hid0, slope0, gain_mlp, [w_up, w_down] + r)
        pre = attn_pre(0, 0, grad1, gm0, tokens, saved0, pieces_a0)
        gqkv, keep_a0, *send_a0 = attn_grads(0, 0, mask, saved0, gain_attn, pre, small_m0, pieces_a0)
        one = four_sum(288, [tie(x, gqkv) for x in got], LONG)
        sums = core_sum((256,), (keep_m0, tie(core_swap(send_m0), one)))
        got = scatter(sums)
        grad0 = attn_post(0, 0, tie(gqkv, *sums), gain_attn, tokens, pre, pieces_a0)
        low, high = small_call(early_sum_kernel, [((176 + CUT, 256), BF), ((384 - CUT, 256), BF)], "early_sum")(
            one, *[tie(x, grad0) for x in got])
        sums_a0 = core_sum((160,), (keep_a0, *[core_swap(x) for x in send_a0]))
        late = scatter(sums_a0)
        low, high, late = sum_early_late(low, high, late)
        d_qkv, d_out, d_up, d_down, d_cross, d_ga, d_gm, d_bias = small_call(
            finish_kernel,
            [((LAYERS, 3, HD, 256), F32), ((LAYERS, HD, 256), F32), ((LAYERS, 256, 256), F32), ((LAYERS, 256, 256), F32),
             ((LAYERS, HD, 256), F32), ((LAYERS, 256), F32), ((LAYERS, 256), F32), ((LAYERS, HD), F32)],
            "finish",
        )(low, core_swap(low), high, core_swap(high), late, core_swap(late))
        return (output, grad0, d_ga, d_gm, d_qkv.transpose(0, 3, 1, 2), d_out, d_up, d_down,
                d_cross.transpose(0, 2, 1), d_bias)

    rows, weights = P(("dp", "head"), None), P(None, "head", None)
    return jax.shard_map(
        body,
        mesh=mesh,
        in_specs=(rows, P("dp"), rows, P(), P(), P(None, None, None, "head"), weights, P(None, None, "head"),
                  weights, P(None, None, "head"), P(None, "head")),
        out_specs=(rows, rows, P(), P(), P(None, None, None, "head"), weights, P(None, None, "head"),
                   weights, P(None, None, "head"), P(None, "head")),
        check_vma=False,
    )
```

```python
import functools

import jax
import jax.numpy as jnp
from jax import lax
from jax.experimental import pallas as pl
from jax.experimental.pallas import tpu as pltpu
from jax.sharding import PartitionSpec as P

HD = 64
LAYERS = 2
EPSILON = 1e-06
MASKED_SCORE = -1000000000.0
BF = jnp.bfloat16
F32 = jnp.float32

VMEM_LIMIT = 32 * 2**20
SMALL_LIMIT = 12 * 2**20
CUT = 96
UNROLL = {"attn_fwd": 4, "mlp_fwd": 4, "mlp_both": 4, "mlp_bwd": 4, "attn_bwd": 2, "attn_pre": 2, "attn_post": 2}
KERNEL_FLOPS = 1000
LONG = 50 * 10**9


def nn(a, b):
    return lax.dot_general(a, b, (((1,), (0,)), ((), ())), preferred_element_type=F32)


def nt(a, b):
    return lax.dot_general(a, b, (((1,), (1,)), ((), ())), preferred_element_type=F32)


def tn(a, b):
    return lax.dot_general(a, b, (((0,), (0,)), ((), ())), preferred_element_type=F32)


def rescale_of(values):
    return lax.rsqrt(jnp.mean(values * values, axis=-1, keepdims=True) + EPSILON)


def norm_back(values, rescale, gain, gradient):
    scaled = gradient * gain
    product_mean = jnp.mean(values * scaled, axis=-1, keepdims=True)
    normal = values * rescale
    grad_values = rescale * (scaled - normal * (rescale * product_mean))
    return grad_values, jnp.sum(gradient * normal, axis=0, keepdims=True)


def gelu_and_slope(u):
    cdf = 0.5 + 0.5 * lax.erf(u * 0.7071067811865476)
    density = jnp.exp2((-0.5 * 1.4426950408889634) * (u * u))
    return u * cdf, cdf + u * (density * 0.3989422804014327)


def slot_scores(q, k, mask):
    ones = jnp.where(lax.broadcasted_iota(jnp.int32, mask.shape, 0) == 0, 1.0, 0.0).astype(BF)
    return tn(jnp.concatenate([k, mask], axis=0), jnp.concatenate([q * BF(0.125), ones], axis=0))


def mask_rows(mask_ref, rows):
    return mask_ref[pl.ds(pl.multiple_of(rows.start // 16, 16), 16), :]


def head_index():
    return lax.axis_index("head")


def half_index():
    return lax.axis_index("dp") & 1


def quarter_index():
    return (lax.axis_index("dp") >> 1) & 1


def place_pieces(own, parts, dst, first, rows):
    at = 0
    for ref in own:
        dst[0, at:at + ref.shape[0], :] = ref
        at += ref.shape[0]
    for start, refs in parts:
        for m, ref in enumerate(refs):
            dst[m + 1, pl.ds(pl.multiple_of(start, 16), rows), :] = ref[first:first + rows, :]


def parts_of(pieces, rows):
    c, x = half_index(), quarter_index()
    if len(pieces) == 6:
        return [(c * rows, pieces[0:3]), ((1 - c) * rows, pieces[3:6])]
    places = [c, 1 - c] if len(pieces) == 2 else [2 * i + j for i, j in ((c, x), (c, 1 - x), (1 - c, x), (1 - c, 1 - x))]
    return [(place * rows, [ref.at[pl.ds(m * rows, rows)] for m in range(3)]) for place, ref in zip(places, pieces)]


def place_qkv(layer, pieces, wa):
    place_pieces((pieces[0][...],), parts_of(pieces[1:], 176), wa, 256 * layer, 176)


def place_attn(layer, pieces, wa, w_cross, w_out):
    place_qkv(layer, pieces, wa)
    total = jnp.zeros((1, 256), F32)
    for m in range(4):
        place = pl.multiple_of((head_index() ^ m) * HD, HD)
        w_cross[pl.ds(place, HD), :] = wa[m, 192:256, :]
        w_out[m * HD:(m + 1) * HD, :] = wa[m, 256:320, :]
        total = total + wa[m, 320:336, :].astype(F32)[0:1, :]
    return total


def place_mlp(layer, pieces, wm):
    rows = 256 if len(pieces) == 8 else 128
    place_pieces((pieces[0][layer], pieces[1][layer]), parts_of(pieces[2:], rows), wm, 0, rows)


def each_sample(rows, unroll, step, *init, size=256):
    def body(i, carried):
        return step(pl.ds(pl.multiple_of(i * size, size), size), *carried)

    return lax.fori_loop(0, rows // size, body, init, unroll=unroll)


def attn_fwd_kernel(layer, count, *refs):
    pieces = refs[:count]
    (cur_ref, mask_ref, gain_ref, middle_ref, base_ref, nrm_ref, qkv_ref, mix_ref, lse_ref, wa, w_cross, w_out) = refs[count:]
    bias = place_attn(layer, pieces, wa, w_cross, w_out)
    gain = gain_ref[layer:layer + 1, :]
    def step(rows):
        cur = cur_ref[rows, :].astype(F32)
        nrm = (cur * rescale_of(cur) * gain).astype(BF)
        nrm_ref[rows, :] = nrm
        mask = mask_rows(mask_ref, rows)
        qkv = [nt(wa[m, 0:192, :], nrm).astype(BF) for m in range(4)]
        scores = [slot_scores(qkv[m][0:64], qkv[m][64:128], mask) for m in range(4)]
        cross = nt(nrm, w_cross[...]) + bias
        probs = []
        for m in range(4):
            qkv_ref[m * 192:(m + 1) * 192, rows] = qkv[m]
            top = jnp.max(scores[m], axis=0, keepdims=True)
            e = jnp.exp(scores[m] - top)
            total = jnp.sum(e, axis=0, keepdims=True)
            probs.append((e * (1.0 / total)).astype(BF))
            lse_ref[m:m + 1, rows] = top + jnp.log(total)
        mix = jnp.concatenate([nn(qkv[m][128:192], probs[m]).astype(BF) for m in range(4)], axis=0)
        mix_ref[:, rows] = mix
        middle = cur + tn(mix, w_out[...])
        middle_ref[rows, :] = middle
        base_ref[rows, :] = middle + cur * cross
        return ()

    each_sample(cur_ref.shape[0], UNROLL["attn_fwd"], step)


def mlp_fwd_block(middle, gain, wm):
    r = rescale_of(middle)
    n2 = (middle * r * gain).astype(BF)
    us = [nn(n2, wm[m, 0:256, :]) for m in range(4)]
    kept = []
    for u in us:
        hid, slope = gelu_and_slope(u)
        kept.append((hid.astype(BF), slope.astype(BF)))
    feed = [nn(kept[m][0], wm[m, 256:512, :]) for m in range(4)]
    return r, n2, kept, (feed[0] + feed[1]) + (feed[2] + feed[3])


def mlp_fwd_kernel(layer, count, *refs):
    pieces = refs[:count]
    (middle_ref, base_ref, gain_ref, out_ref, hid_ref, slope_ref, wm) = refs[count:]
    place_mlp(layer, pieces, wm)
    gain = gain_ref[layer:layer + 1, :]
    def step(rows):
        _, _, kept, feed = mlp_fwd_block(middle_ref[rows, :], gain, wm)
        for m, (hid, slope) in enumerate(kept):
            hid_ref[rows, m * 256:(m + 1) * 256] = hid
            slope_ref[rows, m * 256:(m + 1) * 256] = slope
        out_ref[rows, :] = base_ref[rows, :] + feed
        return ()

    each_sample(middle_ref.shape[0], UNROLL["mlp_fwd"], step)


def mlp_bwd_block(gf, kept, wm):
    ghs = [nt(gf, wm[m, 256:512, :]) for m in range(4)]
    gps = [(gh * slope.astype(F32)).astype(BF) for gh, (_, slope) in zip(ghs, kept)]
    gn = [nt(gps[m], wm[m, 0:256, :]) for m in range(4)]
    return gps, (gn[0] + gn[1]) + (gn[2] + gn[3])


def put_mlp_grads(hid, gp, n2, gf, keep_ref, send_ref):
    for m in range(4):
        columns = slice(m * 256, (m + 1) * 256)
        up = tn(n2[...], gp[:, columns]).astype(BF)
        down = tn(hid[:, columns], gf[...]).astype(BF)
        own_up = half_index() == 0
        keep_ref[m] = jnp.where(own_up, up, down)
        send_ref[m] = jnp.where(own_up, down, up)


def mlp_both_kernel(layer, count, *refs):
    pieces = refs[:count]
    (middle_ref, base_ref, cot_ref, gain_ref, out_ref, gm_ref, keep_ref, send_ref, small_ref, wm, hid_all, gp_all,
     n2_all) = refs[count:]
    place_mlp(layer, pieces, wm)
    gain = gain_ref[layer:layer + 1, :]
    def step(rows, gain_grad):
        middle = middle_ref[rows, :]
        r, n2, kept, feed = mlp_fwd_block(middle, gain, wm)
        out_ref[rows, :] = base_ref[rows, :] + feed
        gf = cot_ref[rows, :]
        gps, gn = mlp_bwd_block(gf, kept, wm)
        n2_all[rows, :] = n2
        for m in range(4):
            hid_all[rows, m * 256:(m + 1) * 256] = kept[m][0]
            gp_all[rows, m * 256:(m + 1) * 256] = gps[m]
        back, part = norm_back(middle, r, gain, gn)
        gain_grad = gain_grad + part
        gm_ref[rows, :] = gf.astype(F32) + back
        return (gain_grad, )

    gain_grad, = each_sample(middle_ref.shape[0], UNROLL["mlp_both"], step, jnp.zeros((1, 256), F32))
    small_ref[...] = jnp.broadcast_to(gain_grad, small_ref.shape)
    put_mlp_grads(hid_all, gp_all, n2_all, cot_ref, keep_ref, send_ref)


def mlp_bwd_kernel(layer, count, *refs):
    pieces = refs[:count]
    (grad_ref, middle_ref, hid_ref, slope_ref, gain_ref, gm_ref, keep_ref, send_ref, small_ref, wm, gp_all, n2_all,
     gf_all) = refs[count:]
    place_mlp(layer, pieces, wm)
    gain = gain_ref[layer:layer + 1, :]
    def step(rows, gain_grad):
        middle = middle_ref[rows, :]
        r = rescale_of(middle)
        n2_all[rows, :] = (middle * r * gain).astype(BF)
        grad = grad_ref[rows, :]
        gf = grad.astype(BF)
        gf_all[rows, :] = gf
        kept = [(None, slope_ref[rows, m * 256:(m + 1) * 256]) for m in range(4)]
        gps, gn = mlp_bwd_block(gf, kept, wm)
        for m in range(4):
            gp_all[rows, m * 256:(m + 1) * 256] = gps[m]
        back, part = norm_back(middle, r, gain, gn)
        gain_grad = gain_grad + part
        gm_ref[rows, :] = grad + back
        return (gain_grad, )

    gain_grad, = each_sample(middle_ref.shape[0], UNROLL["mlp_bwd"], step, jnp.zeros((1, 256), F32))
    small_ref[...] = jnp.broadcast_to(gain_grad, small_ref.shape)
    put_mlp_grads(hid_ref, gp_all, n2_all, gf_all, keep_ref, send_ref)


def attn_pre_kernel(layer, count, *refs):
    pieces = refs[:count]
    (grad_ref, gm_ref, cur_ref, nrm_ref, mix_ref, gmix_ref, d_cross_ref, d_out_ref, base_ref, gn_ref, small_ref,
     dot_ref, wa, w_cross, w_out, ga_all, gc_all) = refs[count:]
    bias = place_attn(layer, pieces, wa, w_cross, w_out)

    def step(rows, bias_grad):
        grad = grad_ref[rows, :].astype(F32)
        gm = gm_ref[rows, :]
        ga = gm.astype(BF)
        ga_all[rows, :] = ga
        gc = (grad * cur_ref[rows, :].astype(F32)).astype(BF)
        gc_all[rows, :] = gc
        gmix = nt(w_out[...], ga).astype(BF)
        gmix_ref[:, rows] = gmix
        for m in range(4):
            head = slice(m * HD, (m + 1) * HD)
            product = gmix[head].astype(F32) * mix_ref[head, rows].astype(F32)
            dot_ref[m:m + 1, rows] = jnp.sum(product, axis=0, keepdims=True)
        gn_ref[rows, :] = nn(gc, w_cross[...])
        base_ref[rows, :] = gm + grad * (nt(nrm_ref[rows, :], w_cross[...]) + bias)
        return (bias_grad + jnp.sum(gc.astype(F32), axis=0, keepdims=True), )

    bias_grad, = each_sample(cur_ref.shape[0], UNROLL["attn_pre"], step, jnp.zeros((1, 256), F32))
    d_cross = tn(gc_all[...], nrm_ref[...])
    d_cross_ref[...] = d_cross.astype(BF)
    d_out_ref[...] = nn(mix_ref[...], ga_all[...]).astype(BF)
    small_ref[0:1, :] = bias_grad
    small_ref[1:2, :] = jnp.sum(d_cross * w_cross[...].astype(F32), axis=0, keepdims=True)


def qkv_back(rows, mask_ref, qkv_ref, lse_ref, gmix_ref, dot_ref):
    mask = mask_rows(mask_ref, rows)
    parts = []
    for m in range(4):
        q, k, v = (qkv_ref[m * 192 + i * HD:m * 192 + (i + 1) * HD, rows] for i in range(3))
        parts.append((q, k, v, gmix_ref[m * HD:(m + 1) * HD, rows]))
    scores = [slot_scores(q, k, mask) for q, k, v, go in parts]
    gps = [tn(v, go) for q, k, v, go in parts]
    ps, gss = [], []
    for m in range(4):
        p = jnp.exp(scores[m] - lse_ref[m:m + 1, rows])
        ps.append(p.astype(BF))
        gss.append((p * (gps[m] - dot_ref[m:m + 1, rows])).astype(BF))
    return [
        jnp.concatenate([nn(k, gs) * 0.125, nt(q, gs) * 0.125, nt(go, p)], axis=0).astype(BF)
        for (q, k, v, go), p, gs in zip(parts, ps, gss)
    ]


def norm_grad(cur, gain, gn):
    r = rescale_of(cur)
    scaled = gn * gain
    return r * (scaled - cur * (r * r * jnp.mean(cur * scaled, axis=-1, keepdims=True)))


def put_attn_grads(layer, nrm, gqkv_all, wa, gain_ref, d_cross_ref, d_out_ref, small, mlp_small, payload, keep_ref, sends):
    gain_grad = small[1:2, :]
    for m in range(4):
        place = pl.multiple_of((head_index() ^ m) * HD, HD)
        d_qkv = nn(gqkv_all[m * 192:(m + 1) * 192, :], nrm)
        gain_grad = gain_grad + jnp.sum(d_qkv * wa[m, 0:192, :].astype(F32), axis=0, keepdims=True)
        payload[m, 0:192, :] = d_qkv.astype(BF)
        payload[m, 192:256, :] = d_cross_ref[pl.ds(place, HD), :]
        payload[m, 256:320, :] = d_out_ref[m * HD:(m + 1) * HD, :]
    gain_grad = gain_grad / gain_ref[layer:layer + 1, :]
    high, low = split_rows(jnp.concatenate([gain_grad, small[0:1, :], mlp_small[0:1, :], jnp.zeros((5, 256), F32)], axis=0))
    keep = pl.multiple_of(half_index() * 160, 16)
    other = pl.multiple_of((1 - half_index()) * 160, 16)
    for m in range(4):
        each = 4 // len(sends)
        for ref, i, at in ((keep_ref, m, keep), (sends[m // each], m % each, other)):
            ref[i, 0:160, :] = payload[m, pl.ds(at, 160), :]
            ref[i, 160:168, :] = high
            ref[i, 168:176, :] = low


def attn_bwd_kernel(layer, count, *refs):
    pieces = refs[:count]
    (mask_ref, nrm_ref, qkv_ref, lse_ref, gain_ref, gmix_ref, d_cross_ref, d_out_ref, small, dot_ref, mlp_small,
     cur_ref, base_ref, gn_ref, out_ref, keep_ref, send_ref, wa, gqkv_all, payload) = refs[count:]
    place_qkv(layer, pieces, wa)

    def step(rows):
        gn = gn_ref[rows, :]
        for m, gqkv in enumerate(qkv_back(rows, mask_ref, qkv_ref, lse_ref, gmix_ref, dot_ref)):
            gqkv_all[m * 192:(m + 1) * 192, rows] = gqkv
            gn = gn + tn(gqkv, wa[m, 0:192, :])
        out_ref[rows, :] = base_ref[rows, :] + norm_grad(cur_ref[rows, :].astype(F32), gain_ref[layer:layer + 1, :], gn)
        return ()

    each_sample(nrm_ref.shape[0], UNROLL["attn_bwd"], step)
    put_attn_grads(layer, nrm_ref[...], gqkv_all, wa, gain_ref, d_cross_ref, d_out_ref, small, mlp_small,
                   payload, keep_ref, (send_ref,))


def attn_grads_kernel(layer, count, *refs):
    pieces = refs[:count]
    (mask_ref, nrm_ref, qkv_ref, lse_ref, gain_ref, gmix_ref, d_cross_ref, d_out_ref, small, dot_ref, mlp_small,
     gqkv_all, keep_ref, send_low, send_high, wa, payload) = refs[count:]
    place_qkv(layer, pieces, wa)

    def step(rows):
        for m, gqkv in enumerate(qkv_back(rows, mask_ref, qkv_ref, lse_ref, gmix_ref, dot_ref)):
            gqkv_all[m * 192:(m + 1) * 192, rows] = gqkv
        return ()

    each_sample(nrm_ref.shape[0], UNROLL["attn_bwd"], step)
    put_attn_grads(layer, nrm_ref[...], gqkv_all, wa, gain_ref, d_cross_ref, d_out_ref, small, mlp_small,
                   payload, keep_ref, (send_low, send_high))


def attn_post_kernel(layer, count, *refs):
    pieces = refs[:count]
    (gqkv_all, gain_ref, cur_ref, base_ref, gn_ref, out_ref, wa) = refs[count:]
    place_qkv(layer, pieces, wa)

    def step(rows):
        gn = gn_ref[rows, :]
        for m in range(4):
            gn = gn + tn(gqkv_all[m * 192:(m + 1) * 192, rows], wa[m, 0:192, :])
        out_ref[rows, :] = base_ref[rows, :] + norm_grad(cur_ref[rows, :].astype(F32), gain_ref[layer:layer + 1, :], gn)
        return ()

    each_sample(cur_ref.shape[0], UNROLL["attn_post"], step)


def split_rows(x):
    high = x.astype(BF)
    return high, (x - high.astype(F32)).astype(BF)


def pack_kernel(lens, qkv, cross, out, up, down, b, own0, own1, first_l0, half_l1, mask, sems):
    copies = []
    for l, own in ((0, own0), (1, own1)):
        for t in range(3):
            copies.append(pltpu.make_async_copy(qkv.at[l, t], own.at[pl.ds(t * HD, HD)], sems.at[0]))
        copies.append(pltpu.make_async_copy(cross.at[l], own.at[pl.ds(192, HD)], sems.at[0]))
        copies.append(pltpu.make_async_copy(out.at[l], own.at[pl.ds(256, HD)], sems.at[0]))
    for copy in copies:
        copy.start()

    x = pl.multiple_of(quarter_index() * 128, 16)

    def mlp_parts(weight):
        return (pltpu.make_async_copy(weight.at[0, pl.ds(x, 128)], first_l0.at[pl.ds(176, 128)], sems.at[1]),
                pltpu.make_async_copy(weight.at[1], half_l1.at[pl.ds(0, 256)], sems.at[1]))

    @pl.when(half_index() == 0)
    def _():
        for copy in mlp_parts(up):
            copy.start()

    @pl.when(half_index() != 0)
    def _():
        for copy in mlp_parts(down):
            copy.start()

    slots = lax.broadcasted_iota(jnp.int32, (16, 256), 1)
    first = lax.broadcasted_iota(jnp.int32, (16, 256), 0) == 0
    samples = mask.shape[0] // 16
    for i in range(samples):
        length = lens[head_index() * samples + i]
        mask[i * 16:(i + 1) * 16, :] = jnp.where(jnp.logical_and(first, slots >= length), MASKED_SCORE, 0.0).astype(BF)
    lane = lax.broadcasted_iota(jnp.int32, (LAYERS, 256), 1) // HD
    wide = jnp.concatenate([b[...].astype(F32)] * 4, axis=1)
    wide = jnp.where(lane == head_index(), wide, 0.0)
    for l, own in ((0, own0), (1, own1)):
        own[320:352, :] = jnp.broadcast_to(wide[l:l + 1], (32, 256)).astype(BF)
    for copy in copies:
        copy.wait()
    at = pl.multiple_of(half_index() * 176, 16)
    first_l0[0:176, :] = own0[pl.ds(at, 176), :]
    half_l1[256:432, :] = own1[pl.ds(at, 176), :]
    for copy in mlp_parts(up):
        copy.wait()


def stack_kernel(a, b, c, attn, mlp):
    for m, ref in enumerate((a, b, c)):
        attn[m * 176:(m + 1) * 176, :] = ref[0:176, :]
        mlp[m * 128:(m + 1) * 128, :] = ref[176:304, :]


def put_sum(out, at, small_at, rows, total):
    for low, high in ((0, small_at), (small_at + 16, rows)):
        if low < high:
            out[at + low:at + high, :] = total(low, high).astype(BF)
    if small_at < rows:
        both = total(small_at, small_at + 16)
        high, low = split_rows(both[0:8] + both[8:16])
        out[at + small_at:at + small_at + 8, :] = high
        out[at + small_at + 8:at + small_at + 16, :] = low


def core_sum_kernel(small_at, *refs):
    ins, outs = refs[:-4], refs[-4:]
    for m, out in enumerate(outs):
        at = 0
        rest = list(ins)
        for where in small_at:
            keep = rest.pop(0)
            if where is None:
                out[at:at + keep.shape[1], :] = keep[m]
                at += keep.shape[1]
                continue
            got, index = rest.pop(0), m
            if got.shape[0] < keep.shape[0]:
                got, index = (got, rest.pop(0))[m // 2], m % 2
            rows = keep.shape[1]
            put_sum(out, at, where, rows, lambda i, j: keep[m, i:j].astype(F32) + got[index, i:j].astype(F32))
            at += rows


def core_split_kernel(keep, got, keep_out, send_out):
    at = pl.multiple_of(quarter_index() * 128, 16)
    other = pl.multiple_of((1 - quarter_index()) * 128, 16)
    for out, rows in ((keep_out, pl.ds(at, 128)), (send_out, pl.ds(other, 128))):
        for m in range(4):
            out[m] = (keep[m, rows, :].astype(F32) + got[m, rows, :].astype(F32)).astype(BF)


def add_kernel(a, b, out):
    out[...] = (a[...].astype(F32) + b[...].astype(F32)).astype(BF)


def four_sum_kernel(small_at, *refs):
    s, a, b, c, out = refs
    put_sum(out, 0, small_at, s.shape[0],
            lambda i, j: (s[i:j].astype(F32) + a[i:j].astype(F32)) + (b[i:j].astype(F32) + c[i:j].astype(F32)))


def early_sum_kernel(one, s, a, b, c, low, high):
    total = (s[...].astype(F32) + a[...].astype(F32)) + (b[...].astype(F32) + c[...].astype(F32))
    low[0:176, :] = one[128:304, :]
    low[176:176 + CUT, :] = total[0:CUT].astype(BF)
    high[0:256 - CUT, :] = total[CUT:256].astype(BF)
    high[256 - CUT:384 - CUT, :] = one[0:128, :]


def pair_sum_kernel(low, low_got, high, high_got, low_out, high_out):
    put_sum(low_out, 0, 160, low.shape[0], lambda i, j: low[i:j].astype(F32) + low_got[i:j].astype(F32))
    high_out[...] = (high[...].astype(F32) + high_got[...].astype(F32)).astype(BF)


def last_pair_kernel(low, low_got, high, high_got, low_out, high_out):
    put_sum(low_out, 0, 160, low.shape[0], lambda i, j: low[i:j].astype(F32) + low_got[i:j].astype(F32))
    rows = 256 - CUT
    high_out[0:rows, :] = (high[0:rows].astype(F32) + high_got[0:rows].astype(F32)).astype(BF)
    high_out[rows:rows + 128, :] = high[rows:rows + 128]
    high_out[rows + 128:rows + 256, :] = high_got[rows:rows + 128]


def finish_kernel(low, low_other, high, high_other, late, late_other,
                  d_qkv, d_out, d_up, d_down, d_cross, gain_attn, gain_mlp, bias):
    rows = 256 - CUT
    mine = pl.multiple_of(quarter_index() * 128, 16)
    other = pl.multiple_of((1 - quarter_index()) * 128, 16)

    def place(first, second):
        for l, a, b in ((1, first[0], second[0]), (0, first[2], second[2])):
            d_qkv[l, 0] = a[0:64].astype(F32)
            d_qkv[l, 1] = a[64:128].astype(F32)
            d_qkv[l, 2, 0:32] = a[128:160].astype(F32)
            d_qkv[l, 2, 32:64] = b[0:32].astype(F32)
            d_cross[l] = b[32:96].astype(F32)
            d_out[l] = b[96:160].astype(F32)
        for dst, (lo, hi, _) in ((d_up, first), (d_down, second)):
            dst[0, 0:CUT] = lo[176:176 + CUT].astype(F32)
            dst[0, CUT:256] = hi[0:rows].astype(F32)
            dst[1, pl.ds(mine, 128)] = hi[rows:rows + 128].astype(F32)
            dst[1, pl.ds(other, 128)] = hi[rows + 128:rows + 256].astype(F32)

    @pl.when(half_index() == 0)
    def _():
        place((low, high, late), (low_other, high_other, late_other))

    @pl.when(half_index() != 0)
    def _():
        place((low_other, high_other, late_other), (low, high, late))

    for l, ref in ((0, late), (1, low)):
        small = ref[160:168].astype(F32) + ref[168:176].astype(F32)
        gain_attn[l:l + 1, :] = small[0:1]
        gain_mlp[l:l + 1, :] = small[2:3]
        total = jnp.zeros((1, HD), F32)
        for h in range(4):
            total = total + jnp.where(head_index() == h, small[1:2, h * HD:(h + 1) * HD], 0.0)
        bias[l:l + 1, :] = total


SMEM = pl.BlockSpec(memory_space=pltpu.SMEM)
ANY = pl.BlockSpec(memory_space=pl.ANY)


def call(kernel, outs, scratch, name, *args, flops=KERNEL_FLOPS):
    return pl.pallas_call(
        kernel,
        in_specs=[VMEM] * len(args),
        out_specs=[VMEM] * len(outs),
        out_shape=[jax.ShapeDtypeStruct(shape, dtype) for shape, dtype in outs],
        scratch_shapes=[pltpu.VMEM(shape, dtype) for shape, dtype in scratch],
        compiler_params=pltpu.CompilerParams(vmem_limit_bytes=VMEM_LIMIT),
        cost_estimate=pl.CostEstimate(flops=flops, bytes_accessed=1024, transcendentals=0),
        name=name,
    )(*args)


ATTN_SCRATCH = [((4, 352, 256), BF), ((256, 256), BF), ((256, 256), BF)]
MLP_GRADS = [((4, 256, 256), BF), ((4, 256, 256), BF), ((8, 256), F32)]


def attn_fwd(layer, cur, mask, gain, pieces):
    rows = cur.shape[0]
    outs = [((rows, 256), F32), ((rows, 256), F32), ((rows, 256), BF), ((768, rows), BF), ((256, rows), BF), ((8, rows), F32)]
    return call(functools.partial(attn_fwd_kernel, layer, len(pieces)), outs, ATTN_SCRATCH, "attn_fwd", *pieces, cur, mask, gain,
                flops=(LONG, KERNEL_FLOPS)[layer])


def mlp_fwd(layer, middle, base, gain, pieces):
    rows = middle.shape[0]
    outs = [((rows, 256), F32), ((rows, 1024), BF), ((rows, 1024), BF)]
    return call(functools.partial(mlp_fwd_kernel, layer, len(pieces)), outs, [((4, 512, 256), BF)], "mlp_fwd", *pieces,
                middle, base, gain)


def mlp_both(layer, middle, base, cot, gain, pieces):
    rows = middle.shape[0]
    outs = [((rows, 256), F32), ((rows, 256), F32)] + MLP_GRADS
    scratch = [((4, 512, 256), BF), ((rows, 1024), BF), ((rows, 1024), BF), ((rows, 256), BF)]
    return call(functools.partial(mlp_both_kernel, layer, len(pieces)), outs, scratch, "mlp_both", *pieces, middle, base, cot, gain)


def mlp_bwd(layer, grad, middle, hid, slope, gain, pieces):
    rows = middle.shape[0]
    outs = [((rows, 256), F32)] + MLP_GRADS
    scratch = [((4, 512, 256), BF), ((rows, 1024), BF), ((rows, 256), BF), ((rows, 256), BF)]
    return call(functools.partial(mlp_bwd_kernel, layer, len(pieces)), outs, scratch, "mlp_bwd", *pieces,
                grad, middle, hid, slope, gain)


def attn_pre(layer, grad, gm, cur, saved, pieces):
    rows = cur.shape[0]
    nrm, _, mix, _ = saved
    outs = [((256, rows), BF), ((256, 256), BF), ((256, 256), BF), ((rows, 256), F32), ((rows, 256), F32), ((8, 256), F32), ((8, rows), F32)]
    scratch = ATTN_SCRATCH + [((rows, 256), BF), ((rows, 256), BF)]
    return call(functools.partial(attn_pre_kernel, layer, len(pieces)), outs, scratch, "attn_pre", *pieces, grad, gm, cur, nrm, mix)


PAYLOAD = [((4, 176, 256), BF), ((4, 176, 256), BF)]


def attn_bwd(layer, cur, mask, saved, gain, pre, mlp_small, pieces):
    rows = cur.shape[0]
    nrm, qkv, _, lse = saved
    gmix, d_cross, d_out, base, gn, small, dot = pre
    scratch = [((4, 352, 256), BF), ((768, rows), BF), ((4, 320, 256), BF)]
    return call(functools.partial(attn_bwd_kernel, layer, len(pieces)), [((rows, 256), F32)] + PAYLOAD, scratch, "attn_bwd", *pieces,
                mask, nrm, qkv, lse, gain, gmix, d_cross, d_out, small, dot, mlp_small, cur, base, gn)


def attn_grads(layer, mask, saved, gain, pre, mlp_small, pieces):
    nrm, qkv, _, lse = saved
    gmix, d_cross, d_out, _, _, small, dot = pre
    scratch = [((4, 352, 256), BF), ((4, 320, 256), BF)]
    return call(functools.partial(attn_grads_kernel, layer, len(pieces)), [((768, nrm.shape[0]), BF), ((4, 176, 256), BF), ((2, 176, 256), BF), ((2, 176, 256), BF)], scratch, "attn_grads", *pieces,
                mask, nrm, qkv, lse, gain, gmix, d_cross, d_out, small, dot, mlp_small)


def attn_post(layer, gqkv, gain, cur, pre, pieces):
    return call(functools.partial(attn_post_kernel, layer, len(pieces)), [((cur.shape[0], 256), F32)], [((4, 352, 256), BF)], "attn_post", *pieces,
                gqkv, gain, cur, pre[3], pre[4])[0]


VMEM = pl.BlockSpec(memory_space=pltpu.VMEM)


def small_call(kernel, shapes, name, flops=1000):
    def run(*args):
        return pl.pallas_call(
            kernel,
            in_specs=[VMEM] * len(args),
            out_specs=[VMEM] * len(shapes),
            out_shape=[jax.ShapeDtypeStruct(shape, dtype) for shape, dtype in shapes],
            compiler_params=pltpu.CompilerParams(vmem_limit_bytes=SMALL_LIMIT),
            cost_estimate=pl.CostEstimate(flops=flops, bytes_accessed=1024, transcendentals=0),
            name=name,
        )(*args)
    return run


def core_sum(small_at, *groups):
    rows = sum(group[0].shape[1] for group in groups)
    return small_call(functools.partial(core_sum_kernel, small_at), [((rows, 256), BF)] * 4, "core_sum")(
        *[x for group in groups for x in group])


def four_sum(small_at, terms, flops=1000):
    return small_call(functools.partial(four_sum_kernel, small_at), [(terms[0].shape, BF)], "four_sum", flops)(*terms)[0]


def swap(x, axis, size, mask):
    return lax.ppermute(x, axis, [(i, i ^ mask) for i in range(size)])


def tie(x, *before):
    return lax.optimization_barrier((x,) + before)[0]


def solution(mesh):
    dp_size, head_size = mesh.shape["dp"], mesh.shape["head"]

    def core_swap(x):
        return swap(x, "dp", dp_size, 1)

    def fetch(x):
        return [swap(x, "head", head_size, m) for m in range(1, head_size)]

    def scatter(sums):
        return [sums[0]] + [swap(sums[m], "head", head_size, m) for m in range(1, head_size)]

    bits = [1 << i for i in range(1, dp_size.bit_length() - 1)]

    def late_steps():
        return [(bits[i], bits[i + 1], bits[i] + bits[i + 1]) if i + 1 < len(bits) else (bits[i],) for i in range(0, len(bits), 2)]

    def sum_early_late(low, high, late):
        pairs = list(zip(bits, bits[1:] + bits[:1]))

        def pair(low, high, masks, before, last):
            got = [tie(swap(x, "dp", dp_size, mask), *before) for x, mask in zip((low, high), masks)]
            kernel, more = (last_pair_kernel, 128) if last else (pair_sum_kernel, 0)
            return small_call(kernel, [(low.shape, BF), ((high.shape[0] + more, 256), BF)], "pair_sum")(low, got[0], high, got[1])

        late = four_sum(160, late, LONG)
        low, high = pair(low, high, pairs[0], [late], len(pairs) == 1)
        for masks in late_steps():
            terms = [late] + [swap(late, "dp", dp_size, mask) for mask in masks]
            before = terms[1:]
            late = four_sum(160, terms + [jnp.zeros_like(late)] * (4 - len(terms)))
        for i, masks in enumerate(pairs[1:]):
            low, high = pair(low, high, masks, before, i == len(pairs) - 2)
        return low, high, late

    def body(tokens, lengths, cotangent, gain_attn, gain_mlp, w_qkv, w_out, w_up, w_down, w_cross, b_cross):
        rows = tokens.shape[0]
        own0, own1, first_l0, half_l1, mask = pl.pallas_call(
            pack_kernel,
            in_specs=[SMEM] + [ANY] * 5 + [VMEM],
            out_specs=[VMEM] * 5,
            out_shape=[jax.ShapeDtypeStruct((n, 256), BF) for n in (352, 352, 304, 432)]
            + [jax.ShapeDtypeStruct((rows // 16, 256), BF)],
            scratch_shapes=[pltpu.SemaphoreType.DMA((2,))],
            name="pack",
        )(lengths, w_qkv.transpose(0, 2, 3, 1), w_cross.transpose(0, 2, 1), w_out, w_up, w_down, b_cross)

        l1 = fetch(half_l1)
        a0, m0 = small_call(stack_kernel, [((528, 256), BF), ((384, 256), BF)], "stack")(*fetch(first_l0))
        a0 = [own0, a0, core_swap(a0)]
        mid0, base0, *saved0 = attn_fwd(0, tokens, mask, gain_attn, a0)
        m0 = [m0, tie(swap(m0, "dp", dp_size, 2), mid0)]
        m0 = [w_up, w_down] + m0 + [core_swap(x) for x in m0]
        cur1, hid0, slope0 = mlp_fwd(0, mid0, base0, gain_mlp, m0)
        l1 = [tie(x, cur1) for x in l1]
        l1 = l1 + [core_swap(x) for x in l1]
        a1, m1 = [own1] + l1, [w_up, w_down] + l1
        mid1, base1, *saved1 = attn_fwd(1, cur1, mask, gain_attn, a1)
        output, gm1, keep_m1, send_m1, small_m1 = mlp_both(1, mid1, base1, cotangent, gain_mlp, m1)
        pre = attn_pre(1, cotangent, gm1, cur1, saved1, a1)
        pre_done = pre[0]
        keep_m1, send_m1 = small_call(core_split_kernel, [((4, 128, 256), BF)] * 2, "core_split")(
            keep_m1, tie(core_swap(send_m1), pre_done))
        got_m1 = swap(send_m1, "dp", dp_size, 2)
        grad1, keep_a1, send_a1 = attn_bwd(1, cur1, tie(mask, send_m1), saved1, gain_attn, pre, small_m1, a1)
        m1_sum = small_call(add_kernel, [((4, 128, 256), BF)], "add", LONG)(keep_m1, tie(got_m1, grad1))[0]
        sums = core_sum((None, 160), (m1_sum,), (keep_a1, tie(core_swap(send_a1), m1_sum)))
        got = scatter(sums)
        gm0, keep_m0, send_m0, small_m0 = mlp_bwd(0, tie(grad1, *sums), mid0, hid0, slope0, gain_mlp, m0)
        pre = attn_pre(0, grad1, gm0, tokens, saved0, a0)
        gqkv, keep_a0, *send_a0 = attn_grads(0, mask, saved0, gain_attn, pre, small_m0, a0)
        one = four_sum(288, [tie(x, gqkv) for x in got], LONG)
        sums = core_sum((256,), (keep_m0, tie(core_swap(send_m0), one)))
        got = scatter(sums)
        grad0 = attn_post(0, tie(gqkv, *sums), gain_attn, tokens, pre, a0)
        low, high = small_call(early_sum_kernel, [((176 + CUT, 256), BF), ((384 - CUT, 256), BF)], "early_sum")(
            one, *[tie(x, grad0) for x in got])
        sums_a0 = core_sum((160,), (keep_a0, *[core_swap(x) for x in send_a0]))
        late = scatter(sums_a0)
        low, high, late = sum_early_late(low, high, late)
        d_qkv, d_out, d_up, d_down, d_cross, d_ga, d_gm, d_bias = small_call(
            finish_kernel,
            [((LAYERS, 3, HD, 256), F32), ((LAYERS, HD, 256), F32), ((LAYERS, 256, 256), F32), ((LAYERS, 256, 256), F32),
             ((LAYERS, HD, 256), F32), ((LAYERS, 256), F32), ((LAYERS, 256), F32), ((LAYERS, HD), F32)],
            "finish",
        )(low, core_swap(low), high, core_swap(high), late, core_swap(late))
        return (output, grad0, d_ga, d_gm, d_qkv.transpose(0, 3, 1, 2), d_out, d_up, d_down,
                d_cross.transpose(0, 2, 1), d_bias)

    rows, weights = P(("dp", "head"), None), P(None, "head", None)
    return jax.shard_map(
        body,
        mesh=mesh,
        in_specs=(rows, P("dp"), rows, P(), P(), P(None, None, None, "head"), weights, P(None, None, "head"),
                  weights, P(None, None, "head"), P(None, "head")),
        out_specs=(rows, rows, P(), P(), P(None, None, None, "head"), weights, P(None, None, "head"),
                   weights, P(None, None, "head"), P(None, "head")),
        check_vma=False,
    )
```

```python
import functools

import jax
import jax.numpy as jnp
from jax import lax
from jax.experimental import pallas as pl
from jax.experimental.pallas import tpu as pltpu
from jax.sharding import PartitionSpec as P

HD = 64
LAYERS = 2
EPSILON = 1e-06
MASKED_SCORE = -1000000000.0
BF = jnp.bfloat16
F32 = jnp.float32

VMEM_LIMIT = 32 * 2**20
SMALL_LIMIT = 12 * 2**20
UNROLL = {"attn_fwd": 4, "mlp_fwd": 4, "mlp_both": 4, "mlp_bwd": 4, "attn_bwd": 2, "attn_pre": 2, "attn_post": 2}
KERNEL_FLOPS = 1000
LONG = 50 * 10**9


def nn(a, b):
    return lax.dot_general(a, b, (((1,), (0,)), ((), ())), preferred_element_type=F32)


def nt(a, b):
    return lax.dot_general(a, b, (((1,), (1,)), ((), ())), preferred_element_type=F32)


def tn(a, b):
    return lax.dot_general(a, b, (((0,), (0,)), ((), ())), preferred_element_type=F32)


def rescale_of(values):
    return lax.rsqrt(jnp.mean(values * values, axis=-1, keepdims=True) + EPSILON)


def norm_back(values, rescale, gain, gradient):
    scaled = gradient * gain
    product_mean = jnp.mean(values * scaled, axis=-1, keepdims=True)
    normal = values * rescale
    grad_values = rescale * (scaled - normal * (rescale * product_mean))
    return grad_values, jnp.sum(gradient * normal, axis=0, keepdims=True)


def gelu_and_slope(u):
    cdf = 0.5 + 0.5 * lax.erf(u * 0.7071067811865476)
    density = jnp.exp2((-0.5 * 1.4426950408889634) * (u * u))
    return u * cdf, cdf + u * (density * 0.3989422804014327)


def slot_scores(q, k, mask):
    ones = jnp.where(lax.broadcasted_iota(jnp.int32, mask.shape, 0) == 0, 1.0, 0.0).astype(BF)
    return tn(jnp.concatenate([k, mask], axis=0), jnp.concatenate([q * BF(0.125), ones], axis=0))


def mask_rows(mask_ref, rows):
    return mask_ref[pl.ds(pl.multiple_of(rows.start // 16, 16), 16), :]


def head_index():
    return lax.axis_index("head")


def half_index():
    return lax.axis_index("dp") & 1


def quarter_index():
    return (lax.axis_index("dp") >> 1) & 1


def place_pieces(own, parts, dst, first, rows):
    at = 0
    for ref in own:
        dst[0, at:at + ref.shape[0], :] = ref
        at += ref.shape[0]
    for start, refs in parts:
        for m, ref in enumerate(refs):
            dst[m + 1, pl.ds(pl.multiple_of(start, 16), rows), :] = ref[first:first + rows, :]


def parts_of(pieces, rows):
    c, x = half_index(), quarter_index()
    if len(pieces) == 6:
        return [(c * rows, pieces[0:3]), ((1 - c) * rows, pieces[3:6])]
    places = [c, 1 - c] if len(pieces) == 2 else [2 * i + j for i, j in ((c, x), (c, 1 - x), (1 - c, x), (1 - c, 1 - x))]
    return [(place * rows, [ref.at[pl.ds(m * rows, rows)] for m in range(3)]) for place, ref in zip(places, pieces)]


def place_qkv(layer, pieces, wa):
    place_pieces((pieces[0][...],), parts_of(pieces[1:], 176), wa, 256 * layer, 176)


def place_attn(layer, pieces, wa, w_cross, w_out):
    place_qkv(layer, pieces, wa)
    total = jnp.zeros((1, 256), F32)
    for m in range(4):
        place = pl.multiple_of((head_index() ^ m) * HD, HD)
        w_cross[pl.ds(place, HD), :] = wa[m, 192:256, :]
        w_out[m * HD:(m + 1) * HD, :] = wa[m, 256:320, :]
        total = total + wa[m, 320:336, :].astype(F32)[0:1, :]
    return total


def place_mlp(layer, pieces, wm):
    rows = 256 if len(pieces) == 8 else 128
    place_pieces((pieces[0][layer], pieces[1][layer]), parts_of(pieces[2:], rows), wm, 0, rows)


def each_sample(rows, unroll, step, *init, size=256):
    def body(i, carried):
        return step(pl.ds(pl.multiple_of(i * size, size), size), *carried)

    return lax.fori_loop(0, rows // size, body, init, unroll=unroll)


def attn_fwd_kernel(layer, count, *refs):
    pieces = refs[:count]
    (cur_ref, mask_ref, gain_ref, middle_ref, base_ref, nrm_ref, qkv_ref, mix_ref, lse_ref, wa, w_cross, w_out) = refs[count:]
    bias = place_attn(layer, pieces, wa, w_cross, w_out)
    gain = gain_ref[layer:layer + 1, :]
    def step(rows):
        cur = cur_ref[rows, :].astype(F32)
        nrm = (cur * rescale_of(cur) * gain).astype(BF)
        nrm_ref[rows, :] = nrm
        mask = mask_rows(mask_ref, rows)
        qkv = [nt(wa[m, 0:192, :], nrm).astype(BF) for m in range(4)]
        scores = [slot_scores(qkv[m][0:64], qkv[m][64:128], mask) for m in range(4)]
        cross = nt(nrm, w_cross[...]) + bias
        probs = []
        for m in range(4):
            qkv_ref[m * 192:(m + 1) * 192, rows] = qkv[m]
            top = jnp.max(scores[m], axis=0, keepdims=True)
            e = jnp.exp(scores[m] - top)
            total = jnp.sum(e, axis=0, keepdims=True)
            probs.append((e * (1.0 / total)).astype(BF))
            lse_ref[m:m + 1, rows] = top + jnp.log(total)
        mix = jnp.concatenate([nn(qkv[m][128:192], probs[m]).astype(BF) for m in range(4)], axis=0)
        mix_ref[:, rows] = mix
        middle = cur + tn(mix, w_out[...])
        middle_ref[rows, :] = middle
        base_ref[rows, :] = middle + cur * cross
        return ()

    each_sample(cur_ref.shape[0], UNROLL["attn_fwd"], step)


def mlp_fwd_block(middle, gain, wm):
    r = rescale_of(middle)
    n2 = (middle * r * gain).astype(BF)
    us = [nn(n2, wm[m, 0:256, :]) for m in range(4)]
    kept = []
    for u in us:
        hid, slope = gelu_and_slope(u)
        kept.append((hid.astype(BF), slope.astype(BF)))
    feed = [nn(kept[m][0], wm[m, 256:512, :]) for m in range(4)]
    return r, n2, kept, (feed[0] + feed[1]) + (feed[2] + feed[3])


def mlp_fwd_kernel(layer, count, *refs):
    pieces = refs[:count]
    (middle_ref, base_ref, gain_ref, out_ref, hid_ref, slope_ref, wm) = refs[count:]
    place_mlp(layer, pieces, wm)
    gain = gain_ref[layer:layer + 1, :]
    def step(rows):
        _, _, kept, feed = mlp_fwd_block(middle_ref[rows, :], gain, wm)
        for m, (hid, slope) in enumerate(kept):
            hid_ref[rows, m * 256:(m + 1) * 256] = hid
            slope_ref[rows, m * 256:(m + 1) * 256] = slope
        out_ref[rows, :] = base_ref[rows, :] + feed
        return ()

    each_sample(middle_ref.shape[0], UNROLL["mlp_fwd"], step)


def mlp_bwd_block(gf, kept, wm):
    ghs = [nt(gf, wm[m, 256:512, :]) for m in range(4)]
    gps = [(gh * slope.astype(F32)).astype(BF) for gh, (_, slope) in zip(ghs, kept)]
    gn = [nt(gps[m], wm[m, 0:256, :]) for m in range(4)]
    return gps, (gn[0] + gn[1]) + (gn[2] + gn[3])


def put_mlp_grads(hid, gp, n2, gf, keep_ref, send_ref):
    for m in range(4):
        columns = slice(m * 256, (m + 1) * 256)
        up = tn(n2[...], gp[:, columns]).astype(BF)
        down = tn(hid[:, columns], gf[...]).astype(BF)
        own_up = half_index() == 0
        keep_ref[m] = jnp.where(own_up, up, down)
        send_ref[m] = jnp.where(own_up, down, up)


def mlp_both_kernel(layer, count, *refs):
    pieces = refs[:count]
    (middle_ref, base_ref, cot_ref, gain_ref, out_ref, gm_ref, keep_ref, send_ref, small_ref, wm, hid_all, gp_all,
     n2_all) = refs[count:]
    place_mlp(layer, pieces, wm)
    gain = gain_ref[layer:layer + 1, :]
    def step(rows, gain_grad):
        middle = middle_ref[rows, :]
        r, n2, kept, feed = mlp_fwd_block(middle, gain, wm)
        out_ref[rows, :] = base_ref[rows, :] + feed
        gf = cot_ref[rows, :]
        gps, gn = mlp_bwd_block(gf, kept, wm)
        n2_all[rows, :] = n2
        for m in range(4):
            hid_all[rows, m * 256:(m + 1) * 256] = kept[m][0]
            gp_all[rows, m * 256:(m + 1) * 256] = gps[m]
        back, part = norm_back(middle, r, gain, gn)
        gain_grad = gain_grad + part
        gm_ref[rows, :] = gf.astype(F32) + back
        return (gain_grad, )

    gain_grad, = each_sample(middle_ref.shape[0], UNROLL["mlp_both"], step, jnp.zeros((1, 256), F32))
    small_ref[...] = jnp.broadcast_to(gain_grad, small_ref.shape)
    put_mlp_grads(hid_all, gp_all, n2_all, cot_ref, keep_ref, send_ref)


def mlp_bwd_kernel(layer, count, *refs):
    pieces = refs[:count]
    (grad_ref, middle_ref, hid_ref, slope_ref, gain_ref, gm_ref, keep_ref, send_ref, small_ref, wm, gp_all, n2_all,
     gf_all) = refs[count:]
    place_mlp(layer, pieces, wm)
    gain = gain_ref[layer:layer + 1, :]
    def step(rows, gain_grad):
        middle = middle_ref[rows, :]
        r = rescale_of(middle)
        n2_all[rows, :] = (middle * r * gain).astype(BF)
        grad = grad_ref[rows, :]
        gf = grad.astype(BF)
        gf_all[rows, :] = gf
        kept = [(None, slope_ref[rows, m * 256:(m + 1) * 256]) for m in range(4)]
        gps, gn = mlp_bwd_block(gf, kept, wm)
        for m in range(4):
            gp_all[rows, m * 256:(m + 1) * 256] = gps[m]
        back, part = norm_back(middle, r, gain, gn)
        gain_grad = gain_grad + part
        gm_ref[rows, :] = grad + back
        return (gain_grad, )

    gain_grad, = each_sample(middle_ref.shape[0], UNROLL["mlp_bwd"], step, jnp.zeros((1, 256), F32))
    small_ref[...] = jnp.broadcast_to(gain_grad, small_ref.shape)
    put_mlp_grads(hid_ref, gp_all, n2_all, gf_all, keep_ref, send_ref)


def attn_pre_kernel(layer, count, *refs):
    pieces = refs[:count]
    (grad_ref, gm_ref, cur_ref, nrm_ref, mix_ref, gmix_ref, d_cross_ref, d_out_ref, base_ref, gn_ref, small_ref,
     dot_ref, wa, w_cross, w_out, ga_all, gc_all) = refs[count:]
    bias = place_attn(layer, pieces, wa, w_cross, w_out)

    def step(rows, bias_grad):
        grad = grad_ref[rows, :].astype(F32)
        gm = gm_ref[rows, :]
        ga = gm.astype(BF)
        ga_all[rows, :] = ga
        gc = (grad * cur_ref[rows, :].astype(F32)).astype(BF)
        gc_all[rows, :] = gc
        gmix = nt(w_out[...], ga).astype(BF)
        gmix_ref[:, rows] = gmix
        for m in range(4):
            head = slice(m * HD, (m + 1) * HD)
            product = gmix[head].astype(F32) * mix_ref[head, rows].astype(F32)
            dot_ref[m:m + 1, rows] = jnp.sum(product, axis=0, keepdims=True)
        gn_ref[rows, :] = nn(gc, w_cross[...])
        base_ref[rows, :] = gm + grad * (nt(nrm_ref[rows, :], w_cross[...]) + bias)
        return (bias_grad + jnp.sum(gc.astype(F32), axis=0, keepdims=True), )

    bias_grad, = each_sample(cur_ref.shape[0], UNROLL["attn_pre"], step, jnp.zeros((1, 256), F32))
    d_cross = tn(gc_all[...], nrm_ref[...])
    d_cross_ref[...] = d_cross.astype(BF)
    d_out_ref[...] = nn(mix_ref[...], ga_all[...]).astype(BF)
    small_ref[0:1, :] = bias_grad
    small_ref[1:2, :] = jnp.sum(d_cross * w_cross[...].astype(F32), axis=0, keepdims=True)


def qkv_back(rows, mask_ref, qkv_ref, lse_ref, gmix_ref, dot_ref):
    mask = mask_rows(mask_ref, rows)
    parts = []
    for m in range(4):
        q, k, v = (qkv_ref[m * 192 + i * HD:m * 192 + (i + 1) * HD, rows] for i in range(3))
        parts.append((q, k, v, gmix_ref[m * HD:(m + 1) * HD, rows]))
    scores = [slot_scores(q, k, mask) for q, k, v, go in parts]
    gps = [tn(v, go) for q, k, v, go in parts]
    ps, gss = [], []
    for m in range(4):
        p = jnp.exp(scores[m] - lse_ref[m:m + 1, rows])
        ps.append(p.astype(BF))
        gss.append((p * (gps[m] - dot_ref[m:m + 1, rows])).astype(BF))
    return [
        jnp.concatenate([nn(k, gs) * 0.125, nt(q, gs) * 0.125, nt(go, p)], axis=0).astype(BF)
        for (q, k, v, go), p, gs in zip(parts, ps, gss)
    ]


def norm_grad(cur, gain, gn):
    r = rescale_of(cur)
    scaled = gn * gain
    return r * (scaled - cur * (r * r * jnp.mean(cur * scaled, axis=-1, keepdims=True)))


def put_attn_grads(layer, nrm, gqkv_all, wa, gain_ref, d_cross_ref, d_out_ref, small, mlp_small, payload, keep_ref, sends):
    gain_grad = small[1:2, :]
    for m in range(4):
        place = pl.multiple_of((head_index() ^ m) * HD, HD)
        d_qkv = nn(gqkv_all[m * 192:(m + 1) * 192, :], nrm)
        gain_grad = gain_grad + jnp.sum(d_qkv * wa[m, 0:192, :].astype(F32), axis=0, keepdims=True)
        payload[m, 0:192, :] = d_qkv.astype(BF)
        payload[m, 192:256, :] = d_cross_ref[pl.ds(place, HD), :]
        payload[m, 256:320, :] = d_out_ref[m * HD:(m + 1) * HD, :]
    gain_grad = gain_grad / gain_ref[layer:layer + 1, :]
    high, low = split_rows(jnp.concatenate([gain_grad, small[0:1, :], mlp_small[0:1, :], jnp.zeros((5, 256), F32)], axis=0))
    keep = pl.multiple_of(half_index() * 160, 16)
    other = pl.multiple_of((1 - half_index()) * 160, 16)
    for m in range(4):
        each = 4 // len(sends)
        for ref, i, at in ((keep_ref, m, keep), (sends[m // each], m % each, other)):
            ref[i, 0:160, :] = payload[m, pl.ds(at, 160), :]
            ref[i, 160:168, :] = high
            ref[i, 168:176, :] = low


def attn_bwd_kernel(layer, count, *refs):
    pieces = refs[:count]
    (mask_ref, nrm_ref, qkv_ref, lse_ref, gain_ref, gmix_ref, d_cross_ref, d_out_ref, small, dot_ref, mlp_small,
     cur_ref, base_ref, gn_ref, out_ref, keep_ref, send_ref, wa, gqkv_all, payload) = refs[count:]
    place_qkv(layer, pieces, wa)

    def step(rows):
        gn = gn_ref[rows, :]
        for m, gqkv in enumerate(qkv_back(rows, mask_ref, qkv_ref, lse_ref, gmix_ref, dot_ref)):
            gqkv_all[m * 192:(m + 1) * 192, rows] = gqkv
            gn = gn + tn(gqkv, wa[m, 0:192, :])
        out_ref[rows, :] = base_ref[rows, :] + norm_grad(cur_ref[rows, :].astype(F32), gain_ref[layer:layer + 1, :], gn)
        return ()

    each_sample(nrm_ref.shape[0], UNROLL["attn_bwd"], step)
    put_attn_grads(layer, nrm_ref[...], gqkv_all, wa, gain_ref, d_cross_ref, d_out_ref, small, mlp_small,
                   payload, keep_ref, (send_ref,))


def attn_grads_kernel(layer, count, *refs):
    pieces = refs[:count]
    (mask_ref, nrm_ref, qkv_ref, lse_ref, gain_ref, gmix_ref, d_cross_ref, d_out_ref, small, dot_ref, mlp_small,
     gqkv_all, keep_ref, send_low, send_high, wa, payload) = refs[count:]
    place_qkv(layer, pieces, wa)

    def step(rows):
        for m, gqkv in enumerate(qkv_back(rows, mask_ref, qkv_ref, lse_ref, gmix_ref, dot_ref)):
            gqkv_all[m * 192:(m + 1) * 192, rows] = gqkv
        return ()

    each_sample(nrm_ref.shape[0], UNROLL["attn_bwd"], step)
    put_attn_grads(layer, nrm_ref[...], gqkv_all, wa, gain_ref, d_cross_ref, d_out_ref, small, mlp_small,
                   payload, keep_ref, (send_low, send_high))


def attn_post_kernel(layer, count, *refs):
    pieces = refs[:count]
    (gqkv_all, gain_ref, cur_ref, base_ref, gn_ref, out_ref, wa) = refs[count:]
    place_qkv(layer, pieces, wa)

    def step(rows):
        gn = gn_ref[rows, :]
        for m in range(4):
            gn = gn + tn(gqkv_all[m * 192:(m + 1) * 192, rows], wa[m, 0:192, :])
        out_ref[rows, :] = base_ref[rows, :] + norm_grad(cur_ref[rows, :].astype(F32), gain_ref[layer:layer + 1, :], gn)
        return ()

    each_sample(cur_ref.shape[0], UNROLL["attn_post"], step)


def split_rows(x):
    high = x.astype(BF)
    return high, (x - high.astype(F32)).astype(BF)


def pack_kernel(lens, qkv, cross, out, up, down, b, own0, own1, first_l0, half_l1, mask, sems):
    copies = []
    for l, own in ((0, own0), (1, own1)):
        for t in range(3):
            copies.append(pltpu.make_async_copy(qkv.at[l, t], own.at[pl.ds(t * HD, HD)], sems.at[0]))
        copies.append(pltpu.make_async_copy(cross.at[l], own.at[pl.ds(192, HD)], sems.at[0]))
        copies.append(pltpu.make_async_copy(out.at[l], own.at[pl.ds(256, HD)], sems.at[0]))
    for copy in copies:
        copy.start()

    x = pl.multiple_of(quarter_index() * 128, 16)

    def mlp_parts(weight):
        return (pltpu.make_async_copy(weight.at[0, pl.ds(x, 128)], first_l0.at[pl.ds(176, 128)], sems.at[1]),
                pltpu.make_async_copy(weight.at[1], half_l1.at[pl.ds(0, 256)], sems.at[1]))

    @pl.when(half_index() == 0)
    def _():
        for copy in mlp_parts(up):
            copy.start()

    @pl.when(half_index() != 0)
    def _():
        for copy in mlp_parts(down):
            copy.start()

    slots = lax.broadcasted_iota(jnp.int32, (16, 256), 1)
    first = lax.broadcasted_iota(jnp.int32, (16, 256), 0) == 0
    samples = mask.shape[0] // 16
    for i in range(samples):
        length = lens[head_index() * samples + i]
        mask[i * 16:(i + 1) * 16, :] = jnp.where(jnp.logical_and(first, slots >= length), MASKED_SCORE, 0.0).astype(BF)
    lane = lax.broadcasted_iota(jnp.int32, (LAYERS, 256), 1) // HD
    wide = jnp.concatenate([b[...].astype(F32)] * 4, axis=1)
    wide = jnp.where(lane == head_index(), wide, 0.0)
    for l, own in ((0, own0), (1, own1)):
        own[320:352, :] = jnp.broadcast_to(wide[l:l + 1], (32, 256)).astype(BF)
    for copy in copies:
        copy.wait()
    at = pl.multiple_of(half_index() * 176, 16)
    first_l0[0:176, :] = own0[pl.ds(at, 176), :]
    half_l1[256:432, :] = own1[pl.ds(at, 176), :]
    for copy in mlp_parts(up):
        copy.wait()


def stack_kernel(a, b, c, attn, mlp):
    for m, ref in enumerate((a, b, c)):
        attn[m * 176:(m + 1) * 176, :] = ref[0:176, :]
        mlp[m * 128:(m + 1) * 128, :] = ref[176:304, :]


def put_sum(out, at, small_at, rows, total):
    for low, high in ((0, small_at), (small_at + 16, rows)):
        if low < high:
            out[at + low:at + high, :] = total(low, high).astype(BF)
    if small_at < rows:
        both = total(small_at, small_at + 16)
        high, low = split_rows(both[0:8] + both[8:16])
        out[at + small_at:at + small_at + 8, :] = high
        out[at + small_at + 8:at + small_at + 16, :] = low


def core_sum_kernel(small_at, *refs):
    ins, outs = refs[:-4], refs[-4:]
    for m, out in enumerate(outs):
        at = 0
        rest = list(ins)
        for where in small_at:
            keep = rest.pop(0)
            if where is None:
                out[at:at + keep.shape[1], :] = keep[m]
                at += keep.shape[1]
                continue
            got, index = rest.pop(0), m
            if got.shape[0] < keep.shape[0]:
                got, index = (got, rest.pop(0))[m // 2], m % 2
            rows = keep.shape[1]
            put_sum(out, at, where, rows, lambda i, j: keep[m, i:j].astype(F32) + got[index, i:j].astype(F32))
            at += rows


def core_split_kernel(keep, got, keep_out, send_out):
    at = pl.multiple_of(quarter_index() * 128, 16)
    other = pl.multiple_of((1 - quarter_index()) * 128, 16)
    for out, rows in ((keep_out, pl.ds(at, 128)), (send_out, pl.ds(other, 128))):
        for m in range(4):
            out[m] = (keep[m, rows, :].astype(F32) + got[m, rows, :].astype(F32)).astype(BF)


def add_kernel(a, b, out):
    out[...] = (a[...].astype(F32) + b[...].astype(F32)).astype(BF)


def four_sum_kernel(small_at, *refs):
    s, a, b, c, out = refs
    put_sum(out, 0, small_at, s.shape[0],
            lambda i, j: (s[i:j].astype(F32) + a[i:j].astype(F32)) + (b[i:j].astype(F32) + c[i:j].astype(F32)))


def four_split_kernel(*refs):
    done, (s, a, b, c, mlp, attn) = refs[:-6], refs[-6:]

    def total(i, j):
        return (s[i:j].astype(F32) + a[i:j].astype(F32)) + (b[i:j].astype(F32) + c[i:j].astype(F32))

    at = 0
    for ref in done:
        mlp[at:at + 128, :] = ref[...]
        at += 128
    mlp[at:at + 128, :] = total(0, 128).astype(BF)
    put_sum(attn, 0, 160, 176, lambda i, j: total(i + 128, j + 128))


def pair_sum_kernel(low, low_got, high, high_got, low_out, high_out):
    put_sum(low_out, 0, 160, low.shape[0], lambda i, j: low[i:j].astype(F32) + low_got[i:j].astype(F32))
    high_out[...] = (high[...].astype(F32) + high_got[...].astype(F32)).astype(BF)


def last_pair_kernel(low, low_got, high, high_got, low_out, high_out):
    put_sum(low_out, 0, 160, low.shape[0], lambda i, j: low[i:j].astype(F32) + low_got[i:j].astype(F32))
    high_out[0:256, :] = high[...]
    high_out[256:512, :] = high_got[...]


def finish_kernel(low, low_other, high, high_other, late, late_other,
                  d_qkv, d_out, d_up, d_down, d_cross, gain_attn, gain_mlp, bias):
    mine = pl.multiple_of(quarter_index() * 128, 16)
    other = pl.multiple_of((1 - quarter_index()) * 128, 16)

    def place(first, second):
        for l, a, b in ((1, first[0], second[0]), (0, first[2], second[2])):
            d_qkv[l, 0] = a[0:64].astype(F32)
            d_qkv[l, 1] = a[64:128].astype(F32)
            d_qkv[l, 2, 0:32] = a[128:160].astype(F32)
            d_qkv[l, 2, 32:64] = b[0:32].astype(F32)
            d_cross[l] = b[32:96].astype(F32)
            d_out[l] = b[96:160].astype(F32)
        for dst, ref in ((d_up, first[1]), (d_down, second[1])):
            for l, at in ((1, 0), (0, 128)):
                dst[l, pl.ds(mine, 128)] = ref[at:at + 128].astype(F32)
                dst[l, pl.ds(other, 128)] = ref[at + 256:at + 384].astype(F32)

    @pl.when(half_index() == 0)
    def _():
        place((low, high, late), (low_other, high_other, late_other))

    @pl.when(half_index() != 0)
    def _():
        place((low_other, high_other, late_other), (low, high, late))

    for l, ref in ((0, late), (1, low)):
        small = ref[160:168].astype(F32) + ref[168:176].astype(F32)
        gain_attn[l:l + 1, :] = small[0:1]
        gain_mlp[l:l + 1, :] = small[2:3]
        total = jnp.zeros((1, HD), F32)
        for h in range(4):
            total = total + jnp.where(head_index() == h, small[1:2, h * HD:(h + 1) * HD], 0.0)
        bias[l:l + 1, :] = total


SMEM = pl.BlockSpec(memory_space=pltpu.SMEM)
ANY = pl.BlockSpec(memory_space=pl.ANY)


def call(kernel, outs, scratch, name, *args, flops=KERNEL_FLOPS):
    return pl.pallas_call(
        kernel,
        in_specs=[VMEM] * len(args),
        out_specs=[VMEM] * len(outs),
        out_shape=[jax.ShapeDtypeStruct(shape, dtype) for shape, dtype in outs],
        scratch_shapes=[pltpu.VMEM(shape, dtype) for shape, dtype in scratch],
        compiler_params=pltpu.CompilerParams(vmem_limit_bytes=VMEM_LIMIT),
        cost_estimate=pl.CostEstimate(flops=flops, bytes_accessed=1024, transcendentals=0),
        name=name,
    )(*args)


ATTN_SCRATCH = [((4, 352, 256), BF), ((256, 256), BF), ((256, 256), BF)]
MLP_GRADS = [((4, 256, 256), BF), ((4, 256, 256), BF), ((8, 256), F32)]


def attn_fwd(layer, cur, mask, gain, pieces):
    rows = cur.shape[0]
    outs = [((rows, 256), F32), ((rows, 256), F32), ((rows, 256), BF), ((768, rows), BF), ((256, rows), BF), ((8, rows), F32)]
    return call(functools.partial(attn_fwd_kernel, layer, len(pieces)), outs, ATTN_SCRATCH, "attn_fwd", *pieces, cur, mask, gain,
                flops=(LONG, KERNEL_FLOPS)[layer])


def mlp_fwd(layer, middle, base, gain, pieces):
    rows = middle.shape[0]
    outs = [((rows, 256), F32), ((rows, 1024), BF), ((rows, 1024), BF)]
    return call(functools.partial(mlp_fwd_kernel, layer, len(pieces)), outs, [((4, 512, 256), BF)], "mlp_fwd", *pieces,
                middle, base, gain)


def mlp_both(layer, middle, base, cot, gain, pieces):
    rows = middle.shape[0]
    outs = [((rows, 256), F32), ((rows, 256), F32)] + MLP_GRADS
    scratch = [((4, 512, 256), BF), ((rows, 1024), BF), ((rows, 1024), BF), ((rows, 256), BF)]
    return call(functools.partial(mlp_both_kernel, layer, len(pieces)), outs, scratch, "mlp_both", *pieces, middle, base, cot, gain)


def mlp_bwd(layer, grad, middle, hid, slope, gain, pieces):
    rows = middle.shape[0]
    outs = [((rows, 256), F32)] + MLP_GRADS
    scratch = [((4, 512, 256), BF), ((rows, 1024), BF), ((rows, 256), BF), ((rows, 256), BF)]
    return call(functools.partial(mlp_bwd_kernel, layer, len(pieces)), outs, scratch, "mlp_bwd", *pieces,
                grad, middle, hid, slope, gain)


def attn_pre(layer, grad, gm, cur, saved, pieces):
    rows = cur.shape[0]
    nrm, _, mix, _ = saved
    outs = [((256, rows), BF), ((256, 256), BF), ((256, 256), BF), ((rows, 256), F32), ((rows, 256), F32), ((8, 256), F32), ((8, rows), F32)]
    scratch = ATTN_SCRATCH + [((rows, 256), BF), ((rows, 256), BF)]
    return call(functools.partial(attn_pre_kernel, layer, len(pieces)), outs, scratch, "attn_pre", *pieces, grad, gm, cur, nrm, mix)


PAYLOAD = [((4, 176, 256), BF), ((4, 176, 256), BF)]


def attn_bwd(layer, cur, mask, saved, gain, pre, mlp_small, pieces):
    rows = cur.shape[0]
    nrm, qkv, _, lse = saved
    gmix, d_cross, d_out, base, gn, small, dot = pre
    scratch = [((4, 352, 256), BF), ((768, rows), BF), ((4, 320, 256), BF)]
    return call(functools.partial(attn_bwd_kernel, layer, len(pieces)), [((rows, 256), F32)] + PAYLOAD, scratch, "attn_bwd", *pieces,
                mask, nrm, qkv, lse, gain, gmix, d_cross, d_out, small, dot, mlp_small, cur, base, gn)


def attn_grads(layer, mask, saved, gain, pre, mlp_small, pieces):
    nrm, qkv, _, lse = saved
    gmix, d_cross, d_out, _, _, small, dot = pre
    scratch = [((4, 352, 256), BF), ((4, 320, 256), BF)]
    return call(functools.partial(attn_grads_kernel, layer, len(pieces)), [((768, nrm.shape[0]), BF), ((4, 176, 256), BF), ((2, 176, 256), BF), ((2, 176, 256), BF)], scratch, "attn_grads", *pieces,
                mask, nrm, qkv, lse, gain, gmix, d_cross, d_out, small, dot, mlp_small)


def attn_post(layer, gqkv, gain, cur, pre, pieces):
    return call(functools.partial(attn_post_kernel, layer, len(pieces)), [((cur.shape[0], 256), F32)], [((4, 352, 256), BF)], "attn_post", *pieces,
                gqkv, gain, cur, pre[3], pre[4])[0]


VMEM = pl.BlockSpec(memory_space=pltpu.VMEM)


def small_call(kernel, shapes, name, flops=1000):
    def run(*args):
        return pl.pallas_call(
            kernel,
            in_specs=[VMEM] * len(args),
            out_specs=[VMEM] * len(shapes),
            out_shape=[jax.ShapeDtypeStruct(shape, dtype) for shape, dtype in shapes],
            compiler_params=pltpu.CompilerParams(vmem_limit_bytes=SMALL_LIMIT),
            cost_estimate=pl.CostEstimate(flops=flops, bytes_accessed=1024, transcendentals=0),
            name=name,
        )(*args)
    return run


def core_sum(small_at, *groups):
    rows = sum(group[0].shape[1] for group in groups)
    return small_call(functools.partial(core_sum_kernel, small_at), [((rows, 256), BF)] * 4, "core_sum")(
        *[x for group in groups for x in group])


def four_sum(small_at, terms, flops=1000):
    return small_call(functools.partial(four_sum_kernel, small_at), [(terms[0].shape, BF)], "four_sum", flops)(*terms)[0]


def swap(x, axis, size, mask):
    return lax.ppermute(x, axis, [(i, i ^ mask) for i in range(size)])


def tie(x, *before):
    return lax.optimization_barrier((x,) + before)[0]


def solution(mesh):
    dp_size, head_size = mesh.shape["dp"], mesh.shape["head"]

    def core_swap(x):
        return swap(x, "dp", dp_size, 1)

    def fetch(x):
        return [swap(x, "head", head_size, m) for m in range(1, head_size)]

    def scatter(sums):
        return [sums[0]] + [swap(sums[m], "head", head_size, m) for m in range(1, head_size)]

    def split(keep, got):
        return small_call(core_split_kernel, [((4, 128, 256), BF)] * 2, "core_split")(keep, got)

    def four_split(terms, done=(), flops=1000):
        return small_call(four_split_kernel, [((128 * (len(done) + 1), 256), BF), ((176, 256), BF)], "four_split", flops)(*done, *terms)

    bits = [1 << i for i in range(1, dp_size.bit_length() - 1)]

    def sum_direct(x):
        for i in range(0, len(bits), 2):
            masks = (bits[i], bits[i + 1], bits[i] + bits[i + 1]) if i + 1 < len(bits) else (bits[i],)
            terms = [x] + [swap(x, "dp", dp_size, mask) for mask in masks]
            x = four_sum(160, terms + [jnp.zeros_like(x)] * (4 - len(terms)))
        return x

    def sum_pairs(low, high):
        pairs = list(zip(bits, bits[1:] + bits[:1]))
        for i, (one, two) in enumerate(pairs):
            kernel, more = (last_pair_kernel, 256) if i == len(pairs) - 1 else (pair_sum_kernel, 0)
            low, high = small_call(kernel, [(low.shape, BF), ((high.shape[0] + more, 256), BF)], "pair_sum")(
                low, swap(low, "dp", dp_size, one), high, swap(high, "dp", dp_size, two))
        return low, high

    def body(tokens, lengths, cotangent, gain_attn, gain_mlp, w_qkv, w_out, w_up, w_down, w_cross, b_cross):
        rows = tokens.shape[0]
        own0, own1, first_l0, half_l1, mask = pl.pallas_call(
            pack_kernel,
            in_specs=[SMEM] + [ANY] * 5 + [VMEM],
            out_specs=[VMEM] * 5,
            out_shape=[jax.ShapeDtypeStruct((n, 256), BF) for n in (352, 352, 304, 432)]
            + [jax.ShapeDtypeStruct((rows // 16, 256), BF)],
            scratch_shapes=[pltpu.SemaphoreType.DMA((2,))],
            name="pack",
        )(lengths, w_qkv.transpose(0, 2, 3, 1), w_cross.transpose(0, 2, 1), w_out, w_up, w_down, b_cross)

        l1 = fetch(half_l1)
        a0, m0 = small_call(stack_kernel, [((528, 256), BF), ((384, 256), BF)], "stack")(*fetch(first_l0))
        a0 = [own0, a0, core_swap(a0)]
        mid0, base0, *saved0 = attn_fwd(0, tokens, mask, gain_attn, a0)
        m0 = [m0, tie(swap(m0, "dp", dp_size, 2), mid0)]
        m0 = [w_up, w_down] + m0 + [core_swap(x) for x in m0]
        cur1, hid0, slope0 = mlp_fwd(0, mid0, base0, gain_mlp, m0)
        l1 = [tie(x, cur1) for x in l1]
        l1 = l1 + [core_swap(x) for x in l1]
        a1, m1 = [own1] + l1, [w_up, w_down] + l1
        mid1, base1, *saved1 = attn_fwd(1, cur1, mask, gain_attn, a1)
        output, gm1, keep_m1, send_m1, small_m1 = mlp_both(1, mid1, base1, cotangent, gain_mlp, m1)
        pre = attn_pre(1, cotangent, gm1, cur1, saved1, a1)
        keep_m1, send_m1 = split(keep_m1, tie(core_swap(send_m1), pre[0]))
        got_m1 = swap(send_m1, "dp", dp_size, 2)
        grad1, keep_a1, send_a1 = attn_bwd(1, cur1, tie(mask, send_m1), saved1, gain_attn, pre, small_m1, a1)
        gm0, keep_m0, send_m0, small_m0 = mlp_bwd(0, grad1, mid0, hid0, slope0, gain_mlp, m0)
        m1_sum = small_call(add_kernel, [((4, 128, 256), BF)], "add", LONG)(keep_m1, tie(got_m1, gm0))[0]
        sums = core_sum((None, 160), (m1_sum,), (keep_a1, tie(core_swap(send_a1), m1_sum)))
        got = scatter(sums)
        pre = attn_pre(0, grad1, gm0, tokens, saved0, a0)
        keep_m0, send_m0 = split(keep_m0, tie(core_swap(send_m0), pre[0]))
        got_m0 = swap(send_m0, "dp", dp_size, 2)
        gqkv, keep_a0, *send_a0 = attn_grads(0, tie(mask, send_m0), saved0, gain_attn, pre, small_m0, a0)
        mlp1, attn1 = four_split([tie(x, gqkv) for x in got], (), LONG)
        sums = core_sum((128, 160), (keep_m0, tie(got_m0, mlp1)), (keep_a0, *[core_swap(x) for x in send_a0]))
        got = scatter(sums)
        grad0 = attn_post(0, tie(gqkv, *sums), gain_attn, tokens, pre, a0)
        attn1 = sum_direct(attn1)
        mlp, attn0 = four_split([tie(x, grad0, attn1) for x in got], (mlp1,))
        attn0, mlp = sum_pairs(attn0, mlp)
        d_qkv, d_out, d_up, d_down, d_cross, d_ga, d_gm, d_bias = small_call(
            finish_kernel,
            [((LAYERS, 3, HD, 256), F32), ((LAYERS, HD, 256), F32), ((LAYERS, 256, 256), F32), ((LAYERS, 256, 256), F32),
             ((LAYERS, HD, 256), F32), ((LAYERS, 256), F32), ((LAYERS, 256), F32), ((LAYERS, HD), F32)],
            "finish",
        )(attn1, core_swap(attn1), mlp, core_swap(mlp), attn0, core_swap(attn0))
        return (output, grad0, d_ga, d_gm, d_qkv.transpose(0, 3, 1, 2), d_out, d_up, d_down,
                d_cross.transpose(0, 2, 1), d_bias)

    rows, weights = P(("dp", "head"), None), P(None, "head", None)
    return jax.shard_map(
        body,
        mesh=mesh,
        in_specs=(rows, P("dp"), rows, P(), P(), P(None, None, None, "head"), weights, P(None, None, "head"),
                  weights, P(None, None, "head"), P(None, "head")),
        out_specs=(rows, rows, P(), P(), P(None, None, None, "head"), weights, P(None, None, "head"),
                   weights, P(None, None, "head"), P(None, "head")),
        check_vma=False,
    )
```

```python
import functools

import jax
import jax.numpy as jnp
from jax import lax
from jax.experimental import pallas as pl
from jax.experimental.pallas import tpu as pltpu
from jax.sharding import PartitionSpec as P

HD = 64
LAYERS = 2
EPSILON = 1e-06
MASKED_SCORE = -1000000000.0
BF = jnp.bfloat16
F32 = jnp.float32

VMEM_LIMIT = 32 * 2**20
SMALL_LIMIT = 12 * 2**20
UNROLL = {"attn_fwd": 4, "mlp_fwd": 1, "mlp_both": 1, "mlp_bwd": 1, "attn_bwd": 4, "attn_pre": 4, "attn_post": 2}
KERNEL_FLOPS = 1000
LONG = 50 * 10**9


def nn(a, b):
    return lax.dot_general(a, b, (((1,), (0,)), ((), ())), preferred_element_type=F32)


def nt(a, b):
    return lax.dot_general(a, b, (((1,), (1,)), ((), ())), preferred_element_type=F32)


def tn(a, b):
    return lax.dot_general(a, b, (((0,), (0,)), ((), ())), preferred_element_type=F32)


def rescale_of(values):
    return lax.rsqrt(jnp.mean(values * values, axis=-1, keepdims=True) + EPSILON)


def norm_back(values, rescale, gain, gradient):
    scaled = gradient * gain
    product_mean = jnp.mean(values * scaled, axis=-1, keepdims=True)
    normal = values * rescale
    grad_values = rescale * (scaled - normal * (rescale * product_mean))
    return grad_values, jnp.sum(gradient * normal, axis=0, keepdims=True)


def gelu_and_slope(u):
    cdf = 0.5 + 0.5 * lax.erf(u * 0.7071067811865476)
    density = jnp.exp2((-0.5 * 1.4426950408889634) * (u * u))
    return u * cdf, cdf + u * (density * 0.3989422804014327)


def slot_scores(q, k, mask):
    ones = jnp.where(lax.broadcasted_iota(jnp.int32, mask.shape, 0) == 0, 1.0, 0.0).astype(BF)
    return tn(jnp.concatenate([k, mask], axis=0), jnp.concatenate([q * BF(0.125), ones], axis=0))


def mask_rows(mask_ref, rows):
    return mask_ref[pl.ds(pl.multiple_of(rows.start // 16, 16), 16), :]


def head_index():
    return lax.axis_index("head")


def half_index():
    return lax.axis_index("dp") & 1


def quarter_index():
    return (lax.axis_index("dp") >> 1) & 1


def place_pieces(own, parts, dst, first, rows):
    at = 0
    for ref in own:
        dst[0, at:at + ref.shape[0], :] = ref
        at += ref.shape[0]
    for start, refs in parts:
        for m, ref in enumerate(refs):
            dst[m + 1, pl.ds(pl.multiple_of(start, 16), rows), :] = ref[first:first + rows, :]


def parts_of(pieces, rows):
    c, x = half_index(), quarter_index()
    if len(pieces) == 6:
        return [(c * rows, pieces[0:3]), ((1 - c) * rows, pieces[3:6])]
    places = [c, 1 - c] if len(pieces) == 2 else [2 * i + j for i, j in ((c, x), (c, 1 - x), (1 - c, x), (1 - c, 1 - x))]
    return [(place * rows, [ref.at[pl.ds(m * rows, rows)] for m in range(3)]) for place, ref in zip(places, pieces)]


def place_attn_pieces(layer, pieces, wa):
    place_pieces((pieces[0][...],), parts_of(pieces[1:], 176), wa, 256 * layer, 176)


def place_qkv(layer, pieces, wa, wq):
    place_attn_pieces(layer, pieces, wa)
    side_by_side(wa, wq)


def side_by_side(wa, wq):
    for m in range(4):
        wq[m * 192:(m + 1) * 192, :] = wa[m, 0:192, :]


def place_attn(layer, pieces, wa, w_cross, w_out):
    place_attn_pieces(layer, pieces, wa)
    total = jnp.zeros((1, 256), F32)
    for m in range(4):
        place = pl.multiple_of((head_index() ^ m) * HD, HD)
        w_cross[pl.ds(place, HD), :] = wa[m, 192:256, :]
        w_out[m * HD:(m + 1) * HD, :] = wa[m, 256:320, :]
        total = total + wa[m, 320:336, :].astype(F32)[0:1, :]
    return total


def place_mlp(layer, pieces, wm, up_all, down_all):
    rows = 256 if len(pieces) == 8 else 128
    place_pieces((pieces[0][layer], pieces[1][layer]), parts_of(pieces[2:], rows), wm, 0, rows)
    for m in range(4):
        up_all[:, m * 256:(m + 1) * 256] = wm[m, 0:256, :]
        down_all[m * 256:(m + 1) * 256, :] = wm[m, 256:512, :]


def each_sample(rows, unroll, step, *init, size=256):
    def body(i, carried):
        return step(pl.ds(pl.multiple_of(i * size, size), size), *carried)

    return lax.fori_loop(0, rows // size, body, init, unroll=unroll)


def attn_fwd_kernel(layer, count, *refs):
    pieces = refs[:count]
    (cur_ref, mask_ref, gain_ref, middle_ref, base_ref, nrm_ref, qkv_ref, mix_ref, lse_ref, wa, w_cross, w_out,
     wq) = refs[count:]
    bias = place_attn(layer, pieces, wa, w_cross, w_out)
    side_by_side(wa, wq)
    gain = gain_ref[layer:layer + 1, :]
    def step(rows):
        cur = cur_ref[rows, :].astype(F32)
        nrm = (cur * rescale_of(cur) * gain).astype(BF)
        nrm_ref[rows, :] = nrm
        mask = mask_rows(mask_ref, rows)
        qkv_all = nt(wq[...], nrm).astype(BF)
        qkv_ref[:, rows] = qkv_all
        qkv = [qkv_all[m * 192:(m + 1) * 192] for m in range(4)]
        scores = [slot_scores(qkv[m][0:64], qkv[m][64:128], mask) for m in range(4)]
        cross = nt(nrm, w_cross[...]) + bias
        probs = []
        for m in range(4):
            top = jnp.max(scores[m], axis=0, keepdims=True)
            e = jnp.exp(scores[m] - top)
            total = jnp.sum(e, axis=0, keepdims=True)
            probs.append((e * (1.0 / total)).astype(BF))
            lse_ref[m:m + 1, rows] = top + jnp.log(total)
        mix = jnp.concatenate([nn(qkv[m][128:192], probs[m]).astype(BF) for m in range(4)], axis=0)
        mix_ref[:, rows] = mix
        middle = cur + tn(mix, w_out[...])
        middle_ref[rows, :] = middle
        base_ref[rows, :] = middle + cur * cross
        return ()

    each_sample(cur_ref.shape[0], UNROLL["attn_fwd"], step)


def mlp_fwd_block(middle, gain, up_all, down_all):
    r = rescale_of(middle)
    n2 = (middle * r * gain).astype(BF)
    hid, slope = gelu_and_slope(nn(n2, up_all[...]))
    hid = hid.astype(BF)
    return r, n2, hid, slope.astype(BF), nn(hid, down_all[...])


def mlp_fwd_kernel(layer, count, *refs):
    pieces = refs[:count]
    (middle_ref, base_ref, gain_ref, out_ref, hid_ref, slope_ref, wm, up_all, down_all) = refs[count:]
    place_mlp(layer, pieces, wm, up_all, down_all)
    gain = gain_ref[layer:layer + 1, :]

    def step(rows):
        _, _, hid, slope, feed = mlp_fwd_block(middle_ref[rows, :], gain, up_all, down_all)
        hid_ref[rows, :] = hid
        slope_ref[rows, :] = slope
        out_ref[rows, :] = base_ref[rows, :] + feed
        return ()

    each_sample(middle_ref.shape[0], UNROLL["mlp_fwd"], step, size=middle_ref.shape[0])


def mlp_bwd_block(gf, slope, up_all, down_all):
    gp = (nt(gf, down_all[...]) * slope.astype(F32)).astype(BF)
    return gp, nt(gp, up_all[...])


def put_mlp_grads(hid, gp, n2, gf, keep_ref, send_ref):
    up = tn(n2[...], gp[...]).astype(BF)
    down = tn(hid[...], gf[...]).astype(BF)
    own_up = half_index() == 0
    for m in range(4):
        part = slice(m * 256, (m + 1) * 256)
        keep_ref[m] = jnp.where(own_up, up[:, part], down[part])
        send_ref[m] = jnp.where(own_up, down[part], up[:, part])


def mlp_both_kernel(layer, count, *refs):
    pieces = refs[:count]
    (middle_ref, base_ref, cot_ref, gain_ref, out_ref, gm_ref, keep_ref, send_ref, small_ref,
     wm, up_all, down_all, hid_all, gp_all, n2_all) = refs[count:]
    place_mlp(layer, pieces, wm, up_all, down_all)
    gain = gain_ref[layer:layer + 1, :]

    def step(rows, gain_grad):
        middle = middle_ref[rows, :]
        r, n2, hid, slope, feed = mlp_fwd_block(middle, gain, up_all, down_all)
        out_ref[rows, :] = base_ref[rows, :] + feed
        gf = cot_ref[rows, :]
        gp, gn = mlp_bwd_block(gf, slope, up_all, down_all)
        n2_all[rows, :] = n2
        hid_all[rows, :] = hid
        gp_all[rows, :] = gp
        back, part = norm_back(middle, r, gain, gn)
        gm_ref[rows, :] = gf.astype(F32) + back
        return (gain_grad + part, )

    gain_grad, = each_sample(middle_ref.shape[0], UNROLL["mlp_both"], step, jnp.zeros((1, 256), F32), size=middle_ref.shape[0])
    small_ref[...] = jnp.broadcast_to(gain_grad, small_ref.shape)
    put_mlp_grads(hid_all, gp_all, n2_all, cot_ref, keep_ref, send_ref)


def mlp_bwd_kernel(layer, count, *refs):
    pieces = refs[:count]
    (grad_ref, middle_ref, hid_ref, slope_ref, gain_ref, gm_ref, keep_ref, send_ref, small_ref,
     wm, up_all, down_all, gp_all, n2_all, gf_all) = refs[count:]
    place_mlp(layer, pieces, wm, up_all, down_all)
    gain = gain_ref[layer:layer + 1, :]

    def step(rows, gain_grad):
        middle = middle_ref[rows, :]
        r = rescale_of(middle)
        n2_all[rows, :] = (middle * r * gain).astype(BF)
        grad = grad_ref[rows, :]
        gf = grad.astype(BF)
        gf_all[rows, :] = gf
        gp, gn = mlp_bwd_block(gf, slope_ref[rows, :], up_all, down_all)
        gp_all[rows, :] = gp
        back, part = norm_back(middle, r, gain, gn)
        gm_ref[rows, :] = grad + back
        return (gain_grad + part, )

    gain_grad, = each_sample(middle_ref.shape[0], UNROLL["mlp_bwd"], step, jnp.zeros((1, 256), F32), size=middle_ref.shape[0])
    small_ref[...] = jnp.broadcast_to(gain_grad, small_ref.shape)
    put_mlp_grads(hid_ref, gp_all, n2_all, gf_all, keep_ref, send_ref)


def attn_pre_kernel(layer, count, *refs):
    pieces = refs[:count]
    (grad_ref, gm_ref, cur_ref, nrm_ref, mix_ref, gmix_ref, d_cross_ref, d_out_ref, base_ref, gn_ref, small_ref,
     dot_ref, wa, w_cross, w_out, ga_all, gc_all) = refs[count:]
    bias = place_attn(layer, pieces, wa, w_cross, w_out)

    def step(rows, bias_grad):
        grad = grad_ref[rows, :].astype(F32)
        gm = gm_ref[rows, :]
        ga = gm.astype(BF)
        ga_all[rows, :] = ga
        gc = (grad * cur_ref[rows, :].astype(F32)).astype(BF)
        gc_all[rows, :] = gc
        gmix = nt(w_out[...], ga).astype(BF)
        gmix_ref[:, rows] = gmix
        for m in range(4):
            head = slice(m * HD, (m + 1) * HD)
            product = gmix[head].astype(F32) * mix_ref[head, rows].astype(F32)
            dot_ref[m:m + 1, rows] = jnp.sum(product, axis=0, keepdims=True)
        gn_ref[rows, :] = nn(gc, w_cross[...])
        base_ref[rows, :] = gm + grad * (nt(nrm_ref[rows, :], w_cross[...]) + bias)
        return (bias_grad + jnp.sum(gc.astype(F32), axis=0, keepdims=True), )

    bias_grad, = each_sample(cur_ref.shape[0], UNROLL["attn_pre"], step, jnp.zeros((1, 256), F32))
    d_cross = tn(gc_all[...], nrm_ref[...])
    d_cross_ref[...] = d_cross.astype(BF)
    d_out_ref[...] = nn(mix_ref[...], ga_all[...]).astype(BF)
    small_ref[0:1, :] = bias_grad
    small_ref[1:2, :] = jnp.sum(d_cross * w_cross[...].astype(F32), axis=0, keepdims=True)


def qkv_back(rows, mask_ref, qkv_ref, lse_ref, gmix_ref, dot_ref):
    mask = mask_rows(mask_ref, rows)
    parts = []
    for m in range(4):
        q, k, v = (qkv_ref[m * 192 + i * HD:m * 192 + (i + 1) * HD, rows] for i in range(3))
        parts.append((q, k, v, gmix_ref[m * HD:(m + 1) * HD, rows]))
    scores = [slot_scores(q, k, mask) for q, k, v, go in parts]
    gps = [tn(v, go) for q, k, v, go in parts]
    ps, gss = [], []
    for m in range(4):
        p = jnp.exp(scores[m] - lse_ref[m:m + 1, rows])
        ps.append(p.astype(BF))
        gss.append((p * (gps[m] - dot_ref[m:m + 1, rows])).astype(BF))
    return [
        jnp.concatenate([nn(k, gs) * 0.125, nt(q, gs) * 0.125, nt(go, p)], axis=0).astype(BF)
        for (q, k, v, go), p, gs in zip(parts, ps, gss)
    ]


def norm_grad(cur, gain, gn):
    r = rescale_of(cur)
    scaled = gn * gain
    return r * (scaled - cur * (r * r * jnp.mean(cur * scaled, axis=-1, keepdims=True)))


def put_attn_grads(layer, nrm, gqkv_all, wq, gain_ref, d_cross_ref, d_out_ref, small, mlp_small, payload, keep_ref, sends):
    d_qkv = nn(gqkv_all[...], nrm)
    gain_grad = small[1:2, :] + jnp.sum(d_qkv * wq[...].astype(F32), axis=0, keepdims=True)
    for m in range(4):
        place = pl.multiple_of((head_index() ^ m) * HD, HD)
        payload[m, 0:192, :] = d_qkv[m * 192:(m + 1) * 192].astype(BF)
        payload[m, 192:256, :] = d_cross_ref[pl.ds(place, HD), :]
        payload[m, 256:320, :] = d_out_ref[m * HD:(m + 1) * HD, :]
    gain_grad = gain_grad / gain_ref[layer:layer + 1, :]
    high, low = split_rows(jnp.concatenate([gain_grad, small[0:1, :], mlp_small[0:1, :], jnp.zeros((5, 256), F32)], axis=0))
    keep = pl.multiple_of(half_index() * 160, 16)
    other = pl.multiple_of((1 - half_index()) * 160, 16)
    for m in range(4):
        each = 4 // len(sends)
        for ref, i, at in ((keep_ref, m, keep), (sends[m // each], m % each, other)):
            ref[i, 0:160, :] = payload[m, pl.ds(at, 160), :]
            ref[i, 160:168, :] = high
            ref[i, 168:176, :] = low


def attn_bwd_kernel(layer, count, *refs):
    pieces = refs[:count]
    (mask_ref, nrm_ref, qkv_ref, lse_ref, gain_ref, gmix_ref, d_cross_ref, d_out_ref, small, dot_ref, mlp_small,
     cur_ref, base_ref, gn_ref, out_ref, keep_ref, send_ref, wa, wq, gqkv_all, payload) = refs[count:]
    place_qkv(layer, pieces, wa, wq)

    def step(rows):
        gn = gn_ref[rows, :]
        gqkv = jnp.concatenate(qkv_back(rows, mask_ref, qkv_ref, lse_ref, gmix_ref, dot_ref), axis=0)
        gqkv_all[:, rows] = gqkv
        gn = gn + tn(gqkv, wq[...])
        out_ref[rows, :] = base_ref[rows, :] + norm_grad(cur_ref[rows, :].astype(F32), gain_ref[layer:layer + 1, :], gn)
        return ()

    each_sample(nrm_ref.shape[0], UNROLL["attn_bwd"], step)
    put_attn_grads(layer, nrm_ref[...], gqkv_all, wq, gain_ref, d_cross_ref, d_out_ref, small, mlp_small,
                   payload, keep_ref, (send_ref,))


def attn_grads_kernel(layer, count, *refs):
    pieces = refs[:count]
    (mask_ref, nrm_ref, qkv_ref, lse_ref, gain_ref, gmix_ref, d_cross_ref, d_out_ref, small, dot_ref, mlp_small,
     gqkv_all, keep_ref, send_low, send_high, wa, wq, payload) = refs[count:]
    place_qkv(layer, pieces, wa, wq)

    def step(rows):
        for m, gqkv in enumerate(qkv_back(rows, mask_ref, qkv_ref, lse_ref, gmix_ref, dot_ref)):
            gqkv_all[m * 192:(m + 1) * 192, rows] = gqkv
        return ()

    each_sample(nrm_ref.shape[0], UNROLL["attn_bwd"], step)
    put_attn_grads(layer, nrm_ref[...], gqkv_all, wq, gain_ref, d_cross_ref, d_out_ref, small, mlp_small,
                   payload, keep_ref, (send_low, send_high))


def attn_post_kernel(layer, count, *refs):
    pieces = refs[:count]
    (gqkv_all, gain_ref, cur_ref, base_ref, gn_ref, out_ref, wa, wq) = refs[count:]
    place_qkv(layer, pieces, wa, wq)

    def step(rows):
        gn = gn_ref[rows, :]
        gn = gn + tn(gqkv_all[:, rows], wq[...])
        out_ref[rows, :] = base_ref[rows, :] + norm_grad(cur_ref[rows, :].astype(F32), gain_ref[layer:layer + 1, :], gn)
        return ()

    each_sample(cur_ref.shape[0], UNROLL["attn_post"], step)


def split_rows(x):
    high = x.astype(BF)
    return high, (x - high.astype(F32)).astype(BF)


def pack_kernel(lens, qkv, cross, out, up, down, b, own0, own1, first_l0, half_l1, mask, sems):
    copies = []
    for l, own in ((0, own0), (1, own1)):
        for t in range(3):
            copies.append(pltpu.make_async_copy(qkv.at[l, t], own.at[pl.ds(t * HD, HD)], sems.at[0]))
        copies.append(pltpu.make_async_copy(cross.at[l], own.at[pl.ds(192, HD)], sems.at[0]))
        copies.append(pltpu.make_async_copy(out.at[l], own.at[pl.ds(256, HD)], sems.at[0]))
    for copy in copies:
        copy.start()

    x = pl.multiple_of(quarter_index() * 128, 16)

    def mlp_parts(weight):
        return (pltpu.make_async_copy(weight.at[0, pl.ds(x, 128)], first_l0.at[pl.ds(176, 128)], sems.at[1]),
                pltpu.make_async_copy(weight.at[1], half_l1.at[pl.ds(0, 256)], sems.at[1]))

    @pl.when(half_index() == 0)
    def _():
        for copy in mlp_parts(up):
            copy.start()

    @pl.when(half_index() != 0)
    def _():
        for copy in mlp_parts(down):
            copy.start()

    slots = lax.broadcasted_iota(jnp.int32, (16, 256), 1)
    first = lax.broadcasted_iota(jnp.int32, (16, 256), 0) == 0
    samples = mask.shape[0] // 16
    for i in range(samples):
        length = lens[head_index() * samples + i]
        mask[i * 16:(i + 1) * 16, :] = jnp.where(jnp.logical_and(first, slots >= length), MASKED_SCORE, 0.0).astype(BF)
    lane = lax.broadcasted_iota(jnp.int32, (LAYERS, 256), 1) // HD
    wide = jnp.concatenate([b[...].astype(F32)] * 4, axis=1)
    wide = jnp.where(lane == head_index(), wide, 0.0)
    for l, own in ((0, own0), (1, own1)):
        own[320:352, :] = jnp.broadcast_to(wide[l:l + 1], (32, 256)).astype(BF)
    for copy in copies:
        copy.wait()
    at = pl.multiple_of(half_index() * 176, 16)
    first_l0[0:176, :] = own0[pl.ds(at, 176), :]
    half_l1[256:432, :] = own1[pl.ds(at, 176), :]
    for copy in mlp_parts(up):
        copy.wait()


def stack_kernel(a, b, c, attn, mlp):
    for m, ref in enumerate((a, b, c)):
        attn[m * 176:(m + 1) * 176, :] = ref[0:176, :]
        mlp[m * 128:(m + 1) * 128, :] = ref[176:304, :]


def put_sum(out, at, small_at, rows, total):
    for low, high in ((0, small_at), (small_at + 16, rows)):
        if low < high:
            out[at + low:at + high, :] = total(low, high).astype(BF)
    if small_at < rows:
        both = total(small_at, small_at + 16)
        high, low = split_rows(both[0:8] + both[8:16])
        out[at + small_at:at + small_at + 8, :] = high
        out[at + small_at + 8:at + small_at + 16, :] = low


def core_sum_kernel(small_at, *refs):
    ins, outs = refs[:-4], refs[-4:]
    for m, out in enumerate(outs):
        at = 0
        rest = list(ins)
        for where in small_at:
            keep = rest.pop(0)
            if where is None:
                out[at:at + keep.shape[1], :] = keep[m]
                at += keep.shape[1]
                continue
            got, index = rest.pop(0), m
            if got.shape[0] < keep.shape[0]:
                got, index = (got, rest.pop(0))[m // 2], m % 2
            rows = keep.shape[1]
            put_sum(out, at, where, rows, lambda i, j: keep[m, i:j].astype(F32) + got[index, i:j].astype(F32))
            at += rows


def core_split_kernel(keep, got, keep_out, send_out):
    at = pl.multiple_of(quarter_index() * 128, 16)
    other = pl.multiple_of((1 - quarter_index()) * 128, 16)
    for out, rows in ((keep_out, pl.ds(at, 128)), (send_out, pl.ds(other, 128))):
        for m in range(4):
            out[m] = (keep[m, rows, :].astype(F32) + got[m, rows, :].astype(F32)).astype(BF)


def add_kernel(a, b, out):
    out[...] = (a[...].astype(F32) + b[...].astype(F32)).astype(BF)


def four_sum_kernel(small_at, *refs):
    s, a, b, c, out = refs
    put_sum(out, 0, small_at, s.shape[0],
            lambda i, j: (s[i:j].astype(F32) + a[i:j].astype(F32)) + (b[i:j].astype(F32) + c[i:j].astype(F32)))


def four_split_kernel(*refs):
    done, (s, a, b, c, mlp, attn) = refs[:-6], refs[-6:]

    def total(i, j):
        return (s[i:j].astype(F32) + a[i:j].astype(F32)) + (b[i:j].astype(F32) + c[i:j].astype(F32))

    at = 0
    for ref in done:
        mlp[at:at + 128, :] = ref[...]
        at += 128
    mlp[at:at + 128, :] = total(0, 128).astype(BF)
    put_sum(attn, 0, 160, 176, lambda i, j: total(i + 128, j + 128))


def pair_sum_kernel(low, low_got, high, high_got, low_out, high_out):
    put_sum(low_out, 0, 160, low.shape[0], lambda i, j: low[i:j].astype(F32) + low_got[i:j].astype(F32))
    high_out[...] = (high[...].astype(F32) + high_got[...].astype(F32)).astype(BF)


def last_pair_kernel(low, low_got, high, high_got, low_out, high_out):
    put_sum(low_out, 0, 160, low.shape[0], lambda i, j: low[i:j].astype(F32) + low_got[i:j].astype(F32))
    high_out[0:256, :] = high[...]
    high_out[256:512, :] = high_got[...]


def finish_kernel(low, low_other, high, high_other, late, late_other,
                  d_qkv, d_out, d_up, d_down, d_cross, gain_attn, gain_mlp, bias):
    mine = pl.multiple_of(quarter_index() * 128, 16)
    other = pl.multiple_of((1 - quarter_index()) * 128, 16)

    def place(first, second):
        for l, a, b in ((1, first[0], second[0]), (0, first[2], second[2])):
            d_qkv[l, 0] = a[0:64].astype(F32)
            d_qkv[l, 1] = a[64:128].astype(F32)
            d_qkv[l, 2, 0:32] = a[128:160].astype(F32)
            d_qkv[l, 2, 32:64] = b[0:32].astype(F32)
            d_cross[l] = b[32:96].astype(F32)
            d_out[l] = b[96:160].astype(F32)
        for dst, ref in ((d_up, first[1]), (d_down, second[1])):
            for l, at in ((1, 0), (0, 128)):
                dst[l, pl.ds(mine, 128)] = ref[at:at + 128].astype(F32)
                dst[l, pl.ds(other, 128)] = ref[at + 256:at + 384].astype(F32)

    @pl.when(half_index() == 0)
    def _():
        place((low, high, late), (low_other, high_other, late_other))

    @pl.when(half_index() != 0)
    def _():
        place((low_other, high_other, late_other), (low, high, late))

    for l, ref in ((0, late), (1, low)):
        small = ref[160:168].astype(F32) + ref[168:176].astype(F32)
        gain_attn[l:l + 1, :] = small[0:1]
        gain_mlp[l:l + 1, :] = small[2:3]
        total = jnp.zeros((1, HD), F32)
        for h in range(4):
            total = total + jnp.where(head_index() == h, small[1:2, h * HD:(h + 1) * HD], 0.0)
        bias[l:l + 1, :] = total


SMEM = pl.BlockSpec(memory_space=pltpu.SMEM)
ANY = pl.BlockSpec(memory_space=pl.ANY)


def call(kernel, outs, scratch, name, *args, flops=KERNEL_FLOPS):
    return pl.pallas_call(
        kernel,
        in_specs=[VMEM] * len(args),
        out_specs=[VMEM] * len(outs),
        out_shape=[jax.ShapeDtypeStruct(shape, dtype) for shape, dtype in outs],
        scratch_shapes=[pltpu.VMEM(shape, dtype) for shape, dtype in scratch],
        compiler_params=pltpu.CompilerParams(vmem_limit_bytes=VMEM_LIMIT),
        cost_estimate=pl.CostEstimate(flops=flops, bytes_accessed=1024, transcendentals=0),
        name=name,
    )(*args)


QKV_SCRATCH = [((4, 352, 256), BF), ((768, 256), BF)]
ATTN_SCRATCH = [((4, 352, 256), BF), ((256, 256), BF), ((256, 256), BF)]
MLP_SCRATCH = [((4, 512, 256), BF), ((256, 1024), BF), ((1024, 256), BF)]
MLP_GRADS = [((4, 256, 256), BF), ((4, 256, 256), BF), ((8, 256), F32)]


def attn_fwd(layer, cur, mask, gain, pieces):
    rows = cur.shape[0]
    outs = [((rows, 256), F32), ((rows, 256), F32), ((rows, 256), BF), ((768, rows), BF), ((256, rows), BF), ((8, rows), F32)]
    return call(functools.partial(attn_fwd_kernel, layer, len(pieces)), outs, ATTN_SCRATCH + [((768, 256), BF)], "attn_fwd", *pieces, cur, mask, gain,
                flops=(LONG, KERNEL_FLOPS)[layer])


def mlp_fwd(layer, middle, base, gain, pieces):
    rows = middle.shape[0]
    outs = [((rows, 256), F32), ((rows, 1024), BF), ((rows, 1024), BF)]
    return call(functools.partial(mlp_fwd_kernel, layer, len(pieces)), outs, MLP_SCRATCH, "mlp_fwd", *pieces,
                middle, base, gain)


def mlp_both(layer, middle, base, cot, gain, pieces):
    rows = middle.shape[0]
    outs = [((rows, 256), F32), ((rows, 256), F32)] + MLP_GRADS
    scratch = MLP_SCRATCH + [((rows, 1024), BF), ((rows, 1024), BF), ((rows, 256), BF)]
    return call(functools.partial(mlp_both_kernel, layer, len(pieces)), outs, scratch, "mlp_both", *pieces, middle, base, cot, gain)


def mlp_bwd(layer, grad, middle, hid, slope, gain, pieces):
    rows = middle.shape[0]
    outs = [((rows, 256), F32)] + MLP_GRADS
    scratch = MLP_SCRATCH + [((rows, 1024), BF), ((rows, 256), BF), ((rows, 256), BF)]
    return call(functools.partial(mlp_bwd_kernel, layer, len(pieces)), outs, scratch, "mlp_bwd", *pieces,
                grad, middle, hid, slope, gain)


def attn_pre(layer, grad, gm, cur, saved, pieces):
    rows = cur.shape[0]
    nrm, _, mix, _ = saved
    outs = [((256, rows), BF), ((256, 256), BF), ((256, 256), BF), ((rows, 256), F32), ((rows, 256), F32), ((8, 256), F32), ((8, rows), F32)]
    scratch = ATTN_SCRATCH + [((rows, 256), BF), ((rows, 256), BF)]
    return call(functools.partial(attn_pre_kernel, layer, len(pieces)), outs, scratch, "attn_pre", *pieces, grad, gm, cur, nrm, mix)


PAYLOAD = [((4, 176, 256), BF), ((4, 176, 256), BF)]


def attn_bwd(layer, cur, mask, saved, gain, pre, mlp_small, pieces):
    rows = cur.shape[0]
    nrm, qkv, _, lse = saved
    gmix, d_cross, d_out, base, gn, small, dot = pre
    scratch = QKV_SCRATCH + [((768, rows), BF), ((4, 320, 256), BF)]
    return call(functools.partial(attn_bwd_kernel, layer, len(pieces)), [((rows, 256), F32)] + PAYLOAD, scratch, "attn_bwd", *pieces,
                mask, nrm, qkv, lse, gain, gmix, d_cross, d_out, small, dot, mlp_small, cur, base, gn)


def attn_grads(layer, mask, saved, gain, pre, mlp_small, pieces):
    nrm, qkv, _, lse = saved
    gmix, d_cross, d_out, _, _, small, dot = pre
    scratch = QKV_SCRATCH + [((4, 320, 256), BF)]
    return call(functools.partial(attn_grads_kernel, layer, len(pieces)), [((768, nrm.shape[0]), BF), ((4, 176, 256), BF), ((2, 176, 256), BF), ((2, 176, 256), BF)], scratch, "attn_grads", *pieces,
                mask, nrm, qkv, lse, gain, gmix, d_cross, d_out, small, dot, mlp_small)


def attn_post(layer, gqkv, gain, cur, pre, pieces):
    return call(functools.partial(attn_post_kernel, layer, len(pieces)), [((cur.shape[0], 256), F32)], QKV_SCRATCH, "attn_post", *pieces,
                gqkv, gain, cur, pre[3], pre[4])[0]


VMEM = pl.BlockSpec(memory_space=pltpu.VMEM)


def small_call(kernel, shapes, name, flops=1000):
    def run(*args):
        return pl.pallas_call(
            kernel,
            in_specs=[VMEM] * len(args),
            out_specs=[VMEM] * len(shapes),
            out_shape=[jax.ShapeDtypeStruct(shape, dtype) for shape, dtype in shapes],
            compiler_params=pltpu.CompilerParams(vmem_limit_bytes=SMALL_LIMIT),
            cost_estimate=pl.CostEstimate(flops=flops, bytes_accessed=1024, transcendentals=0),
            name=name,
        )(*args)
    return run


def core_sum(small_at, *groups):
    rows = sum(group[0].shape[1] for group in groups)
    return small_call(functools.partial(core_sum_kernel, small_at), [((rows, 256), BF)] * 4, "core_sum")(
        *[x for group in groups for x in group])


def four_sum(small_at, terms, flops=1000):
    return small_call(functools.partial(four_sum_kernel, small_at), [(terms[0].shape, BF)], "four_sum", flops)(*terms)[0]


def swap(x, axis, size, mask):
    return lax.ppermute(x, axis, [(i, i ^ mask) for i in range(size)])


def tie(x, *before):
    return lax.optimization_barrier((x,) + before)[0]


def solution(mesh):
    dp_size, head_size = mesh.shape["dp"], mesh.shape["head"]

    def core_swap(x):
        return swap(x, "dp", dp_size, 1)

    def fetch(x):
        return [swap(x, "head", head_size, m) for m in range(1, head_size)]

    def scatter(sums):
        return [sums[0]] + [swap(sums[m], "head", head_size, m) for m in range(1, head_size)]

    def split(keep, got):
        return small_call(core_split_kernel, [((4, 128, 256), BF)] * 2, "core_split")(keep, got)

    def four_split(terms, done=(), flops=1000):
        return small_call(four_split_kernel, [((128 * (len(done) + 1), 256), BF), ((176, 256), BF)], "four_split", flops)(*done, *terms)

    bits = [1 << i for i in range(1, dp_size.bit_length() - 1)]

    def sum_direct(x):
        for i in range(0, len(bits), 2):
            masks = (bits[i], bits[i + 1], bits[i] + bits[i + 1]) if i + 1 < len(bits) else (bits[i],)
            terms = [x] + [swap(x, "dp", dp_size, mask) for mask in masks]
            x = four_sum(160, terms + [jnp.zeros_like(x)] * (4 - len(terms)))
        return x

    def sum_pairs(low, high):
        pairs = list(zip(bits, bits[1:] + bits[:1]))
        for i, (one, two) in enumerate(pairs):
            kernel, more = (last_pair_kernel, 256) if i == len(pairs) - 1 else (pair_sum_kernel, 0)
            low, high = small_call(kernel, [(low.shape, BF), ((high.shape[0] + more, 256), BF)], "pair_sum")(
                low, swap(low, "dp", dp_size, one), high, swap(high, "dp", dp_size, two))
        return low, high

    def body(tokens, lengths, cotangent, gain_attn, gain_mlp, w_qkv, w_out, w_up, w_down, w_cross, b_cross):
        rows = tokens.shape[0]
        own0, own1, first_l0, half_l1, mask = pl.pallas_call(
            pack_kernel,
            in_specs=[SMEM] + [ANY] * 5 + [VMEM],
            out_specs=[VMEM] * 5,
            out_shape=[jax.ShapeDtypeStruct((n, 256), BF) for n in (352, 352, 304, 432)]
            + [jax.ShapeDtypeStruct((rows // 16, 256), BF)],
            scratch_shapes=[pltpu.SemaphoreType.DMA((2,))],
            name="pack",
        )(lengths, w_qkv.transpose(0, 2, 3, 1), w_cross.transpose(0, 2, 1), w_out, w_up, w_down, b_cross)

        l1 = fetch(half_l1)
        a0, m0 = small_call(stack_kernel, [((528, 256), BF), ((384, 256), BF)], "stack")(*fetch(first_l0))
        a0 = [own0, a0, core_swap(a0)]
        mid0, base0, *saved0 = attn_fwd(0, tokens, mask, gain_attn, a0)
        m0 = [m0, tie(swap(m0, "dp", dp_size, 2), mid0)]
        m0 = [w_up, w_down] + m0 + [core_swap(x) for x in m0]
        cur1, hid0, slope0 = mlp_fwd(0, mid0, base0, gain_mlp, m0)
        l1 = [tie(x, cur1) for x in l1]
        l1 = l1 + [core_swap(x) for x in l1]
        a1, m1 = [own1] + l1, [w_up, w_down] + l1
        mid1, base1, *saved1 = attn_fwd(1, cur1, mask, gain_attn, a1)
        output, gm1, keep_m1, send_m1, small_m1 = mlp_both(1, mid1, base1, cotangent, gain_mlp, m1)
        pre = attn_pre(1, cotangent, gm1, cur1, saved1, a1)
        keep_m1, send_m1 = split(keep_m1, tie(core_swap(send_m1), pre[0]))
        got_m1 = swap(send_m1, "dp", dp_size, 2)
        grad1, keep_a1, send_a1 = attn_bwd(1, cur1, tie(mask, send_m1), saved1, gain_attn, pre, small_m1, a1)
        gm0, keep_m0, send_m0, small_m0 = mlp_bwd(0, grad1, mid0, hid0, slope0, gain_mlp, m0)
        m1_sum = small_call(add_kernel, [((4, 128, 256), BF)], "add", LONG)(keep_m1, tie(got_m1, gm0))[0]
        sums = core_sum((None, 160), (m1_sum,), (keep_a1, tie(core_swap(send_a1), m1_sum)))
        got = scatter(sums)
        pre = attn_pre(0, grad1, gm0, tokens, saved0, a0)
        keep_m0, send_m0 = split(keep_m0, tie(core_swap(send_m0), pre[0]))
        got_m0 = swap(send_m0, "dp", dp_size, 2)
        gqkv, keep_a0, *send_a0 = attn_grads(0, tie(mask, send_m0), saved0, gain_attn, pre, small_m0, a0)
        mlp1, attn1 = four_split([tie(x, gqkv) for x in got], (), LONG)
        sums = core_sum((128, 160), (keep_m0, tie(got_m0, mlp1)), (keep_a0, *[core_swap(x) for x in send_a0]))
        got = scatter(sums)
        grad0 = attn_post(0, tie(gqkv, *sums), gain_attn, tokens, pre, a0)
        attn1 = sum_direct(attn1)
        mlp, attn0 = four_split([tie(x, grad0, attn1) for x in got], (mlp1,))
        attn0, mlp = sum_pairs(attn0, mlp)
        d_qkv, d_out, d_up, d_down, d_cross, d_ga, d_gm, d_bias = small_call(
            finish_kernel,
            [((LAYERS, 3, HD, 256), F32), ((LAYERS, HD, 256), F32), ((LAYERS, 256, 256), F32), ((LAYERS, 256, 256), F32),
             ((LAYERS, HD, 256), F32), ((LAYERS, 256), F32), ((LAYERS, 256), F32), ((LAYERS, HD), F32)],
            "finish",
        )(attn1, core_swap(attn1), mlp, core_swap(mlp), attn0, core_swap(attn0))
        return (output, grad0, d_ga, d_gm, d_qkv.transpose(0, 3, 1, 2), d_out, d_up, d_down,
                d_cross.transpose(0, 2, 1), d_bias)

    rows, weights = P(("dp", "head"), None), P(None, "head", None)
    return jax.shard_map(
        body,
        mesh=mesh,
        in_specs=(rows, P("dp"), rows, P(), P(), P(None, None, None, "head"), weights, P(None, None, "head"),
                  weights, P(None, None, "head"), P(None, "head")),
        out_specs=(rows, rows, P(), P(), P(None, None, None, "head"), weights, P(None, None, "head"),
                   weights, P(None, None, "head"), P(None, "head")),
        check_vma=False,
    )
```

```python
import functools

import jax
import jax.numpy as jnp
from jax import lax
from jax.experimental import pallas as pl
from jax.experimental.pallas import tpu as pltpu
from jax.sharding import PartitionSpec as P

HD = 64
LAYERS = 2
EPSILON = 1e-06
MASKED_SCORE = -1000000000.0
BF = jnp.bfloat16
F32 = jnp.float32

VMEM_LIMIT = 32 * 2**20
SMALL_LIMIT = 12 * 2**20
UNROLL = {"attn_fwd": 4, "mlp_fwd": 1, "mlp_both": 1, "mlp_bwd": 1, "attn_bwd": 4, "attn_pre": 4, "attn_post": 2}
KERNEL_FLOPS = 1000
LONG = 50 * 10**9


def nn(a, b):
    return lax.dot_general(a, b, (((1,), (0,)), ((), ())), preferred_element_type=F32)


def nt(a, b):
    return lax.dot_general(a, b, (((1,), (1,)), ((), ())), preferred_element_type=F32)


def tn(a, b):
    return lax.dot_general(a, b, (((0,), (0,)), ((), ())), preferred_element_type=F32)


def rescale_of(values):
    return lax.rsqrt(jnp.mean(values * values, axis=-1, keepdims=True) + EPSILON)


def norm_back(values, rescale, gain, gradient):
    scaled = gradient * gain
    product_mean = jnp.mean(values * scaled, axis=-1, keepdims=True)
    normal = values * rescale
    grad_values = rescale * (scaled - normal * (rescale * product_mean))
    return grad_values, jnp.sum(gradient * normal, axis=0, keepdims=True)


def gelu_and_slope(u):
    cdf = 0.5 + 0.5 * lax.erf(u * 0.7071067811865476)
    density = jnp.exp2((-0.5 * 1.4426950408889634) * (u * u))
    return u * cdf, cdf + u * (density * 0.3989422804014327)


def slot_scores(q, k, mask):
    ones = jnp.where(lax.broadcasted_iota(jnp.int32, mask.shape, 0) == 0, 1.0, 0.0).astype(BF)
    return tn(jnp.concatenate([k, mask], axis=0), jnp.concatenate([q * BF(0.125), ones], axis=0))


def mask_rows(mask_ref, rows):
    return mask_ref[pl.ds(pl.multiple_of(rows.start // 16, 16), 16), :]


def head_index():
    return lax.axis_index("head")


def half_index():
    return lax.axis_index("dp") & 1


def quarter_index():
    return (lax.axis_index("dp") >> 1) & 1


def place_pieces(own, parts, dst):
    at = 0
    for ref in own:
        dst[0, at:at + ref.shape[0], :] = ref
        at += ref.shape[0]
    for place, rows, ref in parts:
        for m in range(3):
            dst[m + 1, pl.ds(pl.multiple_of(place * rows, 16), rows), :] = ref[m * rows:(m + 1) * rows, :]


def parts_of(pieces, rows):
    c, x = half_index(), quarter_index()
    if len(pieces) == 2:
        places = [c, 1 - c]
    else:
        each = len(pieces) // 4
        places = [each * (2 * i + j) + part for i, j in ((c, x), (c, 1 - x), (1 - c, x), (1 - c, 1 - x)) for part in range(each)]
    return [(place, rows, ref) for place, ref in zip(places, pieces)]


def place_attn_pieces(pieces, wa):
    place_pieces((pieces[0][...],), parts_of(pieces[1:], 176), wa)


def place_qkv(layer, pieces, wa, wq):
    place_attn_pieces(pieces, wa)
    side_by_side(wa, wq)


def side_by_side(wa, wq):
    for m in range(4):
        wq[m * 192:(m + 1) * 192, :] = wa[m, 0:192, :]


def place_attn(layer, pieces, wa, w_cross, w_out):
    place_attn_pieces(pieces, wa)
    total = jnp.zeros((1, 256), F32)
    for m in range(4):
        place = pl.multiple_of((head_index() ^ m) * HD, HD)
        w_cross[pl.ds(place, HD), :] = wa[m, 192:256, :]
        w_out[m * HD:(m + 1) * HD, :] = wa[m, 256:320, :]
        total = total + wa[m, 320:336, :].astype(F32)[0:1, :]
    return total


def place_mlp(layer, pieces, wm, up_all, down_all):
    place_pieces((pieces[0][layer], pieces[1][layer]), parts_of(pieces[2:], 512 // (len(pieces) - 2)), wm)
    for m in range(4):
        up_all[:, m * 256:(m + 1) * 256] = wm[m, 0:256, :]
        down_all[m * 256:(m + 1) * 256, :] = wm[m, 256:512, :]


def each_sample(rows, unroll, step, *init, size=256):
    def body(i, carried):
        return step(pl.ds(pl.multiple_of(i * size, size), size), *carried)

    return lax.fori_loop(0, rows // size, body, init, unroll=unroll)


def attn_fwd_kernel(layer, count, *refs):
    pieces = refs[:count]
    (cur_ref, mask_ref, gain_ref, middle_ref, base_ref, nrm_ref, qkv_ref, mix_ref, lse_ref, wa, w_cross, w_out,
     wq) = refs[count:]
    bias = place_attn(layer, pieces, wa, w_cross, w_out)
    side_by_side(wa, wq)
    gain = gain_ref[layer:layer + 1, :]
    def step(rows):
        cur = cur_ref[rows, :].astype(F32)
        nrm = (cur * rescale_of(cur) * gain).astype(BF)
        nrm_ref[rows, :] = nrm
        mask = mask_rows(mask_ref, rows)
        qkv_all = nt(wq[...], nrm).astype(BF)
        qkv_ref[:, rows] = qkv_all
        qkv = [qkv_all[m * 192:(m + 1) * 192] for m in range(4)]
        scores = [slot_scores(qkv[m][0:64], qkv[m][64:128], mask) for m in range(4)]
        cross = nt(nrm, w_cross[...]) + bias
        probs = []
        for m in range(4):
            top = jnp.max(scores[m], axis=0, keepdims=True)
            e = jnp.exp(scores[m] - top)
            total = jnp.sum(e, axis=0, keepdims=True)
            probs.append((e * (1.0 / total)).astype(BF))
            lse_ref[m:m + 1, rows] = top + jnp.log(total)
        mix = jnp.concatenate([nn(qkv[m][128:192], probs[m]).astype(BF) for m in range(4)], axis=0)
        mix_ref[:, rows] = mix
        middle = cur + tn(mix, w_out[...])
        middle_ref[rows, :] = middle
        base_ref[rows, :] = middle + cur * cross
        return ()

    each_sample(cur_ref.shape[0], UNROLL["attn_fwd"], step)


def mlp_fwd_block(middle, gain, up_all, down_all):
    r = rescale_of(middle)
    n2 = (middle * r * gain).astype(BF)
    hid, slope = gelu_and_slope(nn(n2, up_all[...]))
    hid = hid.astype(BF)
    return r, n2, hid, slope.astype(BF), nn(hid, down_all[...])


def mlp_fwd_kernel(layer, count, *refs):
    pieces = refs[:count]
    (middle_ref, base_ref, gain_ref, out_ref, hid_ref, slope_ref, wm, up_all, down_all) = refs[count:]
    place_mlp(layer, pieces, wm, up_all, down_all)
    gain = gain_ref[layer:layer + 1, :]

    def step(rows):
        _, _, hid, slope, feed = mlp_fwd_block(middle_ref[rows, :], gain, up_all, down_all)
        hid_ref[rows, :] = hid
        slope_ref[rows, :] = slope
        out_ref[rows, :] = base_ref[rows, :] + feed
        return ()

    each_sample(middle_ref.shape[0], UNROLL["mlp_fwd"], step, size=middle_ref.shape[0])


def mlp_bwd_block(gf, slope, up_all, down_all):
    gp = (nt(gf, down_all[...]) * slope.astype(F32)).astype(BF)
    return gp, nt(gp, up_all[...])


def put_mlp_grads(hid, gp, n2, gf, keep_ref, send_ref):
    up = tn(n2[...], gp[...]).astype(BF)
    down = tn(hid[...], gf[...]).astype(BF)
    own_up = half_index() == 0
    for m in range(4):
        part = slice(m * 256, (m + 1) * 256)
        keep_ref[m] = jnp.where(own_up, up[:, part], down[part])
        send_ref[m] = jnp.where(own_up, down[part], up[:, part])


def mlp_both_kernel(layer, count, *refs):
    pieces = refs[:count]
    (middle_ref, base_ref, cot_ref, gain_ref, out_ref, gm_ref, keep_ref, send_ref, small_ref,
     wm, up_all, down_all, hid_all, gp_all, n2_all) = refs[count:]
    place_mlp(layer, pieces, wm, up_all, down_all)
    gain = gain_ref[layer:layer + 1, :]

    def step(rows, gain_grad):
        middle = middle_ref[rows, :]
        r, n2, hid, slope, feed = mlp_fwd_block(middle, gain, up_all, down_all)
        out_ref[rows, :] = base_ref[rows, :] + feed
        gf = cot_ref[rows, :]
        gp, gn = mlp_bwd_block(gf, slope, up_all, down_all)
        n2_all[rows, :] = n2
        hid_all[rows, :] = hid
        gp_all[rows, :] = gp
        back, part = norm_back(middle, r, gain, gn)
        gm_ref[rows, :] = gf.astype(F32) + back
        return (gain_grad + part, )

    gain_grad, = each_sample(middle_ref.shape[0], UNROLL["mlp_both"], step, jnp.zeros((1, 256), F32), size=middle_ref.shape[0])
    small_ref[...] = jnp.broadcast_to(gain_grad, small_ref.shape)
    put_mlp_grads(hid_all, gp_all, n2_all, cot_ref, keep_ref, send_ref)


def mlp_bwd_kernel(layer, count, *refs):
    pieces = refs[:count]
    (grad_ref, middle_ref, hid_ref, slope_ref, gain_ref, gm_ref, keep_ref, send_ref, small_ref,
     wm, up_all, down_all, gp_all, n2_all, gf_all) = refs[count:]
    place_mlp(layer, pieces, wm, up_all, down_all)
    gain = gain_ref[layer:layer + 1, :]

    def step(rows, gain_grad):
        middle = middle_ref[rows, :]
        r = rescale_of(middle)
        n2_all[rows, :] = (middle * r * gain).astype(BF)
        grad = grad_ref[rows, :]
        gf = grad.astype(BF)
        gf_all[rows, :] = gf
        gp, gn = mlp_bwd_block(gf, slope_ref[rows, :], up_all, down_all)
        gp_all[rows, :] = gp
        back, part = norm_back(middle, r, gain, gn)
        gm_ref[rows, :] = grad + back
        return (gain_grad + part, )

    gain_grad, = each_sample(middle_ref.shape[0], UNROLL["mlp_bwd"], step, jnp.zeros((1, 256), F32), size=middle_ref.shape[0])
    small_ref[...] = jnp.broadcast_to(gain_grad, small_ref.shape)
    put_mlp_grads(hid_ref, gp_all, n2_all, gf_all, keep_ref, send_ref)


def attn_pre_kernel(layer, count, *refs):
    pieces = refs[:count]
    (grad_ref, gm_ref, cur_ref, nrm_ref, mix_ref, gmix_ref, d_cross_ref, d_out_ref, base_ref, gn_ref, small_ref,
     dot_ref, wa, w_cross, w_out, ga_all, gc_all) = refs[count:]
    bias = place_attn(layer, pieces, wa, w_cross, w_out)

    def step(rows, bias_grad):
        grad = grad_ref[rows, :].astype(F32)
        gm = gm_ref[rows, :]
        ga = gm.astype(BF)
        ga_all[rows, :] = ga
        gc = (grad * cur_ref[rows, :].astype(F32)).astype(BF)
        gc_all[rows, :] = gc
        gmix = nt(w_out[...], ga).astype(BF)
        gmix_ref[:, rows] = gmix
        for m in range(4):
            head = slice(m * HD, (m + 1) * HD)
            product = gmix[head].astype(F32) * mix_ref[head, rows].astype(F32)
            dot_ref[m:m + 1, rows] = jnp.sum(product, axis=0, keepdims=True)
        gn_ref[rows, :] = nn(gc, w_cross[...])
        base_ref[rows, :] = gm + grad * (nt(nrm_ref[rows, :], w_cross[...]) + bias)
        return (bias_grad + jnp.sum(gc.astype(F32), axis=0, keepdims=True), )

    bias_grad, = each_sample(cur_ref.shape[0], UNROLL["attn_pre"], step, jnp.zeros((1, 256), F32))
    d_cross = tn(gc_all[...], nrm_ref[...])
    d_cross_ref[...] = d_cross.astype(BF)
    d_out_ref[...] = nn(mix_ref[...], ga_all[...]).astype(BF)
    small_ref[0:1, :] = bias_grad
    small_ref[1:2, :] = jnp.sum(d_cross * w_cross[...].astype(F32), axis=0, keepdims=True)


def qkv_back(rows, mask_ref, qkv_ref, lse_ref, gmix_ref, dot_ref):
    mask = mask_rows(mask_ref, rows)
    parts = []
    for m in range(4):
        q, k, v = (qkv_ref[m * 192 + i * HD:m * 192 + (i + 1) * HD, rows] for i in range(3))
        parts.append((q, k, v, gmix_ref[m * HD:(m + 1) * HD, rows]))
    scores = [slot_scores(q, k, mask) for q, k, v, go in parts]
    gps = [tn(v, go) for q, k, v, go in parts]
    ps, gss = [], []
    for m in range(4):
        p = jnp.exp(scores[m] - lse_ref[m:m + 1, rows])
        ps.append(p.astype(BF))
        gss.append((p * (gps[m] - dot_ref[m:m + 1, rows])).astype(BF))
    return [
        jnp.concatenate([nn(k, gs) * 0.125, nt(q, gs) * 0.125, nt(go, p)], axis=0).astype(BF)
        for (q, k, v, go), p, gs in zip(parts, ps, gss)
    ]


def norm_grad(cur, gain, gn):
    r = rescale_of(cur)
    scaled = gn * gain
    return r * (scaled - cur * (r * r * jnp.mean(cur * scaled, axis=-1, keepdims=True)))


def put_attn_grads(layer, nrm, gqkv_all, wq, gain_ref, d_cross_ref, d_out_ref, small, mlp_small, payload, keep_ref, sends):
    d_qkv = nn(gqkv_all[...], nrm)
    gain_grad = small[1:2, :] + jnp.sum(d_qkv * wq[...].astype(F32), axis=0, keepdims=True)
    for m in range(4):
        place = pl.multiple_of((head_index() ^ m) * HD, HD)
        payload[m, 0:192, :] = d_qkv[m * 192:(m + 1) * 192].astype(BF)
        payload[m, 192:256, :] = d_cross_ref[pl.ds(place, HD), :]
        payload[m, 256:320, :] = d_out_ref[m * HD:(m + 1) * HD, :]
    gain_grad = gain_grad / gain_ref[layer:layer + 1, :]
    high, low = split_rows(jnp.concatenate([gain_grad, small[0:1, :], mlp_small[0:1, :], jnp.zeros((5, 256), F32)], axis=0))
    keep = pl.multiple_of(half_index() * 160, 16)
    other = pl.multiple_of((1 - half_index()) * 160, 16)
    for m in range(4):
        each = 4 // len(sends)
        for ref, i, at in ((keep_ref, m, keep), (sends[m // each], m % each, other)):
            ref[i, 0:160, :] = payload[m, pl.ds(at, 160), :]
            ref[i, 160:168, :] = high
            ref[i, 168:176, :] = low


def attn_bwd_kernel(layer, count, *refs):
    pieces = refs[:count]
    (mask_ref, nrm_ref, qkv_ref, lse_ref, gain_ref, gmix_ref, d_cross_ref, d_out_ref, small, dot_ref, mlp_small,
     cur_ref, base_ref, gn_ref, out_ref, keep_ref, send_ref, wa, wq, gqkv_all, payload) = refs[count:]
    place_qkv(layer, pieces, wa, wq)

    def step(rows):
        gn = gn_ref[rows, :]
        gqkv = jnp.concatenate(qkv_back(rows, mask_ref, qkv_ref, lse_ref, gmix_ref, dot_ref), axis=0)
        gqkv_all[:, rows] = gqkv
        gn = gn + tn(gqkv, wq[...])
        out_ref[rows, :] = base_ref[rows, :] + norm_grad(cur_ref[rows, :].astype(F32), gain_ref[layer:layer + 1, :], gn)
        return ()

    each_sample(nrm_ref.shape[0], UNROLL["attn_bwd"], step)
    put_attn_grads(layer, nrm_ref[...], gqkv_all, wq, gain_ref, d_cross_ref, d_out_ref, small, mlp_small,
                   payload, keep_ref, (send_ref,))


def attn_grads_kernel(layer, count, *refs):
    pieces = refs[:count]
    (mask_ref, nrm_ref, qkv_ref, lse_ref, gain_ref, gmix_ref, d_cross_ref, d_out_ref, small, dot_ref, mlp_small,
     gqkv_all, keep_ref, send_low, send_high, wa, wq, payload) = refs[count:]
    place_qkv(layer, pieces, wa, wq)

    def step(rows):
        for m, gqkv in enumerate(qkv_back(rows, mask_ref, qkv_ref, lse_ref, gmix_ref, dot_ref)):
            gqkv_all[m * 192:(m + 1) * 192, rows] = gqkv
        return ()

    each_sample(nrm_ref.shape[0], UNROLL["attn_bwd"], step)
    put_attn_grads(layer, nrm_ref[...], gqkv_all, wq, gain_ref, d_cross_ref, d_out_ref, small, mlp_small,
                   payload, keep_ref, (send_low, send_high))


def attn_post_kernel(layer, count, *refs):
    pieces = refs[:count]
    (gqkv_all, gain_ref, cur_ref, base_ref, gn_ref, out_ref, wa, wq) = refs[count:]
    place_qkv(layer, pieces, wa, wq)

    def step(rows):
        gn = gn_ref[rows, :]
        gn = gn + tn(gqkv_all[:, rows], wq[...])
        out_ref[rows, :] = base_ref[rows, :] + norm_grad(cur_ref[rows, :].astype(F32), gain_ref[layer:layer + 1, :], gn)
        return ()

    each_sample(cur_ref.shape[0], UNROLL["attn_post"], step)


def split_rows(x):
    high = x.astype(BF)
    return high, (x - high.astype(F32)).astype(BF)


def pack_kernel(lens, qkv, cross, out, up, down, b, own0, own1, group0, group1, mask, sems):
    copies = []
    for l, own in ((0, own0), (1, own1)):
        for t in range(3):
            copies.append(pltpu.make_async_copy(qkv.at[l, t], own.at[pl.ds(t * HD, HD)], sems.at[0]))
        copies.append(pltpu.make_async_copy(cross.at[l], own.at[pl.ds(192, HD)], sems.at[0]))
        copies.append(pltpu.make_async_copy(out.at[l], own.at[pl.ds(256, HD)], sems.at[0]))
    for copy in copies:
        copy.start()

    x = pl.multiple_of(quarter_index() * 128, 16)

    def mlp_parts(weight):
        return [pltpu.make_async_copy(weight.at[l, pl.ds(x, 128)], group.at[pl.ds(176, 128)], sems.at[1])
                for l, group in ((0, group0), (1, group1))]

    @pl.when(half_index() == 0)
    def _():
        for copy in mlp_parts(up):
            copy.start()

    @pl.when(half_index() != 0)
    def _():
        for copy in mlp_parts(down):
            copy.start()

    slots = lax.broadcasted_iota(jnp.int32, (16, 256), 1)
    first = lax.broadcasted_iota(jnp.int32, (16, 256), 0) == 0
    samples = mask.shape[0] // 16
    for i in range(samples):
        length = lens[head_index() * samples + i]
        mask[i * 16:(i + 1) * 16, :] = jnp.where(jnp.logical_and(first, slots >= length), MASKED_SCORE, 0.0).astype(BF)
    lane = lax.broadcasted_iota(jnp.int32, (LAYERS, 256), 1) // HD
    wide = jnp.concatenate([b[...].astype(F32)] * 4, axis=1)
    wide = jnp.where(lane == head_index(), wide, 0.0)
    for l, own in ((0, own0), (1, own1)):
        own[320:352, :] = jnp.broadcast_to(wide[l:l + 1], (32, 256)).astype(BF)
    for copy in copies:
        copy.wait()
    at = pl.multiple_of(half_index() * 176, 16)
    group0[0:176, :] = own0[pl.ds(at, 176), :]
    group1[0:176, :] = own1[pl.ds(at, 176), :]
    for copy in mlp_parts(up):
        copy.wait()


def bring_kernel(*refs):
    half = len(refs) // 2
    for src, dst in zip(refs[:half], refs[half:]):
        dst[...] = src[...]


def stack_kernel(a, b, c, attn, *mlp):
    rows = 128 // len(mlp)
    for m, ref in enumerate((a, b, c)):
        attn[m * 176:(m + 1) * 176, :] = ref[0:176, :]
        for i, out in enumerate(mlp):
            out[m * rows:(m + 1) * rows, :] = ref[176 + i * rows:176 + (i + 1) * rows, :]


def put_sum(out, at, small_at, rows, total):
    for low, high in ((0, small_at), (small_at + 16, rows)):
        if low < high:
            out[at + low:at + high, :] = total(low, high).astype(BF)
    if small_at < rows:
        both = total(small_at, small_at + 16)
        high, low = split_rows(both[0:8] + both[8:16])
        out[at + small_at:at + small_at + 8, :] = high
        out[at + small_at + 8:at + small_at + 16, :] = low


def core_sum_kernel(small_at, *refs):
    ins, outs = refs[:-4], refs[-4:]
    for m, out in enumerate(outs):
        at = 0
        rest = list(ins)
        for where in small_at:
            keep = rest.pop(0)
            if where is None:
                out[at:at + keep.shape[1], :] = keep[m]
                at += keep.shape[1]
                continue
            got, index = rest.pop(0), m
            if got.shape[0] < keep.shape[0]:
                got, index = (got, rest.pop(0))[m // 2], m % 2
            rows = keep.shape[1]
            put_sum(out, at, where, rows, lambda i, j: keep[m, i:j].astype(F32) + got[index, i:j].astype(F32))
            at += rows


def core_split_kernel(keep, got, keep_out, send_out):
    at = pl.multiple_of(quarter_index() * 128, 16)
    other = pl.multiple_of((1 - quarter_index()) * 128, 16)
    for out, rows in ((keep_out, pl.ds(at, 128)), (send_out, pl.ds(other, 128))):
        for m in range(4):
            out[m] = (keep[m, rows, :].astype(F32) + got[m, rows, :].astype(F32)).astype(BF)


def add_kernel(a, b, out):
    out[...] = (a[...].astype(F32) + b[...].astype(F32)).astype(BF)


def four_sum_kernel(small_at, *refs):
    s, a, b, c, out = refs
    put_sum(out, 0, small_at, s.shape[0],
            lambda i, j: (s[i:j].astype(F32) + a[i:j].astype(F32)) + (b[i:j].astype(F32) + c[i:j].astype(F32)))


def four_split_kernel(*refs):
    done, (s, a, b, c, mlp, attn) = refs[:-6], refs[-6:]

    def total(i, j):
        return (s[i:j].astype(F32) + a[i:j].astype(F32)) + (b[i:j].astype(F32) + c[i:j].astype(F32))

    at = 0
    for ref in done:
        mlp[at:at + 128, :] = ref[...]
        at += 128
    mlp[at:at + 128, :] = total(0, 128).astype(BF)
    put_sum(attn, 0, 160, 176, lambda i, j: total(i + 128, j + 128))


def pair_sum_kernel(low, low_got, high, high_got, low_out, high_out):
    put_sum(low_out, 0, 160, low.shape[0], lambda i, j: low[i:j].astype(F32) + low_got[i:j].astype(F32))
    high_out[...] = (high[...].astype(F32) + high_got[...].astype(F32)).astype(BF)


def last_pair_kernel(low, low_got, high, high_got, low_out, high_out):
    put_sum(low_out, 0, 160, low.shape[0], lambda i, j: low[i:j].astype(F32) + low_got[i:j].astype(F32))
    high_out[0:256, :] = high[...]
    high_out[256:512, :] = high_got[...]


def finish_kernel(low, low_other, high, high_other, late, late_other,
                  d_qkv, d_out, d_up, d_down, d_cross, gain_attn, gain_mlp, bias):
    mine = pl.multiple_of(quarter_index() * 128, 16)
    other = pl.multiple_of((1 - quarter_index()) * 128, 16)

    def place(first, second):
        for l, a, b in ((1, first[0], second[0]), (0, first[2], second[2])):
            d_qkv[l, 0] = a[0:64].astype(F32)
            d_qkv[l, 1] = a[64:128].astype(F32)
            d_qkv[l, 2, 0:32] = a[128:160].astype(F32)
            d_qkv[l, 2, 32:64] = b[0:32].astype(F32)
            d_cross[l] = b[32:96].astype(F32)
            d_out[l] = b[96:160].astype(F32)
        for dst, ref in ((d_up, first[1]), (d_down, second[1])):
            for l, at in ((1, 0), (0, 128)):
                dst[l, pl.ds(mine, 128)] = ref[at:at + 128].astype(F32)
                dst[l, pl.ds(other, 128)] = ref[at + 256:at + 384].astype(F32)

    @pl.when(half_index() == 0)
    def _():
        place((low, high, late), (low_other, high_other, late_other))

    @pl.when(half_index() != 0)
    def _():
        place((low_other, high_other, late_other), (low, high, late))

    for l, ref in ((0, late), (1, low)):
        small = ref[160:168].astype(F32) + ref[168:176].astype(F32)
        gain_attn[l:l + 1, :] = small[0:1]
        gain_mlp[l:l + 1, :] = small[2:3]
        total = jnp.zeros((1, HD), F32)
        for h in range(4):
            total = total + jnp.where(head_index() == h, small[1:2, h * HD:(h + 1) * HD], 0.0)
        bias[l:l + 1, :] = total


SMEM = pl.BlockSpec(memory_space=pltpu.SMEM)
ANY = pl.BlockSpec(memory_space=pl.ANY)


def call(kernel, outs, scratch, name, *args, flops=KERNEL_FLOPS):
    return pl.pallas_call(
        kernel,
        in_specs=[VMEM] * len(args),
        out_specs=[VMEM] * len(outs),
        out_shape=[jax.ShapeDtypeStruct(shape, dtype) for shape, dtype in outs],
        scratch_shapes=[pltpu.VMEM(shape, dtype) for shape, dtype in scratch],
        compiler_params=pltpu.CompilerParams(vmem_limit_bytes=VMEM_LIMIT),
        cost_estimate=pl.CostEstimate(flops=flops, bytes_accessed=1024, transcendentals=0),
        name=name,
    )(*args)


QKV_SCRATCH = [((4, 352, 256), BF), ((768, 256), BF)]
ATTN_SCRATCH = [((4, 352, 256), BF), ((256, 256), BF), ((256, 256), BF)]
MLP_SCRATCH = [((4, 512, 256), BF), ((256, 1024), BF), ((1024, 256), BF)]
MLP_GRADS = [((4, 256, 256), BF), ((4, 256, 256), BF), ((8, 256), F32)]


def attn_fwd(layer, cur, mask, gain, pieces):
    rows = cur.shape[0]
    outs = [((rows, 256), F32), ((rows, 256), F32), ((rows, 256), BF), ((768, rows), BF), ((256, rows), BF), ((8, rows), F32)]
    return call(functools.partial(attn_fwd_kernel, layer, len(pieces)), outs, ATTN_SCRATCH + [((768, 256), BF)], "attn_fwd", *pieces, cur, mask, gain,
                flops=(LONG, KERNEL_FLOPS)[layer])


def mlp_fwd(layer, middle, base, gain, pieces):
    rows = middle.shape[0]
    outs = [((rows, 256), F32), ((rows, 1024), BF), ((rows, 1024), BF)]
    return call(functools.partial(mlp_fwd_kernel, layer, len(pieces)), outs, MLP_SCRATCH, "mlp_fwd", *pieces,
                middle, base, gain)


def mlp_both(layer, middle, base, cot, gain, pieces):
    rows = middle.shape[0]
    outs = [((rows, 256), F32), ((rows, 256), F32)] + MLP_GRADS
    scratch = MLP_SCRATCH + [((rows, 1024), BF), ((rows, 1024), BF), ((rows, 256), BF)]
    return call(functools.partial(mlp_both_kernel, layer, len(pieces)), outs, scratch, "mlp_both", *pieces, middle, base, cot, gain)


def mlp_bwd(layer, grad, middle, hid, slope, gain, pieces):
    rows = middle.shape[0]
    outs = [((rows, 256), F32)] + MLP_GRADS
    scratch = MLP_SCRATCH + [((rows, 1024), BF), ((rows, 256), BF), ((rows, 256), BF)]
    return call(functools.partial(mlp_bwd_kernel, layer, len(pieces)), outs, scratch, "mlp_bwd", *pieces,
                grad, middle, hid, slope, gain)


def attn_pre(layer, grad, gm, cur, saved, pieces):
    rows = cur.shape[0]
    nrm, _, mix, _ = saved
    outs = [((256, rows), BF), ((256, 256), BF), ((256, 256), BF), ((rows, 256), F32), ((rows, 256), F32), ((8, 256), F32), ((8, rows), F32)]
    scratch = ATTN_SCRATCH + [((rows, 256), BF), ((rows, 256), BF)]
    return call(functools.partial(attn_pre_kernel, layer, len(pieces)), outs, scratch, "attn_pre", *pieces, grad, gm, cur, nrm, mix)


PAYLOAD = [((4, 176, 256), BF), ((4, 176, 256), BF)]


def attn_bwd(layer, cur, mask, saved, gain, pre, mlp_small, pieces):
    rows = cur.shape[0]
    nrm, qkv, _, lse = saved
    gmix, d_cross, d_out, base, gn, small, dot = pre
    scratch = QKV_SCRATCH + [((768, rows), BF), ((4, 320, 256), BF)]
    return call(functools.partial(attn_bwd_kernel, layer, len(pieces)), [((rows, 256), F32)] + PAYLOAD, scratch, "attn_bwd", *pieces,
                mask, nrm, qkv, lse, gain, gmix, d_cross, d_out, small, dot, mlp_small, cur, base, gn)


def attn_grads(layer, mask, saved, gain, pre, mlp_small, pieces):
    nrm, qkv, _, lse = saved
    gmix, d_cross, d_out, _, _, small, dot = pre
    scratch = QKV_SCRATCH + [((4, 320, 256), BF)]
    return call(functools.partial(attn_grads_kernel, layer, len(pieces)), [((768, nrm.shape[0]), BF), ((4, 176, 256), BF), ((2, 176, 256), BF), ((2, 176, 256), BF)], scratch, "attn_grads", *pieces,
                mask, nrm, qkv, lse, gain, gmix, d_cross, d_out, small, dot, mlp_small)


def attn_post(layer, gqkv, gain, cur, pre, pieces):
    return call(functools.partial(attn_post_kernel, layer, len(pieces)), [((cur.shape[0], 256), F32)], QKV_SCRATCH, "attn_post", *pieces,
                gqkv, gain, cur, pre[3], pre[4])[0]


VMEM = pl.BlockSpec(memory_space=pltpu.VMEM)


def small_call(kernel, shapes, name, flops=1000):
    def run(*args):
        return pl.pallas_call(
            kernel,
            in_specs=[VMEM] * len(args),
            out_specs=[VMEM] * len(shapes),
            out_shape=[jax.ShapeDtypeStruct(shape, dtype) for shape, dtype in shapes],
            compiler_params=pltpu.CompilerParams(vmem_limit_bytes=SMALL_LIMIT),
            cost_estimate=pl.CostEstimate(flops=flops, bytes_accessed=1024, transcendentals=0),
            name=name,
        )(*args)
    return run


def core_sum(small_at, *groups):
    rows = sum(group[0].shape[1] for group in groups)
    return small_call(functools.partial(core_sum_kernel, small_at), [((rows, 256), BF)] * 4, "core_sum")(
        *[x for group in groups for x in group])


def four_sum(small_at, terms, flops=1000):
    return small_call(functools.partial(four_sum_kernel, small_at), [(terms[0].shape, BF)], "four_sum", flops)(*terms)[0]


def swap(x, axis, size, mask):
    return lax.ppermute(x, axis, [(i, i ^ mask) for i in range(size)])


def tie(x, *before):
    return lax.optimization_barrier((x,) + before)[0]


def solution(mesh):
    dp_size, head_size = mesh.shape["dp"], mesh.shape["head"]

    def core_swap(x):
        return swap(x, "dp", dp_size, 1)

    def fetch(x):
        return [swap(x, "head", head_size, m) for m in range(1, head_size)]

    def scatter(sums):
        return [sums[0]] + [swap(sums[m], "head", head_size, m) for m in range(1, head_size)]

    def split(keep, got):
        return small_call(core_split_kernel, [((4, 128, 256), BF)] * 2, "core_split")(keep, got)

    def four_split(terms, done=(), flops=1000):
        return small_call(four_split_kernel, [((128 * (len(done) + 1), 256), BF), ((176, 256), BF)], "four_split", flops)(*done, *terms)

    bits = [1 << i for i in range(1, dp_size.bit_length() - 1)]

    def sum_direct(x):
        for i in range(0, len(bits), 2):
            masks = (bits[i], bits[i + 1], bits[i] + bits[i + 1]) if i + 1 < len(bits) else (bits[i],)
            terms = [x] + [swap(x, "dp", dp_size, mask) for mask in masks]
            x = four_sum(160, terms + [jnp.zeros_like(x)] * (4 - len(terms)))
        return x

    def sum_pairs(low, high):
        pairs = list(zip(bits, bits[1:] + bits[:1]))
        for i, (one, two) in enumerate(pairs):
            kernel, more = (last_pair_kernel, 256) if i == len(pairs) - 1 else (pair_sum_kernel, 0)
            low, high = small_call(kernel, [(low.shape, BF), ((high.shape[0] + more, 256), BF)], "pair_sum")(
                low, swap(low, "dp", dp_size, one), high, swap(high, "dp", dp_size, two))
        return low, high

    def body(tokens, lengths, cotangent, gain_attn, gain_mlp, w_qkv, w_out, w_up, w_down, w_cross, b_cross):
        rows = tokens.shape[0]
        own0, own1, group0, group1, mask = pl.pallas_call(
            pack_kernel,
            in_specs=[SMEM] + [ANY] * 5 + [VMEM],
            out_specs=[VMEM] * 5,
            out_shape=[jax.ShapeDtypeStruct((n, 256), BF) for n in (352, 352, 304, 304)]
            + [jax.ShapeDtypeStruct((rows // 16, 256), BF)],
            scratch_shapes=[pltpu.SemaphoreType.DMA((2,))],
            name="pack",
        )(lengths, w_qkv.transpose(0, 2, 3, 1), w_cross.transpose(0, 2, 1), w_out, w_up, w_down, b_cross)

        def stack(pieces, arrays):
            return small_call(stack_kernel, [((528, 256), BF)] + [((384 // arrays, 256), BF)] * arrays, "stack")(*pieces)

        def quarters(own, before):
            parts = own + [tie(swap(x, "dp", dp_size, 2), before) for x in own]
            return [w_up, w_down] + parts + [core_swap(x) for x in parts]

        pieces0, pieces1 = fetch(group0), fetch(group1)
        near = (tokens, mask, gain_attn, own0)
        tokens, mask, gain_attn, own0 = small_call(bring_kernel, [(x.shape, x.dtype) for x in near], "bring")(*near)
        a0, *m0 = stack([tie(x, own0) for x in pieces0], 2)
        a0 = [own0, a0, core_swap(a0)]
        mid0, base0, *saved0 = attn_fwd(0, tokens, mask, gain_attn, a0)
        m0 = quarters(m0, mid0)
        cur1, hid0, slope0 = mlp_fwd(0, mid0, base0, gain_mlp, m0)
        a1, *m1 = stack([tie(x, cur1) for x in pieces1], 1)
        a1 = [own1, a1, core_swap(a1)]
        mid1, base1, *saved1 = attn_fwd(1, cur1, mask, gain_attn, a1)
        m1 = quarters(m1, mid1)
        output, gm1, keep_m1, send_m1, small_m1 = mlp_both(1, mid1, base1, cotangent, gain_mlp, m1)
        pre = attn_pre(1, cotangent, gm1, cur1, saved1, a1)
        keep_m1, send_m1 = split(keep_m1, tie(core_swap(send_m1), pre[0]))
        got_m1 = swap(send_m1, "dp", dp_size, 2)
        grad1, keep_a1, send_a1 = attn_bwd(1, cur1, tie(mask, send_m1), saved1, gain_attn, pre, small_m1, a1)
        gm0, keep_m0, send_m0, small_m0 = mlp_bwd(0, grad1, mid0, hid0, slope0, gain_mlp, m0)
        m1_sum = small_call(add_kernel, [((4, 128, 256), BF)], "add", LONG)(keep_m1, tie(got_m1, gm0))[0]
        sums = core_sum((None, 160), (m1_sum,), (keep_a1, tie(core_swap(send_a1), m1_sum)))
        got = scatter(sums)
        pre = attn_pre(0, grad1, gm0, tokens, saved0, a0)
        keep_m0, send_m0 = split(keep_m0, tie(core_swap(send_m0), pre[0]))
        got_m0 = swap(send_m0, "dp", dp_size, 2)
        gqkv, keep_a0, *send_a0 = attn_grads(0, tie(mask, send_m0), saved0, gain_attn, pre, small_m0, a0)
        mlp1, attn1 = four_split([tie(x, gqkv) for x in got], (), LONG)
        sums = core_sum((128, 160), (keep_m0, tie(got_m0, mlp1)), (keep_a0, *[core_swap(x) for x in send_a0]))
        got = scatter(sums)
        grad0 = attn_post(0, tie(gqkv, *sums), gain_attn, tokens, pre, a0)
        attn1 = sum_direct(attn1)
        mlp, attn0 = four_split([tie(x, grad0, attn1) for x in got], (mlp1,))
        attn0, mlp = sum_pairs(attn0, mlp)
        d_qkv, d_out, d_up, d_down, d_cross, d_ga, d_gm, d_bias = small_call(
            finish_kernel,
            [((LAYERS, 3, HD, 256), F32), ((LAYERS, HD, 256), F32), ((LAYERS, 256, 256), F32), ((LAYERS, 256, 256), F32),
             ((LAYERS, HD, 256), F32), ((LAYERS, 256), F32), ((LAYERS, 256), F32), ((LAYERS, HD), F32)],
            "finish",
        )(attn1, core_swap(attn1), mlp, core_swap(mlp), attn0, core_swap(attn0))
        return (output, grad0, d_ga, d_gm, d_qkv.transpose(0, 3, 1, 2), d_out, d_up, d_down,
                d_cross.transpose(0, 2, 1), d_bias)

    rows, weights = P(("dp", "head"), None), P(None, "head", None)
    return jax.shard_map(
        body,
        mesh=mesh,
        in_specs=(rows, P("dp"), rows, P(), P(), P(None, None, None, "head"), weights, P(None, None, "head"),
                  weights, P(None, None, "head"), P(None, "head")),
        out_specs=(rows, rows, P(), P(), P(None, None, None, "head"), weights, P(None, None, "head"),
                   weights, P(None, None, "head"), P(None, "head")),
        check_vma=False,
    )
```

```python
import functools

import jax
import jax.numpy as jnp
from jax import lax
from jax.experimental import pallas as pl
from jax.experimental.pallas import tpu as pltpu
from jax.sharding import PartitionSpec as P

HD = 64
LAYERS = 2
EPSILON = 1e-06
MASKED_SCORE = -1000000000.0
BF = jnp.bfloat16
F32 = jnp.float32

VMEM_LIMIT = 32 * 2**20
SMALL_LIMIT = 12 * 2**20
UNROLL = {"attn_fwd": 4, "mlp_fwd": 1, "mlp_both": 1, "mlp_bwd": 1, "attn_bwd": 4, "attn_pre": 4, "attn_post": 2}
KERNEL_FLOPS = 1000
LONG = 50 * 10**9


def nn(a, b):
    return lax.dot_general(a, b, (((1,), (0,)), ((), ())), preferred_element_type=F32)


def nt(a, b):
    return lax.dot_general(a, b, (((1,), (1,)), ((), ())), preferred_element_type=F32)


def tn(a, b):
    return lax.dot_general(a, b, (((0,), (0,)), ((), ())), preferred_element_type=F32)


def rescale_of(values):
    return lax.rsqrt(jnp.mean(values * values, axis=-1, keepdims=True) + EPSILON)


def norm_back(values, rescale, gain, gradient):
    scaled = gradient * gain
    product_mean = jnp.mean(values * scaled, axis=-1, keepdims=True)
    normal = values * rescale
    grad_values = rescale * (scaled - normal * (rescale * product_mean))
    return grad_values, jnp.sum(gradient * normal, axis=0, keepdims=True)


def gelu_and_slope(u):
    cdf = 0.5 + 0.5 * lax.erf(u * 0.7071067811865476)
    density = jnp.exp2((-0.5 * 1.4426950408889634) * (u * u))
    return u * cdf, cdf + u * (density * 0.3989422804014327)


def slot_scores(q, k, mask):
    ones = jnp.where(lax.broadcasted_iota(jnp.int32, mask.shape, 0) == 0, 1.0, 0.0).astype(BF)
    return tn(jnp.concatenate([k, mask], axis=0), jnp.concatenate([q * BF(0.125), ones], axis=0))


def mask_rows(mask_ref, rows):
    return mask_ref[pl.ds(pl.multiple_of(rows.start // 16, 16), 16), :]


def head_index():
    return lax.axis_index("head")


def half_index():
    return lax.axis_index("dp") & 1


def quarter_index():
    return (lax.axis_index("dp") >> 1) & 1


def place_pieces(own, parts, dst):
    at = 0
    for ref in own:
        dst[0, at:at + ref.shape[0], :] = ref
        at += ref.shape[0]
    for place, rows, ref in parts:
        for m in range(3):
            dst[m + 1, pl.ds(pl.multiple_of(place * rows, 16), rows), :] = ref[m * rows:(m + 1) * rows, :]


def parts_of(pieces, rows):
    c, x = half_index(), quarter_index()
    if len(pieces) == 2:
        places = [c, 1 - c]
    else:
        each = len(pieces) // 4
        places = [each * (2 * i + j) + part for i, j in ((c, x), (c, 1 - x), (1 - c, x), (1 - c, 1 - x)) for part in range(each)]
    return [(place, rows, ref) for place, ref in zip(places, pieces)]


def place_attn_pieces(pieces, wa):
    place_pieces((pieces[0][...],), parts_of(pieces[1:], 176), wa)


def place_qkv(layer, pieces, wa, wq):
    place_attn_pieces(pieces, wa)
    side_by_side(wa, wq)


def side_by_side(wa, wq):
    for m in range(4):
        wq[m * 192:(m + 1) * 192, :] = wa[m, 0:192, :]


def place_attn(layer, pieces, wa, w_cross, w_out):
    place_attn_pieces(pieces, wa)
    total = jnp.zeros((1, 256), F32)
    for m in range(4):
        place = pl.multiple_of((head_index() ^ m) * HD, HD)
        w_cross[pl.ds(place, HD), :] = wa[m, 192:256, :]
        w_out[m * HD:(m + 1) * HD, :] = wa[m, 256:320, :]
        total = total + wa[m, 320:336, :].astype(F32)[0:1, :]
    return total


def place_mlp(layer, pieces, wm, up_all, down_all):
    place_pieces((pieces[0][layer], pieces[1][layer]), parts_of(pieces[2:], 512 // (len(pieces) - 2)), wm)
    for m in range(4):
        up_all[:, m * 256:(m + 1) * 256] = wm[m, 0:256, :]
        down_all[m * 256:(m + 1) * 256, :] = wm[m, 256:512, :]


def each_sample(rows, unroll, step, *init, size=256):
    def body(i, carried):
        return step(pl.ds(pl.multiple_of(i * size, size), size), *carried)

    return lax.fori_loop(0, rows // size, body, init, unroll=unroll)


def attn_fwd_kernel(layer, count, *refs):
    pieces = refs[:count]
    (cur_ref, mask_ref, gain_ref, middle_ref, base_ref, nrm_ref, qkv_ref, mix_ref, lse_ref, wa, w_cross, w_out,
     wq) = refs[count:]
    bias = place_attn(layer, pieces, wa, w_cross, w_out)
    side_by_side(wa, wq)
    gain = gain_ref[layer:layer + 1, :]
    def step(rows):
        cur = cur_ref[rows, :].astype(F32)
        nrm = (cur * rescale_of(cur) * gain).astype(BF)
        nrm_ref[rows, :] = nrm
        mask = mask_rows(mask_ref, rows)
        qkv_all = nt(wq[...], nrm).astype(BF)
        qkv_ref[:, rows] = qkv_all
        qkv = [qkv_all[m * 192:(m + 1) * 192] for m in range(4)]
        scores = [slot_scores(qkv[m][0:64], qkv[m][64:128], mask) for m in range(4)]
        cross = nt(nrm, w_cross[...]) + bias
        probs = []
        for m in range(4):
            top = jnp.max(scores[m], axis=0, keepdims=True)
            e = jnp.exp(scores[m] - top)
            total = jnp.sum(e, axis=0, keepdims=True)
            probs.append((e * (1.0 / total)).astype(BF))
            lse_ref[m:m + 1, rows] = top + jnp.log(total)
        mix = jnp.concatenate([nn(qkv[m][128:192], probs[m]).astype(BF) for m in range(4)], axis=0)
        mix_ref[:, rows] = mix
        middle = cur + tn(mix, w_out[...])
        middle_ref[rows, :] = middle
        base_ref[rows, :] = middle + cur * cross
        return ()

    each_sample(cur_ref.shape[0], UNROLL["attn_fwd"], step)


def mlp_fwd_block(middle, gain, up_all, down_all):
    r = rescale_of(middle)
    n2 = (middle * r * gain).astype(BF)
    hid, slope = gelu_and_slope(nn(n2, up_all[...]))
    hid = hid.astype(BF)
    return r, n2, hid, slope.astype(BF), nn(hid, down_all[...])


def mlp_fwd_kernel(layer, count, *refs):
    pieces = refs[:count]
    (middle_ref, base_ref, gain_ref, out_ref, hid_ref, slope_ref, wm, up_all, down_all) = refs[count:]
    place_mlp(layer, pieces, wm, up_all, down_all)
    gain = gain_ref[layer:layer + 1, :]

    def step(rows):
        _, _, hid, slope, feed = mlp_fwd_block(middle_ref[rows, :], gain, up_all, down_all)
        hid_ref[rows, :] = hid
        slope_ref[rows, :] = slope
        out_ref[rows, :] = base_ref[rows, :] + feed
        return ()

    each_sample(middle_ref.shape[0], UNROLL["mlp_fwd"], step, size=middle_ref.shape[0])


def mlp_bwd_block(gf, slope, up_all, down_all):
    gp = (nt(gf, down_all[...]) * slope.astype(F32)).astype(BF)
    return gp, nt(gp, up_all[...])


def put_mlp_grads(hid, gp, n2, gf, keep_ref, send_ref):
    up = tn(n2[...], gp[...]).astype(BF)
    down = tn(hid[...], gf[...]).astype(BF)
    own_up = half_index() == 0
    for m in range(4):
        part = slice(m * 256, (m + 1) * 256)
        keep_ref[m] = jnp.where(own_up, up[:, part], down[part])
        send_ref[m] = jnp.where(own_up, down[part], up[:, part])


def mlp_both_kernel(layer, count, *refs):
    pieces = refs[:count]
    (middle_ref, base_ref, cot_ref, gain_ref, out_ref, gm_ref, keep_ref, send_ref, small_ref,
     wm, up_all, down_all, hid_all, gp_all, n2_all) = refs[count:]
    place_mlp(layer, pieces, wm, up_all, down_all)
    gain = gain_ref[layer:layer + 1, :]

    def step(rows, gain_grad):
        middle = middle_ref[rows, :]
        r, n2, hid, slope, feed = mlp_fwd_block(middle, gain, up_all, down_all)
        out_ref[rows, :] = base_ref[rows, :] + feed
        gf = cot_ref[rows, :]
        gp, gn = mlp_bwd_block(gf, slope, up_all, down_all)
        n2_all[rows, :] = n2
        hid_all[rows, :] = hid
        gp_all[rows, :] = gp
        back, part = norm_back(middle, r, gain, gn)
        gm_ref[rows, :] = gf.astype(F32) + back
        return (gain_grad + part, )

    gain_grad, = each_sample(middle_ref.shape[0], UNROLL["mlp_both"], step, jnp.zeros((1, 256), F32), size=middle_ref.shape[0])
    small_ref[...] = jnp.broadcast_to(gain_grad, small_ref.shape)
    put_mlp_grads(hid_all, gp_all, n2_all, cot_ref, keep_ref, send_ref)


def mlp_bwd_kernel(layer, count, *refs):
    pieces = refs[:count]
    (grad_ref, middle_ref, hid_ref, slope_ref, gain_ref, gm_ref, keep_ref, send_ref, small_ref,
     wm, up_all, down_all, gp_all, n2_all, gf_all) = refs[count:]
    place_mlp(layer, pieces, wm, up_all, down_all)
    gain = gain_ref[layer:layer + 1, :]

    def step(rows, gain_grad):
        middle = middle_ref[rows, :]
        r = rescale_of(middle)
        n2_all[rows, :] = (middle * r * gain).astype(BF)
        grad = grad_ref[rows, :]
        gf = grad.astype(BF)
        gf_all[rows, :] = gf
        gp, gn = mlp_bwd_block(gf, slope_ref[rows, :], up_all, down_all)
        gp_all[rows, :] = gp
        back, part = norm_back(middle, r, gain, gn)
        gm_ref[rows, :] = grad + back
        return (gain_grad + part, )

    gain_grad, = each_sample(middle_ref.shape[0], UNROLL["mlp_bwd"], step, jnp.zeros((1, 256), F32), size=middle_ref.shape[0])
    small_ref[...] = jnp.broadcast_to(gain_grad, small_ref.shape)
    put_mlp_grads(hid_ref, gp_all, n2_all, gf_all, keep_ref, send_ref)


def attn_pre_kernel(layer, count, *refs):
    pieces = refs[:count]
    (grad_ref, gm_ref, cur_ref, nrm_ref, mix_ref, gmix_ref, d_cross_ref, d_out_ref, base_ref, gn_ref, small_ref,
     dot_ref, wa, w_cross, w_out, ga_all, gc_all) = refs[count:]
    bias = place_attn(layer, pieces, wa, w_cross, w_out)

    def step(rows, bias_grad):
        grad = grad_ref[rows, :].astype(F32)
        gm = gm_ref[rows, :]
        ga = gm.astype(BF)
        ga_all[rows, :] = ga
        gc = (grad * cur_ref[rows, :].astype(F32)).astype(BF)
        gc_all[rows, :] = gc
        gmix = nt(w_out[...], ga).astype(BF)
        gmix_ref[:, rows] = gmix
        for m in range(4):
            head = slice(m * HD, (m + 1) * HD)
            product = gmix[head].astype(F32) * mix_ref[head, rows].astype(F32)
            dot_ref[m:m + 1, rows] = jnp.sum(product, axis=0, keepdims=True)
        gn_ref[rows, :] = nn(gc, w_cross[...])
        base_ref[rows, :] = gm + grad * (nt(nrm_ref[rows, :], w_cross[...]) + bias)
        return (bias_grad + jnp.sum(gc.astype(F32), axis=0, keepdims=True), )

    bias_grad, = each_sample(cur_ref.shape[0], UNROLL["attn_pre"], step, jnp.zeros((1, 256), F32))
    d_cross = tn(gc_all[...], nrm_ref[...])
    d_cross_ref[...] = d_cross.astype(BF)
    d_out_ref[...] = nn(mix_ref[...], ga_all[...]).astype(BF)
    small_ref[0:1, :] = bias_grad
    small_ref[1:2, :] = jnp.sum(d_cross * w_cross[...].astype(F32), axis=0, keepdims=True)


def qkv_back(rows, mask_ref, qkv_ref, lse_ref, gmix_ref, dot_ref):
    mask = mask_rows(mask_ref, rows)
    parts = []
    for m in range(4):
        q, k, v = (qkv_ref[m * 192 + i * HD:m * 192 + (i + 1) * HD, rows] for i in range(3))
        parts.append((q, k, v, gmix_ref[m * HD:(m + 1) * HD, rows]))
    scores = [slot_scores(q, k, mask) for q, k, v, go in parts]
    gps = [tn(v, go) for q, k, v, go in parts]
    ps, gss = [], []
    for m in range(4):
        p = jnp.exp(scores[m] - lse_ref[m:m + 1, rows])
        ps.append(p.astype(BF))
        gss.append((p * (gps[m] - dot_ref[m:m + 1, rows])).astype(BF))
    return [
        jnp.concatenate([nn(k, gs) * 0.125, nt(q, gs) * 0.125, nt(go, p)], axis=0).astype(BF)
        for (q, k, v, go), p, gs in zip(parts, ps, gss)
    ]


def norm_grad(cur, gain, gn):
    r = rescale_of(cur)
    scaled = gn * gain
    return r * (scaled - cur * (r * r * jnp.mean(cur * scaled, axis=-1, keepdims=True)))


def put_attn_grads(layer, nrm, gqkv_all, wq, gain_ref, d_cross_ref, d_out_ref, small, mlp_small, payload, keep_ref, sends):
    d_qkv = nn(gqkv_all[...], nrm)
    gain_grad = small[1:2, :] + jnp.sum(d_qkv * wq[...].astype(F32), axis=0, keepdims=True)
    for m in range(4):
        place = pl.multiple_of((head_index() ^ m) * HD, HD)
        payload[m, 0:192, :] = d_qkv[m * 192:(m + 1) * 192].astype(BF)
        payload[m, 192:256, :] = d_cross_ref[pl.ds(place, HD), :]
        payload[m, 256:320, :] = d_out_ref[m * HD:(m + 1) * HD, :]
    gain_grad = gain_grad / gain_ref[layer:layer + 1, :]
    high, low = split_rows(jnp.concatenate([gain_grad, small[0:1, :], mlp_small[0:1, :], jnp.zeros((5, 256), F32)], axis=0))
    keep = pl.multiple_of(half_index() * 160, 16)
    other = pl.multiple_of((1 - half_index()) * 160, 16)
    for m in range(4):
        each = 4 // len(sends)
        for ref, i, at in ((keep_ref, m, keep), (sends[m // each], m % each, other)):
            ref[i, 0:160, :] = payload[m, pl.ds(at, 160), :]
            ref[i, 160:168, :] = high
            ref[i, 168:176, :] = low


def attn_bwd_kernel(layer, count, *refs):
    pieces = refs[:count]
    (mask_ref, nrm_ref, qkv_ref, lse_ref, gain_ref, gmix_ref, d_cross_ref, d_out_ref, small, dot_ref, mlp_small,
     cur_ref, base_ref, gn_ref, out_ref, keep_ref, send_ref, wa, wq, gqkv_all, payload) = refs[count:]
    place_qkv(layer, pieces, wa, wq)

    def step(rows):
        gn = gn_ref[rows, :]
        gqkv = jnp.concatenate(qkv_back(rows, mask_ref, qkv_ref, lse_ref, gmix_ref, dot_ref), axis=0)
        gqkv_all[:, rows] = gqkv
        gn = gn + tn(gqkv, wq[...])
        out_ref[rows, :] = base_ref[rows, :] + norm_grad(cur_ref[rows, :].astype(F32), gain_ref[layer:layer + 1, :], gn)
        return ()

    each_sample(nrm_ref.shape[0], UNROLL["attn_bwd"], step)
    put_attn_grads(layer, nrm_ref[...], gqkv_all, wq, gain_ref, d_cross_ref, d_out_ref, small, mlp_small,
                   payload, keep_ref, (send_ref,))


def attn_grads_kernel(layer, count, *refs):
    pieces = refs[:count]
    (mask_ref, nrm_ref, qkv_ref, lse_ref, gain_ref, gmix_ref, d_cross_ref, d_out_ref, small, dot_ref, mlp_small,
     gqkv_all, keep_ref, send_low, send_high, wa, wq, payload) = refs[count:]
    place_qkv(layer, pieces, wa, wq)

    def step(rows):
        for m, gqkv in enumerate(qkv_back(rows, mask_ref, qkv_ref, lse_ref, gmix_ref, dot_ref)):
            gqkv_all[m * 192:(m + 1) * 192, rows] = gqkv
        return ()

    each_sample(nrm_ref.shape[0], UNROLL["attn_bwd"], step)
    put_attn_grads(layer, nrm_ref[...], gqkv_all, wq, gain_ref, d_cross_ref, d_out_ref, small, mlp_small,
                   payload, keep_ref, (send_low, send_high))


def attn_post_kernel(layer, count, *refs):
    pieces = refs[:count]
    (gqkv_all, gain_ref, cur_ref, base_ref, gn_ref, out_ref, wa, wq) = refs[count:]
    place_qkv(layer, pieces, wa, wq)

    def step(rows):
        gn = gn_ref[rows, :]
        gn = gn + tn(gqkv_all[:, rows], wq[...])
        out_ref[rows, :] = base_ref[rows, :] + norm_grad(cur_ref[rows, :].astype(F32), gain_ref[layer:layer + 1, :], gn)
        return ()

    each_sample(cur_ref.shape[0], UNROLL["attn_post"], step)


def split_rows(x):
    high = x.astype(BF)
    return high, (x - high.astype(F32)).astype(BF)


def pack_kernel(lens, qkv, cross, out, up, down, b, own0, own1, group0, group1, mask, sems):
    copies = []
    for l, own in ((0, own0), (1, own1)):
        for t in range(3):
            copies.append(pltpu.make_async_copy(qkv.at[l, t], own.at[pl.ds(t * HD, HD)], sems.at[0]))
        copies.append(pltpu.make_async_copy(cross.at[l], own.at[pl.ds(192, HD)], sems.at[0]))
        copies.append(pltpu.make_async_copy(out.at[l], own.at[pl.ds(256, HD)], sems.at[0]))
    for copy in copies:
        copy.start()

    x = pl.multiple_of(quarter_index() * 128, 16)

    def mlp_parts(weight):
        return [pltpu.make_async_copy(weight.at[l, pl.ds(x, 128)], group.at[pl.ds(176, 128)], sems.at[1])
                for l, group in ((0, group0), (1, group1))]

    @pl.when(half_index() == 0)
    def _():
        for copy in mlp_parts(up):
            copy.start()

    @pl.when(half_index() != 0)
    def _():
        for copy in mlp_parts(down):
            copy.start()

    slots = lax.broadcasted_iota(jnp.int32, (16, 256), 1)
    first = lax.broadcasted_iota(jnp.int32, (16, 256), 0) == 0
    samples = mask.shape[0] // 16
    for i in range(samples):
        length = lens[head_index() * samples + i]
        mask[i * 16:(i + 1) * 16, :] = jnp.where(jnp.logical_and(first, slots >= length), MASKED_SCORE, 0.0).astype(BF)
    lane = lax.broadcasted_iota(jnp.int32, (LAYERS, 256), 1) // HD
    wide = jnp.concatenate([b[...].astype(F32)] * 4, axis=1)
    wide = jnp.where(lane == head_index(), wide, 0.0)
    for l, own in ((0, own0), (1, own1)):
        own[320:352, :] = jnp.broadcast_to(wide[l:l + 1], (32, 256)).astype(BF)
    for copy in copies:
        copy.wait()
    at = pl.multiple_of(half_index() * 176, 16)
    group0[0:176, :] = own0[pl.ds(at, 176), :]
    group1[0:176, :] = own1[pl.ds(at, 176), :]
    for copy in mlp_parts(up):
        copy.wait()


def bring_kernel(*refs):
    half = len(refs) // 2
    for src, dst in zip(refs[:half], refs[half:]):
        dst[...] = src[...]


def stack_kernel(a, b, c, attn, *mlp):
    rows = 128 // len(mlp)
    for m, ref in enumerate((a, b, c)):
        attn[m * 176:(m + 1) * 176, :] = ref[0:176, :]
        for i, out in enumerate(mlp):
            out[m * rows:(m + 1) * rows, :] = ref[176 + i * rows:176 + (i + 1) * rows, :]


def put_sum(out, at, small_at, rows, total):
    for low, high in ((0, small_at), (small_at + 16, rows)):
        if low < high:
            out[at + low:at + high, :] = total(low, high).astype(BF)
    if small_at < rows:
        both = total(small_at, small_at + 16)
        high, low = split_rows(both[0:8] + both[8:16])
        out[at + small_at:at + small_at + 8, :] = high
        out[at + small_at + 8:at + small_at + 16, :] = low


def core_sum_kernel(small_at, *refs):
    ins, outs = refs[:-4], refs[-4:]
    for m, out in enumerate(outs):
        at = 0
        rest = list(ins)
        for where in small_at:
            keep = rest.pop(0)
            if where is None:
                out[at:at + keep.shape[1], :] = keep[m]
                at += keep.shape[1]
                continue
            got, index = rest.pop(0), m
            if got.shape[0] < keep.shape[0]:
                got, index = (got, rest.pop(0))[m // 2], m % 2
            rows = keep.shape[1]
            put_sum(out, at, where, rows, lambda i, j: keep[m, i:j].astype(F32) + got[index, i:j].astype(F32))
            at += rows


def core_split_kernel(keep, got, keep_out, send_out):
    at = pl.multiple_of(quarter_index() * 128, 16)
    other = pl.multiple_of((1 - quarter_index()) * 128, 16)
    for out, rows in ((keep_out, pl.ds(at, 128)), (send_out, pl.ds(other, 128))):
        for m in range(4):
            out[m] = (keep[m, rows, :].astype(F32) + got[m, rows, :].astype(F32)).astype(BF)


def add_kernel(a, b, out):
    out[...] = (a[...].astype(F32) + b[...].astype(F32)).astype(BF)


def four_sum_kernel(small_at, *refs):
    s, a, b, c, out = refs
    put_sum(out, 0, small_at, s.shape[0],
            lambda i, j: (s[i:j].astype(F32) + a[i:j].astype(F32)) + (b[i:j].astype(F32) + c[i:j].astype(F32)))


def four_split_kernel(*refs):
    done, (s, a, b, c, mlp, attn) = refs[:-6], refs[-6:]

    def total(i, j):
        return (s[i:j].astype(F32) + a[i:j].astype(F32)) + (b[i:j].astype(F32) + c[i:j].astype(F32))

    at = 0
    for ref in done:
        mlp[at:at + 128, :] = ref[...]
        at += 128
    mlp[at:at + 128, :] = total(0, 128).astype(BF)
    put_sum(attn, 0, 160, 176, lambda i, j: total(i + 128, j + 128))


def pair_sum_kernel(low, low_got, high, high_got, low_out, high_out):
    put_sum(low_out, 0, 160, low.shape[0], lambda i, j: low[i:j].astype(F32) + low_got[i:j].astype(F32))
    high_out[...] = (high[...].astype(F32) + high_got[...].astype(F32)).astype(BF)


def last_pair_kernel(low, low_got, high, high_got, low_out, high_out):
    put_sum(low_out, 0, 160, low.shape[0], lambda i, j: low[i:j].astype(F32) + low_got[i:j].astype(F32))
    high_out[0:256, :] = high[...]
    high_out[256:512, :] = high_got[...]


def finish_kernel(low, low_other, high, high_other, late, late_other,
                  d_qkv, d_out, d_up, d_down, d_cross, gain_attn, gain_mlp, bias):
    mine = pl.multiple_of(quarter_index() * 128, 16)
    other = pl.multiple_of((1 - quarter_index()) * 128, 16)

    def place(first, second):
        for l, a, b in ((1, first[0], second[0]), (0, first[2], second[2])):
            d_qkv[l, 0] = a[0:64].astype(F32)
            d_qkv[l, 1] = a[64:128].astype(F32)
            d_qkv[l, 2, 0:32] = a[128:160].astype(F32)
            d_qkv[l, 2, 32:64] = b[0:32].astype(F32)
            d_cross[l] = b[32:96].astype(F32)
            d_out[l] = b[96:160].astype(F32)
        for dst, ref in ((d_up, first[1]), (d_down, second[1])):
            for l, at in ((1, 0), (0, 128)):
                dst[l, pl.ds(mine, 128)] = ref[at:at + 128].astype(F32)
                dst[l, pl.ds(other, 128)] = ref[at + 256:at + 384].astype(F32)

    @pl.when(half_index() == 0)
    def _():
        place((low, high, late), (low_other, high_other, late_other))

    @pl.when(half_index() != 0)
    def _():
        place((low_other, high_other, late_other), (low, high, late))

    for l, ref in ((0, late), (1, low)):
        small = ref[160:168].astype(F32) + ref[168:176].astype(F32)
        gain_attn[l:l + 1, :] = small[0:1]
        gain_mlp[l:l + 1, :] = small[2:3]
        total = jnp.zeros((1, HD), F32)
        for h in range(4):
            total = total + jnp.where(head_index() == h, small[1:2, h * HD:(h + 1) * HD], 0.0)
        bias[l:l + 1, :] = total


SMEM = pl.BlockSpec(memory_space=pltpu.SMEM)
ANY = pl.BlockSpec(memory_space=pl.ANY)


def call(kernel, outs, scratch, name, *args, flops=KERNEL_FLOPS):
    return pl.pallas_call(
        kernel,
        in_specs=[VMEM] * len(args),
        out_specs=[VMEM] * len(outs),
        out_shape=[jax.ShapeDtypeStruct(shape, dtype) for shape, dtype in outs],
        scratch_shapes=[pltpu.VMEM(shape, dtype) for shape, dtype in scratch],
        compiler_params=pltpu.CompilerParams(vmem_limit_bytes=VMEM_LIMIT),
        cost_estimate=pl.CostEstimate(flops=flops, bytes_accessed=1024, transcendentals=0),
        name=name,
    )(*args)


QKV_SCRATCH = [((4, 352, 256), BF), ((768, 256), BF)]
ATTN_SCRATCH = [((4, 352, 256), BF), ((256, 256), BF), ((256, 256), BF)]
MLP_SCRATCH = [((4, 512, 256), BF), ((256, 1024), BF), ((1024, 256), BF)]
MLP_GRADS = [((4, 256, 256), BF), ((4, 256, 256), BF), ((8, 256), F32)]


def attn_fwd(layer, cur, mask, gain, pieces):
    rows = cur.shape[0]
    outs = [((rows, 256), F32), ((rows, 256), F32), ((rows, 256), BF), ((768, rows), BF), ((256, rows), BF), ((8, rows), F32)]
    return call(functools.partial(attn_fwd_kernel, layer, len(pieces)), outs, ATTN_SCRATCH + [((768, 256), BF)], "attn_fwd", *pieces, cur, mask, gain,
                flops=(LONG, KERNEL_FLOPS)[layer])


def mlp_fwd(layer, middle, base, gain, pieces):
    rows = middle.shape[0]
    outs = [((rows, 256), F32), ((rows, 1024), BF), ((rows, 1024), BF)]
    return call(functools.partial(mlp_fwd_kernel, layer, len(pieces)), outs, MLP_SCRATCH, "mlp_fwd", *pieces,
                middle, base, gain)


def mlp_both(layer, middle, base, cot, gain, pieces):
    rows = middle.shape[0]
    outs = [((rows, 256), F32), ((rows, 256), F32)] + MLP_GRADS
    scratch = MLP_SCRATCH + [((rows, 1024), BF), ((rows, 1024), BF), ((rows, 256), BF)]
    return call(functools.partial(mlp_both_kernel, layer, len(pieces)), outs, scratch, "mlp_both", *pieces, middle, base, cot, gain)


def mlp_bwd(layer, grad, middle, hid, slope, gain, pieces):
    rows = middle.shape[0]
    outs = [((rows, 256), F32)] + MLP_GRADS
    scratch = MLP_SCRATCH + [((rows, 1024), BF), ((rows, 256), BF), ((rows, 256), BF)]
    return call(functools.partial(mlp_bwd_kernel, layer, len(pieces)), outs, scratch, "mlp_bwd", *pieces,
                grad, middle, hid, slope, gain)


def attn_pre(layer, grad, gm, cur, saved, pieces):
    rows = cur.shape[0]
    nrm, _, mix, _ = saved
    outs = [((256, rows), BF), ((256, 256), BF), ((256, 256), BF), ((rows, 256), F32), ((rows, 256), F32), ((8, 256), F32), ((8, rows), F32)]
    scratch = ATTN_SCRATCH + [((rows, 256), BF), ((rows, 256), BF)]
    return call(functools.partial(attn_pre_kernel, layer, len(pieces)), outs, scratch, "attn_pre", *pieces, grad, gm, cur, nrm, mix)


PAYLOAD = [((4, 176, 256), BF), ((4, 176, 256), BF)]


def attn_bwd(layer, cur, mask, saved, gain, pre, mlp_small, pieces):
    rows = cur.shape[0]
    nrm, qkv, _, lse = saved
    gmix, d_cross, d_out, base, gn, small, dot = pre
    scratch = QKV_SCRATCH + [((768, rows), BF), ((4, 320, 256), BF)]
    return call(functools.partial(attn_bwd_kernel, layer, len(pieces)), [((rows, 256), F32)] + PAYLOAD, scratch, "attn_bwd", *pieces,
                mask, nrm, qkv, lse, gain, gmix, d_cross, d_out, small, dot, mlp_small, cur, base, gn)


def attn_grads(layer, mask, saved, gain, pre, mlp_small, pieces):
    nrm, qkv, _, lse = saved
    gmix, d_cross, d_out, _, _, small, dot = pre
    scratch = QKV_SCRATCH + [((4, 320, 256), BF)]
    return call(functools.partial(attn_grads_kernel, layer, len(pieces)), [((768, nrm.shape[0]), BF), ((4, 176, 256), BF), ((2, 176, 256), BF), ((2, 176, 256), BF)], scratch, "attn_grads", *pieces,
                mask, nrm, qkv, lse, gain, gmix, d_cross, d_out, small, dot, mlp_small)


def attn_post(layer, gqkv, gain, cur, pre, pieces):
    return call(functools.partial(attn_post_kernel, layer, len(pieces)), [((cur.shape[0], 256), F32)], QKV_SCRATCH, "attn_post", *pieces,
                gqkv, gain, cur, pre[3], pre[4])[0]


VMEM = pl.BlockSpec(memory_space=pltpu.VMEM)


def small_call(kernel, shapes, name, flops=1000):
    def run(*args):
        return pl.pallas_call(
            kernel,
            in_specs=[VMEM] * len(args),
            out_specs=[VMEM] * len(shapes),
            out_shape=[jax.ShapeDtypeStruct(shape, dtype) for shape, dtype in shapes],
            compiler_params=pltpu.CompilerParams(vmem_limit_bytes=SMALL_LIMIT),
            cost_estimate=pl.CostEstimate(flops=flops, bytes_accessed=1024, transcendentals=0),
            name=name,
        )(*args)
    return run


def core_sum(small_at, *groups):
    rows = sum(group[0].shape[1] for group in groups)
    return small_call(functools.partial(core_sum_kernel, small_at), [((rows, 256), BF)] * 4, "core_sum")(
        *[x for group in groups for x in group])


def four_sum(small_at, terms, flops=1000):
    return small_call(functools.partial(four_sum_kernel, small_at), [(terms[0].shape, BF)], "four_sum", flops)(*terms)[0]


def swap(x, axis, size, mask):
    return lax.ppermute(x, axis, [(i, i ^ mask) for i in range(size)])


def tie(x, *before):
    return lax.optimization_barrier((x,) + before)[0]


def solution(mesh):
    dp_size, head_size = mesh.shape["dp"], mesh.shape["head"]

    def core_swap(x):
        return swap(x, "dp", dp_size, 1)

    def fetch(x):
        return [swap(x, "head", head_size, m) for m in range(1, head_size)]

    def scatter(sums):
        return [sums[0]] + [swap(sums[m], "head", head_size, m) for m in range(1, head_size)]

    def split(keep, got):
        return small_call(core_split_kernel, [((4, 128, 256), BF)] * 2, "core_split")(keep, got)

    def four_split(terms, done=(), flops=1000):
        return small_call(four_split_kernel, [((128 * (len(done) + 1), 256), BF), ((176, 256), BF)], "four_split", flops)(*done, *terms)

    bits = [1 << i for i in range(1, dp_size.bit_length() - 1)]

    def sum_direct(x, after):
        for i in range(0, len(bits), 2):
            masks = (bits[i], bits[i + 1], bits[i] + bits[i + 1]) if i + 1 < len(bits) else (bits[i],)
            terms = [x] + [swap(tie(x, after) if k == 2 else x, "dp", dp_size, mask) for k, mask in enumerate(masks)]
            x = four_sum(160, terms + [jnp.zeros_like(x)] * (4 - len(terms)))
        return x

    def sum_pairs(low, high):
        pairs = list(zip(bits, bits[1:] + bits[:1]))
        for i, (one, two) in enumerate(pairs):
            kernel, more = (last_pair_kernel, 256) if i == len(pairs) - 1 else (pair_sum_kernel, 0)
            low, high = small_call(kernel, [(low.shape, BF), ((high.shape[0] + more, 256), BF)], "pair_sum")(
                low, swap(low, "dp", dp_size, one), high, swap(high, "dp", dp_size, two))
        return low, high

    def body(tokens, lengths, cotangent, gain_attn, gain_mlp, w_qkv, w_out, w_up, w_down, w_cross, b_cross):
        rows = tokens.shape[0]
        own0, own1, group0, group1, mask = pl.pallas_call(
            pack_kernel,
            in_specs=[SMEM] + [ANY] * 5 + [VMEM],
            out_specs=[VMEM] * 5,
            out_shape=[jax.ShapeDtypeStruct((n, 256), BF) for n in (352, 352, 304, 304)]
            + [jax.ShapeDtypeStruct((rows // 16, 256), BF)],
            scratch_shapes=[pltpu.SemaphoreType.DMA((2,))],
            name="pack",
        )(lengths, w_qkv.transpose(0, 2, 3, 1), w_cross.transpose(0, 2, 1), w_out, w_up, w_down, b_cross)

        def stack(pieces, arrays):
            return small_call(stack_kernel, [((528, 256), BF)] + [((384 // arrays, 256), BF)] * arrays, "stack")(*pieces)

        def quarters(own, before):
            parts = own + [tie(swap(x, "dp", dp_size, 2), before) for x in own]
            return [w_up, w_down] + parts + [core_swap(x) for x in parts]

        pieces0, pieces1 = fetch(group0), fetch(group1)
        near = (tokens, mask, gain_attn, own0)
        tokens, mask, gain_attn, own0 = small_call(bring_kernel, [(x.shape, x.dtype) for x in near], "bring")(*near)
        a0, *m0 = stack([tie(x, own0) for x in pieces0], 2)
        a0 = [own0, a0, core_swap(a0)]
        mid0, base0, *saved0 = attn_fwd(0, tokens, mask, gain_attn, a0)
        m0 = quarters(m0, mid0)
        cur1, hid0, slope0 = mlp_fwd(0, mid0, base0, gain_mlp, m0)
        a1, *m1 = stack([tie(x, cur1) for x in pieces1], 1)
        a1 = [own1, a1, core_swap(a1)]
        mid1, base1, *saved1 = attn_fwd(1, cur1, mask, gain_attn, a1)
        m1 = quarters(m1, mid1)
        output, gm1, keep_m1, send_m1, small_m1 = mlp_both(1, mid1, base1, cotangent, gain_mlp, m1)
        pre = attn_pre(1, cotangent, gm1, cur1, saved1, a1)
        keep_m1, send_m1 = split(keep_m1, tie(core_swap(send_m1), pre[0]))
        got_m1 = swap(send_m1, "dp", dp_size, 2)
        grad1, keep_a1, send_a1 = attn_bwd(1, cur1, tie(mask, send_m1), saved1, gain_attn, pre, small_m1, a1)
        gm0, keep_m0, send_m0, small_m0 = mlp_bwd(0, grad1, mid0, hid0, slope0, gain_mlp, m0)
        m1_sum = small_call(add_kernel, [((4, 128, 256), BF)], "add", LONG)(keep_m1, tie(got_m1, gm0))[0]
        sums = core_sum((None, 160), (m1_sum,), (keep_a1, tie(core_swap(send_a1), m1_sum)))
        got = scatter(sums)
        pre = attn_pre(0, grad1, gm0, tokens, saved0, a0)
        keep_m0, send_m0 = split(keep_m0, tie(core_swap(send_m0), pre[0]))
        got_m0 = swap(send_m0, "dp", dp_size, 2)
        gqkv, keep_a0, *send_a0 = attn_grads(0, tie(mask, send_m0), saved0, gain_attn, pre, small_m0, a0)
        mlp1, attn1 = four_split([tie(x, gqkv) for x in got], (), LONG)
        sums = core_sum((128, 160), (keep_m0, tie(got_m0, mlp1)), (keep_a0, *[core_swap(x) for x in send_a0]))
        got = scatter(sums)
        grad0 = attn_post(0, tie(gqkv, *sums), gain_attn, tokens, pre, a0)
        attn1 = sum_direct(attn1, got[1])
        mlp, attn0 = four_split([tie(x, grad0, attn1) for x in got], (mlp1,))
        attn0, mlp = sum_pairs(attn0, mlp)
        d_qkv, d_out, d_up, d_down, d_cross, d_ga, d_gm, d_bias = small_call(
            finish_kernel,
            [((LAYERS, 3, HD, 256), F32), ((LAYERS, HD, 256), F32), ((LAYERS, 256, 256), F32), ((LAYERS, 256, 256), F32),
             ((LAYERS, HD, 256), F32), ((LAYERS, 256), F32), ((LAYERS, 256), F32), ((LAYERS, HD), F32)],
            "finish",
        )(attn1, core_swap(attn1), mlp, core_swap(mlp), attn0, core_swap(attn0))
        return (output, grad0, d_ga, d_gm, d_qkv.transpose(0, 3, 1, 2), d_out, d_up, d_down,
                d_cross.transpose(0, 2, 1), d_bias)

    rows, weights = P(("dp", "head"), None), P(None, "head", None)
    return jax.shard_map(
        body,
        mesh=mesh,
        in_specs=(rows, P("dp"), rows, P(), P(), P(None, None, None, "head"), weights, P(None, None, "head"),
                  weights, P(None, None, "head"), P(None, "head")),
        out_specs=(rows, rows, P(), P(), P(None, None, None, "head"), weights, P(None, None, "head"),
                   weights, P(None, None, "head"), P(None, "head")),
        check_vma=False,
    )
```

```python
import functools

import jax
import jax.numpy as jnp
from jax import lax
from jax.experimental import pallas as pl
from jax.experimental.pallas import tpu as pltpu
from jax.sharding import PartitionSpec as P

HD = 64
LAYERS = 2
EPSILON = 1e-06
MASKED_SCORE = -1000000000.0
BF = jnp.bfloat16
F32 = jnp.float32

VMEM_LIMIT = 32 * 2**20
SMALL_LIMIT = 12 * 2**20
UNROLL = {"attn_fwd": 4, "mlp_fwd": 1, "mlp_both": 1, "mlp_bwd": 1, "attn_bwd": 4, "attn_pre": 4, "attn_post": 2}
KERNEL_FLOPS = 1000
LONG = 50 * 10**9


def nn(a, b):
    return lax.dot_general(a, b, (((1,), (0,)), ((), ())), preferred_element_type=F32)


def nt(a, b):
    return lax.dot_general(a, b, (((1,), (1,)), ((), ())), preferred_element_type=F32)


def tn(a, b):
    return lax.dot_general(a, b, (((0,), (0,)), ((), ())), preferred_element_type=F32)


def rescale_of(values):
    return lax.rsqrt(jnp.mean(values * values, axis=-1, keepdims=True) + EPSILON)


def norm_back(values, rescale, gain, gradient):
    scaled = gradient * gain
    product_mean = jnp.mean(values * scaled, axis=-1, keepdims=True)
    normal = values * rescale
    grad_values = rescale * (scaled - normal * (rescale * product_mean))
    return grad_values, jnp.sum(gradient * normal, axis=0, keepdims=True)


def gelu_and_slope(u):
    cdf = 0.5 + 0.5 * lax.erf(u * 0.7071067811865476)
    density = jnp.exp2((-0.5 * 1.4426950408889634) * (u * u))
    return u * cdf, cdf + u * (density * 0.3989422804014327)


def slot_scores(q, k, mask):
    ones = jnp.where(lax.broadcasted_iota(jnp.int32, mask.shape, 0) == 0, 1.0, 0.0).astype(BF)
    return tn(jnp.concatenate([k, mask], axis=0), jnp.concatenate([q * BF(0.125), ones], axis=0))


def mask_rows(mask_ref, rows):
    return mask_ref[pl.ds(pl.multiple_of(rows.start // 16, 16), 16), :]


def head_index():
    return lax.axis_index("head")


def half_index():
    return lax.axis_index("dp") & 1


def quarter_index():
    return (lax.axis_index("dp") >> 1) & 1


def place_pieces(own, parts, dst):
    at = 0
    for ref in own:
        dst[0, at:at + ref.shape[0], :] = ref
        at += ref.shape[0]
    for place, rows, ref in parts:
        for m in range(3):
            dst[m + 1, pl.ds(pl.multiple_of(place * rows, 16), rows), :] = ref[m * rows:(m + 1) * rows, :]


def parts_of(pieces, rows):
    c, x = half_index(), quarter_index()
    if len(pieces) == 2:
        places = [c, 1 - c]
    else:
        each = len(pieces) // 4
        places = [each * (2 * i + j) + part for i, j in ((c, x), (c, 1 - x), (1 - c, x), (1 - c, 1 - x)) for part in range(each)]
    return [(place, rows, ref) for place, ref in zip(places, pieces)]


def place_attn_pieces(pieces, wa):
    place_pieces((pieces[0][...],), parts_of(pieces[1:], 176), wa)


def place_qkv(layer, pieces, wa, wq):
    place_attn_pieces(pieces, wa)
    side_by_side(wa, wq)


def side_by_side(wa, wq):
    for m in range(4):
        wq[m * 192:(m + 1) * 192, :] = wa[m, 0:192, :]


def place_attn(layer, pieces, wa, w_cross, w_out):
    place_attn_pieces(pieces, wa)
    total = jnp.zeros((1, 256), F32)
    for m in range(4):
        place = pl.multiple_of((head_index() ^ m) * HD, HD)
        w_cross[pl.ds(place, HD), :] = wa[m, 192:256, :]
        w_out[m * HD:(m + 1) * HD, :] = wa[m, 256:320, :]
        total = total + wa[m, 320:336, :].astype(F32)[0:1, :]
    return total


def place_mlp(layer, pieces, wm, up_all, down_all):
    place_pieces((pieces[0][layer], pieces[1][layer]), parts_of(pieces[2:], 512 // (len(pieces) - 2)), wm)
    for m in range(4):
        up_all[:, m * 256:(m + 1) * 256] = wm[m, 0:256, :]
        down_all[m * 256:(m + 1) * 256, :] = wm[m, 256:512, :]


def each_sample(rows, unroll, step, *init, size=256):
    def body(i, carried):
        return step(pl.ds(pl.multiple_of(i * size, size), size), *carried)

    return lax.fori_loop(0, rows // size, body, init, unroll=unroll)


def attn_fwd_kernel(layer, count, *refs):
    pieces = refs[:count]
    (cur_ref, mask_ref, gain_ref, middle_ref, base_ref, nrm_ref, qkv_ref, mix_ref, lse_ref, wa, w_cross, w_out,
     wq) = refs[count:]
    bias = place_attn(layer, pieces, wa, w_cross, w_out)
    side_by_side(wa, wq)
    gain = gain_ref[layer:layer + 1, :]
    def step(rows):
        cur = cur_ref[rows, :].astype(F32)
        nrm = (cur * rescale_of(cur) * gain).astype(BF)
        nrm_ref[rows, :] = nrm
        mask = mask_rows(mask_ref, rows)
        qkv_all = nt(wq[...], nrm).astype(BF)
        qkv_ref[:, rows] = qkv_all
        qkv = [qkv_all[m * 192:(m + 1) * 192] for m in range(4)]
        scores = [slot_scores(qkv[m][0:64], qkv[m][64:128], mask) for m in range(4)]
        cross = nt(nrm, w_cross[...]) + bias
        probs = []
        for m in range(4):
            top = jnp.max(scores[m], axis=0, keepdims=True)
            e = jnp.exp(scores[m] - top)
            total = jnp.sum(e, axis=0, keepdims=True)
            probs.append((e * (1.0 / total)).astype(BF))
            lse_ref[m:m + 1, rows] = top + jnp.log(total)
        mix = jnp.concatenate([nn(qkv[m][128:192], probs[m]).astype(BF) for m in range(4)], axis=0)
        mix_ref[:, rows] = mix
        middle = cur + tn(mix, w_out[...])
        middle_ref[rows, :] = middle
        base_ref[rows, :] = middle + cur * cross
        return ()

    each_sample(cur_ref.shape[0], UNROLL["attn_fwd"], step)


def mlp_fwd_block(middle, gain, up_all, down_all):
    r = rescale_of(middle)
    n2 = (middle * r * gain).astype(BF)
    hid, slope = gelu_and_slope(nn(n2, up_all[...]))
    hid = hid.astype(BF)
    return r, n2, hid, slope.astype(BF), nn(hid, down_all[...])


def mlp_fwd_kernel(layer, count, *refs):
    pieces = refs[:count]
    (middle_ref, base_ref, gain_ref, out_ref, hid_ref, slope_ref, wm, up_all, down_all) = refs[count:]
    place_mlp(layer, pieces, wm, up_all, down_all)
    gain = gain_ref[layer:layer + 1, :]

    def step(rows):
        _, _, hid, slope, feed = mlp_fwd_block(middle_ref[rows, :], gain, up_all, down_all)
        hid_ref[rows, :] = hid
        slope_ref[rows, :] = slope
        out_ref[rows, :] = base_ref[rows, :] + feed
        return ()

    each_sample(middle_ref.shape[0], UNROLL["mlp_fwd"], step, size=middle_ref.shape[0])


def mlp_bwd_block(gf, slope, up_all, down_all):
    gp = (nt(gf, down_all[...]) * slope.astype(F32)).astype(BF)
    return gp, nt(gp, up_all[...])


def put_mlp_grads(hid, gp, n2, gf, keep_ref, send_ref):
    up = tn(n2[...], gp[...]).astype(BF)
    down = tn(hid[...], gf[...]).astype(BF)
    own_up = half_index() == 0
    for m in range(4):
        part = slice(m * 256, (m + 1) * 256)
        keep_ref[m] = jnp.where(own_up, up[:, part], down[part])
        send_ref[m] = jnp.where(own_up, down[part], up[:, part])


def mlp_both_kernel(layer, count, *refs):
    pieces = refs[:count]
    (middle_ref, base_ref, cot_ref, gain_ref, out_ref, gm_ref, keep_ref, send_ref, small_ref,
     wm, up_all, down_all, hid_all, gp_all, n2_all) = refs[count:]
    place_mlp(layer, pieces, wm, up_all, down_all)
    gain = gain_ref[layer:layer + 1, :]

    def step(rows, gain_grad):
        middle = middle_ref[rows, :]
        r, n2, hid, slope, feed = mlp_fwd_block(middle, gain, up_all, down_all)
        out_ref[rows, :] = base_ref[rows, :] + feed
        gf = cot_ref[rows, :]
        gp, gn = mlp_bwd_block(gf, slope, up_all, down_all)
        n2_all[rows, :] = n2
        hid_all[rows, :] = hid
        gp_all[rows, :] = gp
        back, part = norm_back(middle, r, gain, gn)
        gm_ref[rows, :] = gf.astype(F32) + back
        return (gain_grad + part, )

    gain_grad, = each_sample(middle_ref.shape[0], UNROLL["mlp_both"], step, jnp.zeros((1, 256), F32), size=middle_ref.shape[0])
    small_ref[...] = jnp.broadcast_to(gain_grad, small_ref.shape)
    put_mlp_grads(hid_all, gp_all, n2_all, cot_ref, keep_ref, send_ref)


def mlp_bwd_kernel(layer, count, *refs):
    pieces = refs[:count]
    (grad_ref, middle_ref, hid_ref, slope_ref, gain_ref, gm_ref, keep_ref, send_ref, small_ref,
     wm, up_all, down_all, gp_all, n2_all, gf_all) = refs[count:]
    place_mlp(layer, pieces, wm, up_all, down_all)
    gain = gain_ref[layer:layer + 1, :]

    def step(rows, gain_grad):
        middle = middle_ref[rows, :]
        r = rescale_of(middle)
        n2_all[rows, :] = (middle * r * gain).astype(BF)
        grad = grad_ref[rows, :]
        gf = grad.astype(BF)
        gf_all[rows, :] = gf
        gp, gn = mlp_bwd_block(gf, slope_ref[rows, :], up_all, down_all)
        gp_all[rows, :] = gp
        back, part = norm_back(middle, r, gain, gn)
        gm_ref[rows, :] = grad + back
        return (gain_grad + part, )

    gain_grad, = each_sample(middle_ref.shape[0], UNROLL["mlp_bwd"], step, jnp.zeros((1, 256), F32), size=middle_ref.shape[0])
    small_ref[...] = jnp.broadcast_to(gain_grad, small_ref.shape)
    put_mlp_grads(hid_ref, gp_all, n2_all, gf_all, keep_ref, send_ref)


def attn_pre_kernel(layer, count, *refs):
    pieces = refs[:count]
    (grad_ref, gm_ref, cur_ref, nrm_ref, mix_ref, gmix_ref, d_cross_ref, d_out_ref, base_ref, gn_ref, small_ref,
     dot_ref, wa, w_cross, w_out, ga_all, gc_all) = refs[count:]
    bias = place_attn(layer, pieces, wa, w_cross, w_out)

    def step(rows, bias_grad):
        grad = grad_ref[rows, :].astype(F32)
        gm = gm_ref[rows, :]
        ga = gm.astype(BF)
        ga_all[rows, :] = ga
        gc = (grad * cur_ref[rows, :].astype(F32)).astype(BF)
        gc_all[rows, :] = gc
        gmix = nt(w_out[...], ga).astype(BF)
        gmix_ref[:, rows] = gmix
        for m in range(4):
            head = slice(m * HD, (m + 1) * HD)
            product = gmix[head].astype(F32) * mix_ref[head, rows].astype(F32)
            dot_ref[m:m + 1, rows] = jnp.sum(product, axis=0, keepdims=True)
        gn_ref[rows, :] = nn(gc, w_cross[...])
        base_ref[rows, :] = gm + grad * (nt(nrm_ref[rows, :], w_cross[...]) + bias)
        return (bias_grad + jnp.sum(gc.astype(F32), axis=0, keepdims=True), )

    bias_grad, = each_sample(cur_ref.shape[0], UNROLL["attn_pre"], step, jnp.zeros((1, 256), F32))
    d_cross = tn(gc_all[...], nrm_ref[...])
    d_cross_ref[...] = d_cross.astype(BF)
    d_out_ref[...] = nn(mix_ref[...], ga_all[...]).astype(BF)
    small_ref[0:1, :] = bias_grad
    small_ref[1:2, :] = jnp.sum(d_cross * w_cross[...].astype(F32), axis=0, keepdims=True)


def qkv_back(rows, mask_ref, qkv_ref, lse_ref, gmix_ref, dot_ref):
    mask = mask_rows(mask_ref, rows)
    parts = []
    for m in range(4):
        q, k, v = (qkv_ref[m * 192 + i * HD:m * 192 + (i + 1) * HD, rows] for i in range(3))
        parts.append((q, k, v, gmix_ref[m * HD:(m + 1) * HD, rows]))
    scores = [slot_scores(q, k, mask) for q, k, v, go in parts]
    gps = [tn(v, go) for q, k, v, go in parts]
    ps, gss = [], []
    for m in range(4):
        p = jnp.exp(scores[m] - lse_ref[m:m + 1, rows])
        ps.append(p.astype(BF))
        gss.append((p * (gps[m] - dot_ref[m:m + 1, rows])).astype(BF))
    return [
        jnp.concatenate([nn(k, gs) * 0.125, nt(q, gs) * 0.125, nt(go, p)], axis=0).astype(BF)
        for (q, k, v, go), p, gs in zip(parts, ps, gss)
    ]


def norm_grad(cur, gain, gn):
    r = rescale_of(cur)
    scaled = gn * gain
    return r * (scaled - cur * (r * r * jnp.mean(cur * scaled, axis=-1, keepdims=True)))


def put_attn_grads(layer, nrm, gqkv_all, wq, gain_ref, d_cross_ref, d_out_ref, small, mlp_small, payload, keep_ref, sends):
    d_qkv = nn(gqkv_all[...], nrm)
    gain_grad = small[1:2, :] + jnp.sum(d_qkv * wq[...].astype(F32), axis=0, keepdims=True)
    for m in range(4):
        place = pl.multiple_of((head_index() ^ m) * HD, HD)
        payload[m, 0:192, :] = d_qkv[m * 192:(m + 1) * 192].astype(BF)
        payload[m, 192:256, :] = d_cross_ref[pl.ds(place, HD), :]
        payload[m, 256:320, :] = d_out_ref[m * HD:(m + 1) * HD, :]
    gain_grad = gain_grad / gain_ref[layer:layer + 1, :]
    high, low = split_rows(jnp.concatenate([gain_grad, small[0:1, :], mlp_small[0:1, :], jnp.zeros((5, 256), F32)], axis=0))
    keep = pl.multiple_of(half_index() * 160, 16)
    other = pl.multiple_of((1 - half_index()) * 160, 16)
    for m in range(4):
        each = 4 // len(sends)
        for ref, i, at in ((keep_ref, m, keep), (sends[m // each], m % each, other)):
            ref[i, 0:160, :] = payload[m, pl.ds(at, 160), :]
            ref[i, 160:168, :] = high
            ref[i, 168:176, :] = low


def attn_bwd_kernel(layer, count, *refs):
    pieces = refs[:count]
    (mask_ref, nrm_ref, qkv_ref, lse_ref, gain_ref, gmix_ref, d_cross_ref, d_out_ref, small, dot_ref, mlp_small,
     cur_ref, base_ref, gn_ref, out_ref, keep_ref, send_ref, wa, wq, gqkv_all, payload) = refs[count:]
    place_qkv(layer, pieces, wa, wq)

    def step(rows):
        gn = gn_ref[rows, :]
        gqkv = jnp.concatenate(qkv_back(rows, mask_ref, qkv_ref, lse_ref, gmix_ref, dot_ref), axis=0)
        gqkv_all[:, rows] = gqkv
        gn = gn + tn(gqkv, wq[...])
        out_ref[rows, :] = base_ref[rows, :] + norm_grad(cur_ref[rows, :].astype(F32), gain_ref[layer:layer + 1, :], gn)
        return ()

    each_sample(nrm_ref.shape[0], UNROLL["attn_bwd"], step)
    put_attn_grads(layer, nrm_ref[...], gqkv_all, wq, gain_ref, d_cross_ref, d_out_ref, small, mlp_small,
                   payload, keep_ref, (send_ref,))


def attn_grads_kernel(layer, count, *refs):
    pieces = refs[:count]
    (mask_ref, nrm_ref, qkv_ref, lse_ref, gain_ref, gmix_ref, d_cross_ref, d_out_ref, small, dot_ref, mlp_small,
     gqkv_all, keep_ref, send_low, send_high, wa, wq, payload) = refs[count:]
    place_qkv(layer, pieces, wa, wq)

    def step(rows):
        for m, gqkv in enumerate(qkv_back(rows, mask_ref, qkv_ref, lse_ref, gmix_ref, dot_ref)):
            gqkv_all[m * 192:(m + 1) * 192, rows] = gqkv
        return ()

    each_sample(nrm_ref.shape[0], UNROLL["attn_bwd"], step)
    put_attn_grads(layer, nrm_ref[...], gqkv_all, wq, gain_ref, d_cross_ref, d_out_ref, small, mlp_small,
                   payload, keep_ref, (send_low, send_high))


def attn_post_kernel(layer, count, *refs):
    pieces = refs[:count]
    (gqkv_all, gain_ref, cur_ref, base_ref, gn_ref, out_ref, wa, wq) = refs[count:]
    place_qkv(layer, pieces, wa, wq)

    def step(rows):
        gn = gn_ref[rows, :]
        gn = gn + tn(gqkv_all[:, rows], wq[...])
        out_ref[rows, :] = base_ref[rows, :] + norm_grad(cur_ref[rows, :].astype(F32), gain_ref[layer:layer + 1, :], gn)
        return ()

    each_sample(cur_ref.shape[0], UNROLL["attn_post"], step)


def split_rows(x):
    high = x.astype(BF)
    return high, (x - high.astype(F32)).astype(BF)


def pack_kernel(lens, qkv, cross, out, up, down, b, own0, own1, group0, group1, mask, sems):
    copies = []
    for l, own in ((0, own0), (1, own1)):
        for t in range(3):
            copies.append(pltpu.make_async_copy(qkv.at[l, t], own.at[pl.ds(t * HD, HD)], sems.at[0]))
        copies.append(pltpu.make_async_copy(cross.at[l], own.at[pl.ds(192, HD)], sems.at[0]))
        copies.append(pltpu.make_async_copy(out.at[l], own.at[pl.ds(256, HD)], sems.at[0]))
    for copy in copies:
        copy.start()

    x = pl.multiple_of(quarter_index() * 128, 16)

    def mlp_parts(weight):
        return [pltpu.make_async_copy(weight.at[l, pl.ds(x, 128)], group.at[pl.ds(176, 128)], sems.at[1])
                for l, group in ((0, group0), (1, group1))]

    @pl.when(half_index() == 0)
    def _():
        for copy in mlp_parts(up):
            copy.start()

    @pl.when(half_index() != 0)
    def _():
        for copy in mlp_parts(down):
            copy.start()

    slots = lax.broadcasted_iota(jnp.int32, (16, 256), 1)
    first = lax.broadcasted_iota(jnp.int32, (16, 256), 0) == 0
    samples = mask.shape[0] // 16
    for i in range(samples):
        length = lens[head_index() * samples + i]
        mask[i * 16:(i + 1) * 16, :] = jnp.where(jnp.logical_and(first, slots >= length), MASKED_SCORE, 0.0).astype(BF)
    lane = lax.broadcasted_iota(jnp.int32, (LAYERS, 256), 1) // HD
    wide = jnp.concatenate([b[...].astype(F32)] * 4, axis=1)
    wide = jnp.where(lane == head_index(), wide, 0.0)
    for l, own in ((0, own0), (1, own1)):
        own[320:352, :] = jnp.broadcast_to(wide[l:l + 1], (32, 256)).astype(BF)
    for copy in copies:
        copy.wait()
    at = pl.multiple_of(half_index() * 176, 16)
    group0[0:176, :] = own0[pl.ds(at, 176), :]
    group1[0:176, :] = own1[pl.ds(at, 176), :]
    for copy in mlp_parts(up):
        copy.wait()


def bring_kernel(*refs):
    half = len(refs) // 2
    for src, dst in zip(refs[:half], refs[half:]):
        dst[...] = src[...]


def stack_kernel(a, b, c, attn, *mlp):
    rows = 128 // len(mlp)
    for m, ref in enumerate((a, b, c)):
        attn[m * 176:(m + 1) * 176, :] = ref[0:176, :]
        for i, out in enumerate(mlp):
            out[m * rows:(m + 1) * rows, :] = ref[176 + i * rows:176 + (i + 1) * rows, :]


def put_sum(out, at, small_at, rows, total):
    for low, high in ((0, small_at), (small_at + 16, rows)):
        if low < high:
            out[at + low:at + high, :] = total(low, high).astype(BF)
    if small_at < rows:
        both = total(small_at, small_at + 16)
        high, low = split_rows(both[0:8] + both[8:16])
        out[at + small_at:at + small_at + 8, :] = high
        out[at + small_at + 8:at + small_at + 16, :] = low


def core_sum_kernel(small_at, *refs):
    ins, outs = refs[:-4], refs[-4:]
    for m, out in enumerate(outs):
        at = 0
        rest = list(ins)
        for where in small_at:
            keep = rest.pop(0)
            if where is None:
                out[at:at + keep.shape[1], :] = keep[m]
                at += keep.shape[1]
                continue
            got, index = rest.pop(0), m
            if got.shape[0] < keep.shape[0]:
                got, index = (got, rest.pop(0))[m // 2], m % 2
            rows = keep.shape[1]
            put_sum(out, at, where, rows, lambda i, j: keep[m, i:j].astype(F32) + got[index, i:j].astype(F32))
            at += rows


def core_split_kernel(keep, got, keep_out, send_out):
    at = pl.multiple_of(quarter_index() * 128, 16)
    other = pl.multiple_of((1 - quarter_index()) * 128, 16)
    for out, rows in ((keep_out, pl.ds(at, 128)), (send_out, pl.ds(other, 128))):
        for m in range(4):
            out[m] = (keep[m, rows, :].astype(F32) + got[m, rows, :].astype(F32)).astype(BF)


def add_kernel(a, b, out):
    out[...] = (a[...].astype(F32) + b[...].astype(F32)).astype(BF)


def four_sum_kernel(small_at, *refs):
    s, a, b, c, out = refs
    put_sum(out, 0, small_at, s.shape[0],
            lambda i, j: (s[i:j].astype(F32) + a[i:j].astype(F32)) + (b[i:j].astype(F32) + c[i:j].astype(F32)))


def four_split_kernel(*refs):
    done, (s, a, b, c, mlp, attn) = refs[:-6], refs[-6:]

    def total(i, j):
        return (s[i:j].astype(F32) + a[i:j].astype(F32)) + (b[i:j].astype(F32) + c[i:j].astype(F32))

    at = 0
    for ref in done:
        mlp[at:at + 128, :] = ref[...]
        at += 128
    mlp[at:at + 128, :] = total(0, 128).astype(BF)
    put_sum(attn, 0, 160, 176, lambda i, j: total(i + 128, j + 128))


def pair_sum_kernel(low, low_got, high, high_got, low_out, high_out):
    put_sum(low_out, 0, 160, low.shape[0], lambda i, j: low[i:j].astype(F32) + low_got[i:j].astype(F32))
    high_out[...] = (high[...].astype(F32) + high_got[...].astype(F32)).astype(BF)


def last_pair_kernel(low, low_got, high, high_got, low_out, high_out):
    put_sum(low_out, 0, 160, low.shape[0], lambda i, j: low[i:j].astype(F32) + low_got[i:j].astype(F32))
    high_out[0:256, :] = high[...]
    high_out[256:512, :] = high_got[...]


def finish_kernel(low, low_other, high, high_other, late, late_other,
                  d_qkv, d_out, d_up, d_down, d_cross, gain_attn, gain_mlp, bias):
    mine = pl.multiple_of(quarter_index() * 128, 16)
    other = pl.multiple_of((1 - quarter_index()) * 128, 16)

    def place(first, second):
        for l, a, b in ((1, first[0], second[0]), (0, first[2], second[2])):
            d_qkv[l, 0] = a[0:64].astype(F32)
            d_qkv[l, 1] = a[64:128].astype(F32)
            d_qkv[l, 2, 0:32] = a[128:160].astype(F32)
            d_qkv[l, 2, 32:64] = b[0:32].astype(F32)
            d_cross[l] = b[32:96].astype(F32)
            d_out[l] = b[96:160].astype(F32)
        for dst, ref in ((d_up, first[1]), (d_down, second[1])):
            for l, at in ((1, 0), (0, 128)):
                dst[l, pl.ds(mine, 128)] = ref[at:at + 128].astype(F32)
                dst[l, pl.ds(other, 128)] = ref[at + 256:at + 384].astype(F32)

    @pl.when(half_index() == 0)
    def _():
        place((low, high, late), (low_other, high_other, late_other))

    @pl.when(half_index() != 0)
    def _():
        place((low_other, high_other, late_other), (low, high, late))

    for l, ref in ((0, late), (1, low)):
        small = ref[160:168].astype(F32) + ref[168:176].astype(F32)
        gain_attn[l:l + 1, :] = small[0:1]
        gain_mlp[l:l + 1, :] = small[2:3]
        total = jnp.zeros((1, HD), F32)
        for h in range(4):
            total = total + jnp.where(head_index() == h, small[1:2, h * HD:(h + 1) * HD], 0.0)
        bias[l:l + 1, :] = total


SMEM = pl.BlockSpec(memory_space=pltpu.SMEM)
ANY = pl.BlockSpec(memory_space=pl.ANY)


def call(kernel, outs, scratch, name, *args, flops=KERNEL_FLOPS):
    return pl.pallas_call(
        kernel,
        in_specs=[VMEM] * len(args),
        out_specs=[VMEM] * len(outs),
        out_shape=[jax.ShapeDtypeStruct(shape, dtype) for shape, dtype in outs],
        scratch_shapes=[pltpu.VMEM(shape, dtype) for shape, dtype in scratch],
        compiler_params=pltpu.CompilerParams(vmem_limit_bytes=VMEM_LIMIT),
        cost_estimate=pl.CostEstimate(flops=flops, bytes_accessed=1024, transcendentals=0),
        name=name,
    )(*args)


QKV_SCRATCH = [((4, 352, 256), BF), ((768, 256), BF)]
ATTN_SCRATCH = [((4, 352, 256), BF), ((256, 256), BF), ((256, 256), BF)]
MLP_SCRATCH = [((4, 512, 256), BF), ((256, 1024), BF), ((1024, 256), BF)]
MLP_GRADS = [((4, 256, 256), BF), ((4, 256, 256), BF), ((8, 256), F32)]


def attn_fwd(layer, cur, mask, gain, pieces):
    rows = cur.shape[0]
    outs = [((rows, 256), F32), ((rows, 256), F32), ((rows, 256), BF), ((768, rows), BF), ((256, rows), BF), ((8, rows), F32)]
    return call(functools.partial(attn_fwd_kernel, layer, len(pieces)), outs, ATTN_SCRATCH + [((768, 256), BF)], "attn_fwd", *pieces, cur, mask, gain,
                flops=(LONG, KERNEL_FLOPS)[layer])


def mlp_fwd(layer, middle, base, gain, pieces):
    rows = middle.shape[0]
    outs = [((rows, 256), F32), ((rows, 1024), BF), ((rows, 1024), BF)]
    return call(functools.partial(mlp_fwd_kernel, layer, len(pieces)), outs, MLP_SCRATCH, "mlp_fwd", *pieces,
                middle, base, gain)


def mlp_both(layer, middle, base, cot, gain, pieces):
    rows = middle.shape[0]
    outs = [((rows, 256), F32), ((rows, 256), F32)] + MLP_GRADS
    scratch = MLP_SCRATCH + [((rows, 1024), BF), ((rows, 1024), BF), ((rows, 256), BF)]
    return call(functools.partial(mlp_both_kernel, layer, len(pieces)), outs, scratch, "mlp_both", *pieces, middle, base, cot, gain)


def mlp_bwd(layer, grad, middle, hid, slope, gain, pieces):
    rows = middle.shape[0]
    outs = [((rows, 256), F32)] + MLP_GRADS
    scratch = MLP_SCRATCH + [((rows, 1024), BF), ((rows, 256), BF), ((rows, 256), BF)]
    return call(functools.partial(mlp_bwd_kernel, layer, len(pieces)), outs, scratch, "mlp_bwd", *pieces,
                grad, middle, hid, slope, gain)


def attn_pre(layer, grad, gm, cur, saved, pieces):
    rows = cur.shape[0]
    nrm, _, mix, _ = saved
    outs = [((256, rows), BF), ((256, 256), BF), ((256, 256), BF), ((rows, 256), F32), ((rows, 256), F32), ((8, 256), F32), ((8, rows), F32)]
    scratch = ATTN_SCRATCH + [((rows, 256), BF), ((rows, 256), BF)]
    return call(functools.partial(attn_pre_kernel, layer, len(pieces)), outs, scratch, "attn_pre", *pieces, grad, gm, cur, nrm, mix)


PAYLOAD = [((4, 176, 256), BF), ((4, 176, 256), BF)]


def attn_bwd(layer, cur, mask, saved, gain, pre, mlp_small, pieces):
    rows = cur.shape[0]
    nrm, qkv, _, lse = saved
    gmix, d_cross, d_out, base, gn, small, dot = pre
    scratch = QKV_SCRATCH + [((768, rows), BF), ((4, 320, 256), BF)]
    return call(functools.partial(attn_bwd_kernel, layer, len(pieces)), [((rows, 256), F32)] + PAYLOAD, scratch, "attn_bwd", *pieces,
                mask, nrm, qkv, lse, gain, gmix, d_cross, d_out, small, dot, mlp_small, cur, base, gn)


def attn_grads(layer, mask, saved, gain, pre, mlp_small, pieces):
    nrm, qkv, _, lse = saved
    gmix, d_cross, d_out, _, _, small, dot = pre
    scratch = QKV_SCRATCH + [((4, 320, 256), BF)]
    return call(functools.partial(attn_grads_kernel, layer, len(pieces)), [((768, nrm.shape[0]), BF), ((4, 176, 256), BF), ((2, 176, 256), BF), ((2, 176, 256), BF)], scratch, "attn_grads", *pieces,
                mask, nrm, qkv, lse, gain, gmix, d_cross, d_out, small, dot, mlp_small)


def attn_post(layer, gqkv, gain, cur, pre, pieces):
    return call(functools.partial(attn_post_kernel, layer, len(pieces)), [((cur.shape[0], 256), F32)], QKV_SCRATCH, "attn_post", *pieces,
                gqkv, gain, cur, pre[3], pre[4])[0]


VMEM = pl.BlockSpec(memory_space=pltpu.VMEM)


def small_call(kernel, shapes, name, flops=1000):
    def run(*args):
        return pl.pallas_call(
            kernel,
            in_specs=[VMEM] * len(args),
            out_specs=[VMEM] * len(shapes),
            out_shape=[jax.ShapeDtypeStruct(shape, dtype) for shape, dtype in shapes],
            compiler_params=pltpu.CompilerParams(vmem_limit_bytes=SMALL_LIMIT),
            cost_estimate=pl.CostEstimate(flops=flops, bytes_accessed=1024, transcendentals=0),
            name=name,
        )(*args)
    return run


def core_sum(small_at, *groups):
    rows = sum(group[0].shape[1] for group in groups)
    return small_call(functools.partial(core_sum_kernel, small_at), [((rows, 256), BF)] * 4, "core_sum")(
        *[x for group in groups for x in group])


def four_sum(small_at, terms, flops=1000):
    return small_call(functools.partial(four_sum_kernel, small_at), [(terms[0].shape, BF)], "four_sum", flops)(*terms)[0]


def swap(x, axis, size, mask):
    return lax.ppermute(x, axis, [(i, i ^ mask) for i in range(size)])


def tie(x, *before):
    return lax.optimization_barrier((x,) + before)[0]


def solution(mesh):
    dp_size, head_size = mesh.shape["dp"], mesh.shape["head"]

    def core_swap(x):
        return swap(x, "dp", dp_size, 1)

    def fetch(x):
        return [swap(x, "head", head_size, m) for m in range(1, head_size)]

    def scatter(sums):
        return [sums[0]] + [swap(sums[m], "head", head_size, m) for m in range(1, head_size)]

    def split(keep, got):
        return small_call(core_split_kernel, [((4, 128, 256), BF)] * 2, "core_split")(keep, got)

    def four_split(terms, done=(), flops=1000):
        return small_call(four_split_kernel, [((128 * (len(done) + 1), 256), BF), ((176, 256), BF)], "four_split", flops)(*done, *terms)

    bits = [1 << i for i in range(1, dp_size.bit_length() - 1)]

    def sum_direct(x, after):
        for i in range(0, len(bits), 2):
            masks = (bits[i], bits[i + 1], bits[i] + bits[i + 1]) if i + 1 < len(bits) else (bits[i],)
            terms = [x] + [swap(tie(x, after) if k == 2 else x, "dp", dp_size, mask) for k, mask in enumerate(masks)]
            x = four_sum(160, terms + [jnp.zeros_like(x)] * (4 - len(terms)))
        return x

    def sum_pairs(low, high):
        pairs = list(zip(bits, bits[1:] + bits[:1]))
        for i, (one, two) in enumerate(pairs):
            kernel, more = (last_pair_kernel, 256) if i == len(pairs) - 1 else (pair_sum_kernel, 0)
            low, high = small_call(kernel, [(low.shape, BF), ((high.shape[0] + more, 256), BF)], "pair_sum")(
                low, swap(low, "dp", dp_size, one), high, swap(high, "dp", dp_size, two))
        return low, high

    def body(tokens, lengths, cotangent, gain_attn, gain_mlp, w_qkv, w_out, w_up, w_down, w_cross, b_cross):
        rows = tokens.shape[0]
        own0, own1, group0, group1, mask = pl.pallas_call(
            pack_kernel,
            in_specs=[SMEM] + [ANY] * 5 + [VMEM],
            out_specs=[VMEM] * 5,
            out_shape=[jax.ShapeDtypeStruct((n, 256), BF) for n in (352, 352, 304, 304)]
            + [jax.ShapeDtypeStruct((rows // 16, 256), BF)],
            scratch_shapes=[pltpu.SemaphoreType.DMA((2,))],
            name="pack",
        )(lengths, w_qkv.transpose(0, 2, 3, 1), w_cross.transpose(0, 2, 1), w_out, w_up, w_down, b_cross)

        def stack(pieces, arrays):
            return small_call(stack_kernel, [((528, 256), BF)] + [((384 // arrays, 256), BF)] * arrays, "stack")(*pieces)

        def quarters(own, before):
            parts = own + [tie(swap(x, "dp", dp_size, 2), before) for x in own]
            return [w_up, w_down] + parts + [core_swap(x) for x in parts]

        pieces0, pieces1 = fetch(group0), fetch(group1)
        near = (tokens, mask, gain_attn, own0)
        tokens, mask, gain_attn, own0 = small_call(bring_kernel, [(x.shape, x.dtype) for x in near], "bring")(*near)
        a0, *m0 = stack([tie(x, own0) for x in pieces0], 2)
        a0 = [own0, a0, core_swap(a0)]
        mid0, base0, *saved0 = attn_fwd(0, tokens, mask, gain_attn, a0)
        m0 = quarters(m0, mid0)
        cur1, hid0, slope0 = mlp_fwd(0, mid0, base0, gain_mlp, m0)
        a1, *m1 = stack([tie(x, cur1) for x in pieces1], 1)
        a1 = [own1, a1, core_swap(a1)]
        mid1, base1, *saved1 = attn_fwd(1, cur1, mask, gain_attn, a1)
        m1 = quarters(m1, mid1)
        output, gm1, keep_m1, send_m1, small_m1 = mlp_both(1, mid1, base1, cotangent, gain_mlp, m1)
        pre = attn_pre(1, cotangent, gm1, cur1, saved1, a1)
        keep_m1, send_m1 = split(keep_m1, tie(core_swap(send_m1), pre[0]))
        got_m1 = swap(send_m1, "dp", dp_size, 2)
        grad1, keep_a1, send_a1 = attn_bwd(1, cur1, tie(mask, send_m1), saved1, gain_attn, pre, small_m1, a1)
        gm0, keep_m0, send_m0, small_m0 = mlp_bwd(0, grad1, mid0, hid0, slope0, gain_mlp, m0)
        m1_sum = small_call(add_kernel, [((4, 128, 256), BF)], "add", LONG)(keep_m1, tie(got_m1, gm0))[0]
        sums = core_sum((None, 160), (m1_sum,), (keep_a1, tie(core_swap(send_a1), m1_sum)))
        got = scatter(sums)
        pre = attn_pre(0, grad1, gm0, tokens, saved0, a0)
        keep_m0, send_m0 = split(keep_m0, tie(core_swap(send_m0), pre[0]))
        got_m0 = swap(send_m0, "dp", dp_size, 2)
        gqkv, keep_a0, *send_a0 = attn_grads(0, tie(mask, send_m0), saved0, gain_attn, pre, small_m0, a0)
        grad0 = attn_post(0, gqkv, gain_attn, tokens, pre, a0)
        mlp1, attn1 = four_split([tie(x, grad0) for x in got], (), LONG)
        sums = core_sum((128, 160), (keep_m0, tie(got_m0, mlp1)), (keep_a0, *[core_swap(x) for x in send_a0]))
        got = scatter(sums)
        attn1 = sum_direct(attn1, got[1])
        mlp, attn0 = four_split([tie(x, grad0, attn1) for x in got], (mlp1,))
        attn0, mlp = sum_pairs(attn0, mlp)
        d_qkv, d_out, d_up, d_down, d_cross, d_ga, d_gm, d_bias = small_call(
            finish_kernel,
            [((LAYERS, 3, HD, 256), F32), ((LAYERS, HD, 256), F32), ((LAYERS, 256, 256), F32), ((LAYERS, 256, 256), F32),
             ((LAYERS, HD, 256), F32), ((LAYERS, 256), F32), ((LAYERS, 256), F32), ((LAYERS, HD), F32)],
            "finish",
        )(attn1, core_swap(attn1), mlp, core_swap(mlp), attn0, core_swap(attn0))
        return (output, grad0, d_ga, d_gm, d_qkv.transpose(0, 3, 1, 2), d_out, d_up, d_down,
                d_cross.transpose(0, 2, 1), d_bias)

    rows, weights = P(("dp", "head"), None), P(None, "head", None)
    return jax.shard_map(
        body,
        mesh=mesh,
        in_specs=(rows, P("dp"), rows, P(), P(), P(None, None, None, "head"), weights, P(None, None, "head"),
                  weights, P(None, None, "head"), P(None, "head")),
        out_specs=(rows, rows, P(), P(), P(None, None, None, "head"), weights, P(None, None, "head"),
                   weights, P(None, None, "head"), P(None, "head")),
        check_vma=False,
    )
```
